32 devices in a mesh: rep: 2 (over y), dp: 16 (over z, x, core).
Axes of the slice: x: 2, y: 2, z: 4, core: 2. Of those that a mesh axis runs over, the one named last changes fastest.
Arguments:
- x_copy: bfloat16 [32, 1024, 512], P(('rep', 'dp')), may hold values from -6 to 6
- target_embed: bfloat16 [32, 1024, 512], P(('rep', 'dp')), may hold values from -6 to 6
- memory: bfloat16 [32, 1024, 512], P(('rep', 'dp')), may hold values from -6 to 6
- cotangent: bfloat16 [32, 1024, 512], P(('rep', 'dp')), may hold values from -6 to 6
- segment_ids: int32 [32, 1024], P(('rep', 'dp')), may hold values from 0 to 7, never falling along the last dimension, each value on 1 to 256 neighbouring positions
- source_lengths: int32 [32], P(('rep', 'dp')), may hold values from 256 to 1024
- target_lengths: int32 [32], P(('rep', 'dp')), may hold values from 384 to 1024, as said below
- hamming: int32 [32, 8], P(('rep', 'dp')), may hold values from 0 to 256
- priority: int32 [32, 1024], P(('rep', 'dp')), may hold values from 0 to 1048575
- lang_tag: int32 [32], P(('rep', 'dp')), may hold values from 0 to 63
- w_self_qkv: bfloat16 [3, 512, 512], P(None, None, 'dp'), may hold values from -0.25 to 0.25
- w_self_out: bfloat16 [512, 512], P(None, 'dp'), may hold values from -0.75 to 0.75
- w_cross_q: bfloat16 [512, 512], P(None, 'dp'), may hold values from -0.25 to 0.25
- w_cross_kv: bfloat16 [2, 512, 512], P(None, None, 'dp'), may hold values from -0.25 to 0.25
- w_cross_out: bfloat16 [512, 512], P(None, 'dp'), may hold values from -1 to 1
- w_in: bfloat16 [512, 2048], P(None, 'dp'), may hold values from -0.25 to 0.25
- w_out: bfloat16 [2048, 512], P(None, 'dp'), may hold values from -0.125 to 0.125
- biases: bfloat16 [10, 512], P(None, 'dp'), may hold values from -3 to 3
- gains: bfloat16 [3, 512], P(None, 'dp'), may hold values from 0.25 to 1.75
- b_hidden: bfloat16 [2048], P('dp'), may hold values from -3 to 3
- lang_table: bfloat16 [64, 512], P(None, 'dp'), may hold values from -4 to 4
Outputs:
- first_pass: bfloat16 [32, 1024, 512], P(('rep', 'dp'))
- output: bfloat16 [32, 1024, 512], P(('rep', 'dp'))
- input_grad: float32 [32, 1024, 512], P(('rep', 'dp'))
- memory_grad: float32 [32, 1024, 512], P(('rep', 'dp'))
- grad_self_qkv: float32 [3, 512, 512], P(None, None, 'dp')
- grad_self_out: float32 [512, 512], P(None, 'dp')
- grad_cross_q: float32 [512, 512], P(None, 'dp')
- grad_cross_kv: float32 [2, 512, 512], P(None, None, 'dp')
- grad_cross_out: float32 [512, 512], P(None, 'dp')
- grad_w_in: float32 [512, 2048], P(None, 'dp')
- grad_w_out: float32 [2048, 512], P(None, 'dp')
- grad_biases: float32 [10, 512], P(None, 'dp')
- grad_gains: float32 [3, 512], P(None, 'dp')
- grad_b_hidden: float32 [2048], P('dp')
- grad_lang_table: float32 [64, 512], P(None, 'dp')
The draws below stay inside these ranges and needn't reach their ends.
Inputs may be any that keep to these rules, and one draw needn't show every extreme that they name: `segment_ids`: segment numbers never fall along a row; each segment holds 1 to 256 token slots. `target_lengths`: some row is full and some row holds the fewest live tokens.
All inputs are finite; a program needn't handle non-finite values.
Results may differ from the reference program's by a relative error of at most 0.024.
The reference program's roundings to bfloat16 on the way count: a program that leaves them out, or rounds other values in their place, can miss the bound.
Values may be sent and summed in bfloat16 or wider, within the bound.
A program may use at most 320 MiB of HBM per device.

```python
import math
import jax
import jax.numpy as jnp
import numpy as np
from jax import lax

D = 512
HEADS = 8
HD = 64
FF = 2048
LANGS = 64
L = 1024
SRC = 1024
SEGS = 8
MOST_DOC = 256
ROWS = 32


def draw_target_lengths(key, part):
    key = jax.random.fold_in(key, 5)
    first_key, second_key, third_key = jax.random.split(key, 3)
    shortest = L * 3 // 8
    values = jax.random.randint(first_key, (ROWS,), shortest, L + 1, dtype=jnp.int32)
    full_row = jax.random.randint(second_key, (), 0, ROWS, dtype=jnp.int32)
    short_row = (full_row + 1 + jax.random.randint(third_key, (), 0, ROWS - 1, dtype=jnp.int32)) % ROWS
    values = values.at[full_row].set(L)
    values = values.at[short_row].set(shortest)
    return values.astype(jnp.int32)


def touch_ends(values, own_key, low, high):
    longest = values.shape.index(max(values.shape))
    spots = []
    for shift in (0, 1):
        where = [jax.random.randint(jax.random.fold_in(own_key, axis), (), 0, length) for axis, length in enumerate(values.shape)]
        where[longest] = (where[longest] + shift) % values.shape[longest]
        spots.append(tuple(where))
    return values.at[spots[0]].set(low).at[spots[1]].set(high)


def block_scale(own_key, extent, pieces, least, high):
    def one(axis_at, parts):
        steps = jax.random.uniform(jax.random.fold_in(jax.random.fold_in(own_key, 6), axis_at), (parts,), jnp.float32, least / len(pieces), high / len(pieces))
        return jnp.repeat(jnp.exp(steps), extent[axis_at] // parts).reshape((-1,) + (1,) * (len(extent) - axis_at - 1))

    factor_of = one(*pieces[0])
    for cut in pieces[1:]:
        factor_of = factor_of * one(*cut)
    return factor_of


def profile(number_of, total, reach, skew):
    weights = [(1 << 20) // math.isqrt(grade ** skew) + 1 for grade in range(2, number_of + 1)]
    rest, counts = total - reach - (number_of - 1), [1] * (number_of - 1)
    while rest > 0:
        free = [i for i in range(number_of - 1) if counts[i] < reach]
        pool, budget = sum([weights[i] for i in free]), rest
        for i in free:
            extra = min(reach - counts[i], max(1, budget * weights[i] // pool), rest)
            counts[i] = counts[i] + extra
            rest = rest - extra
    return np.array([reach] + counts)


def uneven(stream_key, count, total, limit, lean):
    if count == 2:
        one = jax.random.randint(stream_key, (), max(1, total - limit), min(limit, total - 1) + 1)
        return jnp.stack([one, total - one])
    tallies = jnp.asarray(profile(count, total, limit, lean), jnp.int32)
    twos = (count - 1) // 2
    donor, taker = tallies[1:1 + 2 * twos:2], tallies[2:2 + 2 * twos:2]
    margin = jnp.minimum(donor - 1, limit - taker)
    shifted = jax.random.randint(jax.random.fold_in(stream_key, 1), (twos,), 0, 1 << 20) % (margin + 1)
    tallies = tallies.at[1:1 + 2 * twos:2].set(donor - shifted).at[2:2 + 2 * twos:2].set(taker + shifted)
    return tallies[jax.random.permutation(jax.random.fold_in(stream_key, 2), count)]


def noise(rng, dims, width, most, cuts=(), held_as=jnp.bfloat16):
    values = jax.random.normal(rng, dims, jnp.float32) * width
    if len(cuts) > 0:
        values = block_scale(rng, dims, cuts, -0.22, 0.18) * values
    return jnp.clip(values, min=-most, max=most).astype(held_as)


def setup_inputs(seed: int = 0) -> dict:
    keys = jax.random.split(jax.random.key(seed), 22)
    return {
        "x_copy": noise(keys[0], (ROWS, L, D), 1.0, 6.0, ((0, 32),)),
        "target_embed": noise(keys[1], (ROWS, L, D), 1.0, 6.0, ((0, 32),)),
        "memory": noise(keys[2], (ROWS, SRC, D), 1.0, 6.0, ((0, 32),)),
        "cotangent": noise(keys[3], (ROWS, L, D), 1.0, 6.0, ((0, 32),)),
        "segment_ids": jax.vmap(lambda own: jnp.searchsorted(jnp.cumsum(uneven(own, SEGS, L, MOST_DOC, 2)), jnp.arange(L), side="right"))(jax.random.split(keys[4], ROWS)).reshape((ROWS, L)).astype(jnp.int32),
        "source_lengths": touch_ends(jax.random.randint(keys[5], (ROWS,), SRC // 4, SRC + 1), jax.random.fold_in(keys[5], 1), SRC // 4, SRC).astype(jnp.int32),
        "target_lengths": draw_target_lengths(jax.random.fold_in(keys[21], 71), 0),
        "hamming": touch_ends(jax.random.randint(keys[7], (ROWS, SEGS), 0, MOST_DOC + 1), jax.random.fold_in(keys[7], 1), 0, MOST_DOC).astype(jnp.int32),
        "priority": touch_ends(jax.random.randint(keys[8], (ROWS, L), 0, 1048576), jax.random.fold_in(keys[8], 1), 0, 1048575).astype(jnp.int32),
        "lang_tag": touch_ends(jax.random.randint(keys[9], (ROWS,), 0, LANGS), jax.random.fold_in(keys[9], 1), 0, LANGS - 1).astype(jnp.int32),
        "w_self_qkv": noise(keys[10], (3, D, D), D ** -0.5, 0.25, ((2, 16),)),
        "w_self_out": noise(keys[11], (D, D), (D // 8) ** -0.5, 0.75, ((1, 16),)),
        "w_cross_q": noise(keys[12], (D, D), D ** -0.5, 0.25, ((1, 16),)),
        "w_cross_kv": noise(keys[13], (2, D, D), D ** -0.5, 0.25, ((2, 16),)),
        "w_cross_out": noise(keys[14], (D, D), (D // 16) ** -0.5, 1.0, ((1, 16),)),
        "w_in": noise(keys[15], (D, FF), D ** -0.5, 0.25, ((1, 16),)),
        "w_out": noise(keys[16], (FF, D), FF ** -0.5, 0.125, ((1, 16),)),
        "biases": noise(keys[17], (10, D), 0.3, 3.0, ((1, 16),)),
        "gains": jnp.clip(1.0 + 0.15 * jax.random.normal(keys[18], (3, D), jnp.float32), 0.25, 1.75).astype(jnp.bfloat16),
        "b_hidden": noise(keys[19], (FF,), 0.3, 3.0, ((0, 16),)),
        "lang_table": noise(keys[20], (LANGS, D), 0.5, 4.0, ((1, 16),)),
    }


@jax.custom_vjp
def low(v):
    return lax.optimization_barrier(v.astype(jnp.bfloat16)).astype(jnp.float32)

@jax.custom_vjp
def low_back(v):
    return v

def low_keep(v):
    return (low(v), None)

def low_pass(kept, grad):
    return (grad,)

def back_keep(v):
    return (v, None)

def back_low(kept, grad):
    return (low(grad),)
low.defvjp(low_keep, low_pass)
low_back.defvjp(back_keep, back_low)
EPSILON = 1e-05
MASKED = -1000000000.0
HIGHEST = lax.Precision.HIGHEST

def round_both(value):
    return low(low_back(value))

def product(left, right):
    return jnp.dot(left, right, precision=HIGHEST)

def layer_norm(value, gain_row, shift_row):
    average = lax.optimization_barrier(jnp.mean(value, axis=-1, keepdims=True))
    centred = value - average
    variance = lax.optimization_barrier(jnp.mean(centred * centred, axis=-1, keepdims=True))
    return centred * lax.rsqrt(variance + EPSILON) * gain_row + shift_row

def split_heads(value):
    return value.reshape(value.shape[0], HEADS, HD)

def select_glance(segments, hamming_row, priority_row):
    length = segments.shape[0]
    same_doc = segments[:, None] == segments[None, :]
    doc_length = lax.optimization_barrier(jnp.sum(same_doc.astype(jnp.int32), axis=1)).astype(jnp.int32)
    slots = jnp.arange(hamming_row.shape[0], dtype=jnp.int32)
    wanted = lax.optimization_barrier(jnp.sum(jnp.where(segments[:, None] == slots[None, :], hamming_row[None, :], 0), axis=1)).astype(jnp.int32)
    glance_count = (jnp.minimum(wanted, doc_length) + 1) // 2
    position = jnp.arange(length, dtype=jnp.int32)
    ranked_ahead = (priority_row[None, :] > priority_row[:, None]) | (priority_row[None, :] == priority_row[:, None]) & (position[None, :] < position[:, None])
    rank_in_doc = lax.optimization_barrier(jnp.sum((same_doc & ranked_ahead).astype(jnp.int32), axis=1)).astype(jnp.int32)
    return rank_in_doc < glance_count

def attend(queries, key_rows, value_rows, allowed, scaling):
    length = queries.shape[0]
    block_rows = min(512, length)
    blocks = length // block_rows
    query_blocks = queries.reshape(blocks, block_rows, queries.shape[1], queries.shape[2])
    mask_blocks = allowed.reshape(blocks, block_rows, allowed.shape[1])

    def one_block(pair):
        query_part, mask_part = pair
        scores = low_back(jnp.einsum('qhe,khe->hqk', query_part, key_rows, precision=HIGHEST) * scaling)
        scores = jnp.where(mask_part[None], scores, MASKED)
        largest = lax.optimization_barrier(jnp.max(scores, axis=-1, keepdims=True))
        powers = jnp.exp(scores - largest)
        attn_probs = low(powers / lax.optimization_barrier(jnp.sum(powers, axis=-1, keepdims=True)))
        return jnp.einsum('hqk,khe->qhe', attn_probs, value_rows, precision=HIGHEST)
    result = lax.map(jax.checkpoint(one_block), (query_blocks, mask_blocks))
    return result.reshape(queries.shape)

def decoder(inputs, memory_row, same_doc, source_mask, params):
    w_qkv, w_self_o, w_cross_q, w_cross_kv, w_cross_o, w_up, w_down, bias_rows, gain_rows, bias_mid = params
    length = inputs.shape[0]
    scaling = HD ** (-0.5)
    low_in = low(inputs)
    queries = round_both(product(low_in, w_qkv[0]) + bias_rows[0])
    key_self = round_both(product(low_in, w_qkv[1]))
    value_self = round_both(product(low_in, w_qkv[2]) + bias_rows[1])
    context = attend(split_heads(queries), split_heads(key_self), split_heads(value_self), same_doc, scaling)
    context = round_both(context.reshape(length, -1))
    first_sum = inputs + low_back(product(context, w_self_o) + bias_rows[2])
    after_self = layer_norm(first_sum, gain_rows[0], bias_rows[7])
    cross_queries = round_both(product(low(after_self), w_cross_q) + bias_rows[3])
    key_cross = round_both(product(memory_row, w_cross_kv[0]))
    value_cross = round_both(product(memory_row, w_cross_kv[1]) + bias_rows[4])
    context_two = attend(split_heads(cross_queries), split_heads(key_cross), split_heads(value_cross), source_mask, scaling)
    context_two = round_both(context_two.reshape(length, -1))
    second_sum = after_self + low_back(product(context_two, w_cross_o) + bias_rows[5])
    after_cross = layer_norm(second_sum, gain_rows[1], bias_rows[8])
    before_act = low_back(product(low(after_cross), w_up) + bias_mid)
    hidden = low(jax.nn.gelu(before_act, approximate=False))
    third_sum = after_cross + low_back(product(hidden, w_down) + bias_rows[6])
    return layer_norm(third_sum, gain_rows[2], bias_rows[9])

def reference(x_copy, target_embed, memory, cotangent, segment_ids, source_lengths, target_lengths, hamming, priority, lang_tag, w_self_qkv, w_self_out, w_cross_q, w_cross_kv, w_cross_out, w_in, w_out, biases, gains, b_hidden, lang_table):
    params = tuple((weight.astype(jnp.float32) for weight in (w_self_qkv, w_self_out, w_cross_q, w_cross_kv, w_cross_out, w_in, w_out, biases, gains, b_hidden)))
    lang_float = lang_table.astype(jnp.float32)

    def row_step(totals, row_data):
        copy_row, target_row, memory_row, grad_out, raw_segments, source_len, target_len, hamming_row, priority_row, language = row_data
        live = jnp.arange(raw_segments.shape[0], dtype=jnp.int32) < target_len
        segments = jnp.where(live, raw_segments, jnp.int32(hamming_row.shape[0])).astype(jnp.int32)
        copy_float = copy_row.astype(jnp.float32)
        target_float = target_row.astype(jnp.float32)
        memory_float = memory_row.astype(jnp.float32)
        same_doc = segments[:, None] == segments[None, :]
        source_mask = jnp.broadcast_to(jnp.arange(memory_row.shape[0], dtype=jnp.int32)[None, :] < source_len, (segments.shape[0], memory_row.shape[0]))
        glance = select_glance(segments, hamming_row, priority_row)
        first_out = decoder(copy_float + lang_float[language], memory_float, same_doc, source_mask, params)
        mixed = jnp.where(glance[:, None], target_float, copy_float)

        def run_layer(mixed_in, memory_in, lang_in, params_in):
            return decoder(mixed_in + lang_in[language], memory_in, same_doc, source_mask, params_in)
        final_out, pull = jax.vjp(run_layer, mixed, memory_float, lang_float, params)
        live_grad = grad_out.astype(jnp.float32) * live[:, None].astype(jnp.float32)
        grad_in, grad_memory, grad_lang, grad_params = pull(live_grad)
        totals = jax.tree.map(jnp.add, totals, (grad_lang, grad_params))
        return (totals, (first_out.astype(jnp.bfloat16), final_out.astype(jnp.bfloat16), grad_in, grad_memory))
    zero_sums = jax.tree.map(jnp.zeros_like, (lang_float, params))
    totals, outputs = lax.scan(row_step, zero_sums, (x_copy, target_embed, memory, cotangent, segment_ids, source_lengths, target_lengths, hamming, priority, lang_tag))
    first_pass, output, input_grad, memory_grad = outputs
    grad_lang, grad_params = totals
    g_qkv, g_self_o, g_cross_q, g_cross_kv, g_cross_o, g_up, g_down, g_bias, g_gain, g_mid = grad_params
    return (first_pass, output, input_grad, memory_grad, g_qkv, g_self_o, g_cross_q, g_cross_kv, g_cross_o, g_up, g_down, g_bias, g_gain, g_mid, grad_lang)
```

```python
import functools
import math

import jax
import jax.numpy as jnp
from jax import lax
from jax.experimental import pallas as pl
from jax.experimental.pallas import tpu as pltpu
from jax.sharding import PartitionSpec as P

f32, bf16 = jnp.float32, jnp.bfloat16
MESH = pl.DeviceIdType.MESH
VMEM = pltpu.VMEM

HEADS = 8
HD = 64
EPSILON = 1e-05
MASKED = -1000000000.0
LOG2E = 1.4426950408889634
SCORE = LOG2E * HD ** (-0.5)
SCALING = HD ** (-0.5)

NT = (((1,), (1,)), ((), ()))
NN = (((1,), (0,)), ((), ()))
TN = (((0,), (0,)), ((), ()))

BIASES, GAINS = 10, 3


def dot(left, right, form):
    return lax.dot_general(left, right, form, preferred_element_type=f32)


def own_bits(index, depth):
    return [lax.rem(index // (1 << (depth - 1 - j)), 2) for j in range(depth)]


def partner_of(index, bit, depth, j):
    return index + (1 - 2 * bit) * (1 << (depth - 1 - j))


def enter(rep, me, partners, with_rep):
    barrier = pltpu.get_barrier_semaphore()
    for partner in partners:
        pl.semaphore_signal(barrier, inc=1, device_id=(rep, partner), device_id_type=MESH)
    if with_rep:
        pl.semaphore_signal(barrier, inc=1, device_id=(1 - rep, me), device_id_type=MESH)
    pl.semaphore_wait(barrier, len(partners) + int(with_rep))


def gather_kernel(depth, pieces, count, *refs):
    ins, outs = refs[:count], refs[count : 2 * count]
    send, recv, local = refs[2 * count :]
    rep, me = lax.axis_index("rep"), lax.axis_index("dp")
    bits = own_bits(me, depth)
    partners = [partner_of(me, bits[j], depth, j) for j in range(depth)]
    copies = [
        pltpu.make_async_copy(ins[i], outs[i].at[tuple(bits)], local.at[i]) for i in range(count)
    ]
    for copy in copies:
        copy.start()
    enter(rep, me, partners, False)
    for copy in copies:
        copy.wait()
    started = {}
    for tick in range(len(pieces) + depth - 1):
        for j in reversed(range(depth)):
            b = tick - j
            if not 0 <= b < len(pieces):
                continue
            if j > 0:
                started[b, j - 1].wait_recv()
            which, rows, cols = pieces[b]
            part = outs[which].at[(slice(None),) * j + tuple(bits[j:]) + (rows, cols)]
            copy = pltpu.make_async_remote_copy(
                part,
                part,
                send.at[b, j],
                recv.at[b, j],
                device_id=(rep, partners[j]),
                device_id_type=MESH,
            )
            copy.start()
            started[b, j] = copy
    for (b, j), copy in started.items():
        copy.wait_send()
        if j == depth - 1:
            copy.wait_recv()


def gather_all(n, shards, collective_id):
    depth = int(math.log2(n))
    pieces = []
    for i, shard in enumerate(shards):
        r, c = shard.shape
        if c > 512:
            pieces += [(i, slice(None), pl.ds(at, 512)) for at in range(0, c, 512)]
        elif r >= 128:
            pieces += [(i, pl.ds(at, 32), slice(None)) for at in range(0, r, 32)]
        else:
            pieces.append((i, slice(None), slice(None)))
    count = len(shards)
    outs = pl.pallas_call(
        functools.partial(gather_kernel, depth, pieces, count),
        out_shape=[jax.ShapeDtypeStruct((2,) * depth + s.shape, s.dtype) for s in shards],
        in_specs=[pl.BlockSpec(memory_space=pl.ANY)] * count,
        out_specs=[pl.BlockSpec(memory_space=pl.ANY)] * count,
        scratch_shapes=[
            pltpu.SemaphoreType.DMA((len(pieces), depth)),
            pltpu.SemaphoreType.DMA((len(pieces), depth)),
            pltpu.SemaphoreType.DMA((count,)),
        ],
        name="gather_weights",
        compiler_params=pltpu.CompilerParams(collective_id=collective_id, has_side_effects=True),
    )(*shards)
    return [out.reshape(n * s.shape[0], s.shape[1]) for out, s in zip(outs, shards)]


def scatter_kernel(depth, pieces, groups, count, *refs):
    ins, outs = refs[:count], refs[count : 2 * count]
    at = 2 * count
    stages = depth + 1
    gives = {}
    gets = {}
    for group in groups:
        gives[group] = refs[at : at + stages]
        gets[group] = refs[at + stages : at + 2 * stages]
        at += 2 * stages
    send, recv = refs[at:]
    rep, me = lax.axis_index("rep"), lax.axis_index("dp")
    bits = own_bits(me, depth)
    partners = [partner_of(me, bits[j], depth, j) for j in range(depth)]
    enter(rep, me, partners, True)
    started = {}
    for tick in range(len(pieces) + depth + 1):
        for s in reversed(range(depth + 2)):
            b = tick - s
            if not 0 <= b < len(pieces):
                continue
            which, rows, cols, group, slot = pieces[b]
            source = ins[which]
            j = depth - 1 - s
            if s > 0:
                started[b, s - 1].wait_recv()
            if s == depth + 1:
                mine = gives[group][depth][slot].astype(f32)
                outs[which][rows, cols] = mine + gets[group][depth][slot].astype(f32)
                continue
            if j >= 0:
                head = (slice(None),) * j
                tail = tuple(bits[j + 1 :]) + (rows, cols)
                give = head + (1 - bits[j],) + tail
                keep = head + (bits[j],) + tail
                if s == 0:
                    gives[group][0][slot] = source[give].astype(bf16)
                else:
                    got = gets[group][s - 1].at[slot]
                    gives[group][s][slot] = (
                        source[give] + got[head + (1 - bits[j],)].astype(f32)
                    ).astype(bf16)
                    source[keep] = source[keep] + got[head + (bits[j],)].astype(f32)
                target = (rep, partners[j])
            else:
                got = gets[group][s - 1][slot].astype(f32)
                gives[group][s][slot] = (source[tuple(bits) + (rows, cols)] + got).astype(bf16)
                target = (1 - rep, me)
            copy = pltpu.make_async_remote_copy(
                gives[group][s].at[slot],
                gets[group][s].at[slot],
                send.at[b, s],
                recv.at[b, s],
                device_id=target,
                device_id_type=MESH,
            )
            copy.start()
            started[b, s] = copy
    for copy in started.values():
        copy.wait_send()


def scatter_all(n, grads, collective_id):
    depth = int(math.log2(n))
    pieces, views, shapes, sizes = [], [], [], {}
    for i, grad in enumerate(grads):
        r, c = grad.shape[0] // n, grad.shape[1]
        views.append(grad.reshape((2,) * depth + (r, c)))
        shapes.append((r, c))
        high, wide = min(r, 32), min(c, 512)
        for a in range(0, r, high):
            for q in range(0, c, wide):
                slot = sizes.get((high, wide), 0)
                sizes[high, wide] = slot + 1
                pieces.append((i, pl.ds(a, high), pl.ds(q, wide), (high, wide), slot))
    count = len(grads)
    groups = sorted(sizes)
    scratch = []
    for group in groups:
        buffers = [
            VMEM((sizes[group],) + (2,) * max(depth - 1 - s, 0) + group, bf16)
            for s in range(depth + 1)
        ]
        scratch += buffers + buffers
    return pl.pallas_call(
        functools.partial(scatter_kernel, depth, pieces, groups, count),
        out_shape=[jax.ShapeDtypeStruct(s, f32) for s in shapes],
        in_specs=[pl.BlockSpec(memory_space=VMEM)] * count,
        out_specs=[pl.BlockSpec(memory_space=VMEM)] * count,
        scratch_shapes=scratch
        + [
            pltpu.SemaphoreType.DMA((len(pieces), depth + 1)),
            pltpu.SemaphoreType.DMA((len(pieces), depth + 1)),
        ],
        name="scatter_gradients",
        compiler_params=pltpu.CompilerParams(
            collective_id=collective_id, has_side_effects=True, vmem_limit_bytes=60 * 2**20
        ),
    )(*views)


def both_heads(pair, low):
    zero = jnp.zeros_like(pair)
    return jnp.concatenate([jnp.where(low, pair, zero), jnp.where(low, zero, pair)], axis=0)


def twice(bias):
    return bias if bias.shape[0] == 1 else jnp.concatenate([bias, bias], axis=0)


def attend_block(q, k, v, ctx, lse, rows, key_rows, keys, bias, size):
    low = lax.broadcasted_iota(jnp.int32, (size, 128), 1) < HD
    lanes = lax.broadcasted_iota(jnp.int32, (size, 128), 1)
    bias = twice(bias)
    log_sums = jnp.zeros((size, 128), f32)
    for pair in range(HEADS // 2):
        cols = pl.ds(128 * pair, 128)
        s = dot(both_heads(q[rows, cols], low), k[keys, cols], NT) * SCORE + bias
        largest = jnp.max(s, axis=1, keepdims=True)
        powers = jnp.exp2(s - largest)
        total = jnp.sum(powers, axis=1, keepdims=True)
        c = dot(powers.astype(bf16), v[keys, cols], NN) * (1.0 / total)
        ctx[rows, cols] = jnp.where(low, c[:size], c[size:]).astype(bf16)
        if lse is not None:
            log_sum = largest + jnp.log2(total)
            log_sums = jnp.where(lanes == 2 * pair, log_sum[:size], log_sums)
            log_sums = jnp.where(lanes == 2 * pair + 1, log_sum[size:], log_sums)
    if lse is not None:
        lse[key_rows, :] = log_sums


def column_pair(table, rows, pair):
    return jnp.concatenate(
        [table[rows, 2 * pair : 2 * pair + 1], table[rows, 2 * pair + 1 : 2 * pair + 2]], axis=0
    )


def attend_back_block(q, k, v, g, lse, delta, gq, gk_t, gv_t, rows, keys, bias, size):
    low = lax.broadcasted_iota(jnp.int32, (size, 128), 1) < HD
    bias = twice(bias)
    for pair in range(HEADS // 2):
        cols = pl.ds(128 * pair, 128)
        q_two = both_heads(q[rows, cols], low)
        g_two = both_heads(g[rows, cols], low)
        k_pair, v_pair = k[keys, cols], v[keys, cols]
        probs = jnp.exp2(dot(q_two, k_pair, NT) * SCORE + bias - column_pair(lse, rows, pair))
        grad_s = (probs * (dot(g_two, v_pair, NT) - column_pair(delta, rows, pair))).astype(bf16)
        gv_t[cols, keys] += dot(g_two, probs.astype(bf16), TN)
        gk_t[cols, keys] += dot(q_two, grad_s, TN)
        d = dot(grad_s, k_pair, NN)
        gq[rows, cols] = (jnp.where(low, d[:size], d[size:]) * SCALING).astype(bf16)


def head_sums(value):
    rows = value.shape[0]
    lanes = lax.broadcasted_iota(jnp.int32, (rows, 128), 1)
    low = lanes < HD
    result = jnp.zeros((rows, 128), f32)
    for pair in range(HEADS // 2):
        part = value[:, 128 * pair : 128 * pair + 128]
        first = jnp.sum(jnp.where(low, part, 0.0), axis=1, keepdims=True)
        second = jnp.sum(jnp.where(low, 0.0, part), axis=1, keepdims=True)
        result = jnp.where(lanes == 2 * pair, first, result)
        result = jnp.where(lanes == 2 * pair + 1, second, result)
    return result


def blocks(total, size, body):
    def step(i, carry):
        body(pl.ds(pl.multiple_of(i * size, size), size))
        return carry

    lax.fori_loop(0, total // size, step, 0)


def normalise(value):
    average = jnp.mean(value, axis=1, keepdims=True)
    centred = value - average
    scale = lax.rsqrt(jnp.mean(centred * centred, axis=1, keepdims=True) + EPSILON)
    return centred * scale, scale


def normalise_back(grad, gain, hat, scale):
    g = grad * gain
    first = jnp.mean(g, axis=1, keepdims=True)
    second = jnp.mean(g * hat, axis=1, keepdims=True)
    return scale * (g - first - hat * second)


def column_sum(value):
    return jnp.sum(value, axis=0, keepdims=True)


def prepare_kernel(
    x, t, mem, seg_c, seg_r, key_c, key_r, want_c, lang, wq, wk, wv, wck, wcv, small,
    h, q, k, v, ck, cv,
):
    length = x.shape[0]

    def glanced(rows):
        same = seg_c[rows, :] == seg_r[...]
        doc_length = jnp.sum(same.astype(f32), axis=1, keepdims=True)
        ahead = jnp.logical_and(same, key_r[...] > key_c[rows, :])
        rank = jnp.sum(ahead.astype(f32), axis=1, keepdims=True)
        wanted = jnp.minimum(want_c[rows, :], doc_length.astype(jnp.int32))
        count = lax.shift_right_logical(wanted + 1, jnp.int32(1))
        glance = rank < count.astype(f32)
        plain = x[rows, :].astype(f32)
        h[0, rows, :] = plain + lang[...]
        h[1, rows, :] = jnp.where(glance, t[rows, :].astype(f32), plain) + lang[...]

    blocks(length, 128, glanced)

    def cross(rows):
        m = mem[rows, :]
        ck[rows, :] = dot(m, wck[...], NT).astype(bf16)
        cv[rows, :] = (dot(m, wcv[...], NT) + small[4:5, :]).astype(bf16)

    blocks(mem.shape[0], 512, cross)
    for which in range(2):

        def project(rows):
            low = h[which, rows, :].astype(bf16)
            q[which, rows, :] = (dot(low, wq[...], NT) + small[0:1, :]).astype(bf16)
            k[which, rows, :] = dot(low, wk[...], NT).astype(bf16)
            v[which, rows, :] = (dot(low, wv[...], NT) + small[1:2, :]).astype(bf16)

        blocks(length, 512, project)


def windows(length):
    return [w for w in (256, 384, 512, 640) if w < length] + [length]


def windowed(starts, needs, i, length, body):
    need, begin = needs[i], starts[i]
    sizes = windows(length)
    for at, size in enumerate(sizes):
        fits = need <= size
        if at > 0:
            fits = jnp.logical_and(fits, need > sizes[at - 1])

        @pl.when(fits)
        def _():
            start = pl.multiple_of(jnp.minimum(begin, length - size), 128)
            body(pl.ds(start, size))


def self_kernel(starts, needs, q, k, v, seg_c, seg_r, ctx, lse):
    length = q.shape[1]
    size = 128

    def step(i, carry):
        rows = pl.ds(pl.multiple_of(i * size, size), size)

        def body(keys):
            bias = jnp.where(seg_c[rows, :] == seg_r[:, keys], 0.0, MASKED)
            for which in range(2):
                attend_block(
                    q.at[which], k.at[which], v.at[which], ctx.at[which],
                    lse if which == 1 else None, rows, rows, keys, bias, size,
                )

        windowed(starts, needs, i, length, body)
        return carry

    lax.fori_loop(0, length // size, step, 0)


def after_self(ctx, h, wso, wcq, small, a, cq, rows):
    r1 = h + dot(ctx, wso[...], NT) + small[2:3, :]
    hat, scale = normalise(r1)
    value = hat * small[10:11, :] + small[7:8, :]
    a[rows, :] = value
    low = value.astype(bf16)
    cq[rows, :] = (dot(low, wcq[...], NT) + small[3:4, :]).astype(bf16)
    return hat, scale, low


def after_cross(a, ctx2, wco, win, wout, small, hidden_bias, hid, slope, rows):
    r2 = a[rows, :] + dot(ctx2[rows, :], wco[...], NT) + small[5:6, :]
    hat2, scale2 = normalise(r2)
    b = hat2 * small[11:12, :] + small[8:9, :]
    low = b.astype(bf16)
    total = b + small[6:7, :]
    for j in range(win.shape[0] // 512):
        cols = pl.ds(512 * j, 512)
        z = dot(low, win[cols, :], NT) + hidden_bias[:, cols]
        half = 0.5 + 0.5 * lax.erf(z * 0.7071067811865476)
        hidden = (z * half).astype(bf16)
        if hid is not None:
            hid[:, cols] = hidden
            bell = jnp.exp2(z * z * (-0.5 * LOG2E)) * 0.3989422804014327
            slope[:, cols] = half + z * bell
        total = total + dot(hidden, wout[:, cols], NT)
    hat3, scale3 = normalise(total)
    y = hat3 * small[12:13, :] + small[9:10, :]
    return y, (hat2, scale2, low, hat3, scale3)


def first_kernel(
    h, ctx, ck, cv, source_bias, wso, wcq, wco, win, wout, small, hidden_bias,
    out, a, cq, ctx2,
):
    length = h.shape[1]

    def before(rows):
        after_self(ctx[0, rows, :], h[0, rows, :], wso, wcq, small, a, cq, rows)

    blocks(length, 512, before)
    every = pl.ds(0, ck.shape[0])
    blocks(
        length,
        256,
        lambda rows: attend_block(cq, ck, cv, ctx2, None, rows, rows, every, source_bias[...], 256),
    )

    def last(rows):
        y, _ = after_cross(a, ctx2, wco, win, wout, small, hidden_bias, None, None, rows)
        out[rows, :] = y.astype(bf16)

    blocks(length, 512, last)


def layer_kernel(
    h, ctx, ck, cv, mem, cot, live, source_bias,
    wso, wcq, wck, wcv, wco, win, wout, small, hidden_bias,
    out, gr1, gctx, g_mem,
    g_so, g_cq, g_ck, g_cv, g_co, g_in, g_out, g_small, g_hidden,
    cq, ctx2, lse2, hat1, scale1, low1, hid, slope, delta, gcq, gk_low, gv_low, low2, hat2s,
):
    length = h.shape[1]
    big = 512
    a, gctx2 = gr1, gctx
    for ref in (g_so, g_cq, g_co, g_in, g_out, g_small, g_hidden):
        ref[...] = jnp.zeros_like(ref)

    def before(rows):
        hat, scale, low = after_self(ctx[0, rows, :], h[0, rows, :], wso, wcq, small, a, cq, rows)
        hat1[rows, :] = hat
        scale1[rows, :] = scale
        low1[rows, :] = low

    blocks(length, big, before)
    every = pl.ds(0, ck.shape[0])
    blocks(
        length,
        256,
        lambda rows: attend_block(cq, ck, cv, ctx2, lse2, rows, rows, every, source_bias[...], 256),
    )

    def turn(rows):
        y, (hat2, scale2, low, hat3, scale3) = after_cross(
            a, ctx2, wco, win, wout, small, hidden_bias, hid, slope, rows
        )
        out[rows, :] = y.astype(bf16)
        low2[...] = low
        hat2s[...] = hat2
        gy = cot[rows, :].astype(f32) * live[rows, :]
        g_small[12:13, :] += column_sum(gy * hat3)
        g_small[9:10, :] += column_sum(gy)
        gr3 = normalise_back(gy, small[12:13, :], hat3, scale3)
        gf = gr3.astype(bf16)
        g_small[6:7, :] += column_sum(gf.astype(f32))
        gb = gr3
        for j in range(win.shape[0] // 512):
            cols = pl.ds(512 * j, 512)
            gz = (dot(gf, wout[:, cols], NN) * slope[:, cols]).astype(bf16)
            g_out[:, cols] += dot(gf, hid[:, cols], TN)
            g_in[cols, :] += dot(gz, low2[...], TN)
            g_hidden[:, cols] += column_sum(gz.astype(f32))
            gb = gb + dot(gz, win[cols, :], NN)
        hat2 = hat2s[...]
        g_small[11:12, :] += column_sum(gb * hat2)
        g_small[8:9, :] += column_sum(gb)
        gr2 = normalise_back(gb, small[11:12, :], hat2, scale2)
        a[rows, :] = gr2
        go2 = gr2.astype(bf16)
        g_small[5:6, :] += column_sum(go2.astype(f32))
        context = ctx2[rows, :]
        g_co[...] += dot(go2, context, TN)
        back = dot(go2, wco[...], NN).astype(bf16)
        gctx2[rows, :] = back
        delta[rows, :] = head_sums(back.astype(f32) * context.astype(f32))

    blocks(length, big, turn)
    gk_t, gv_t = slope.at[:, pl.ds(0, ck.shape[0])], slope.at[:, pl.ds(ck.shape[0], ck.shape[0])]
    slope[...] = jnp.zeros_like(slope)
    blocks(
        length,
        256,
        lambda rows: attend_back_block(
            cq, ck, cv, gctx2, lse2, delta, gcq, gk_t, gv_t, rows, every, source_bias[...], 256
        ),
    )
    gk_low[...] = (gk_t[...] * SCALING).astype(bf16)
    gv_low[...] = gv_t[...].astype(bf16)
    g_ck[...] = dot(gk_low[...], mem[...], NN)
    g_cv[...] = dot(gv_low[...], mem[...], NN)
    ones = jnp.ones((8, mem.shape[0]), bf16)
    g_small[4:5, :] = dot(ones, gv_low[...], NT)[0:1, :]
    for at in range(0, mem.shape[0], 512):
        cols = pl.ds(at, 512)
        g_mem[cols, :] = dot(gk_low[:, cols], wck[...], TN) + dot(gv_low[:, cols], wcv[...], TN)

    def final(rows):
        gq = gcq[rows, :]
        g_small[3:4, :] += column_sum(gq.astype(f32))
        g_cq[...] += dot(gq, low1[rows, :], TN)
        ga = a[rows, :] + dot(gq, wcq[...], NN)
        hat = hat1[rows, :]
        g_small[10:11, :] += column_sum(ga * hat)
        g_small[7:8, :] += column_sum(ga)
        g1 = normalise_back(ga, small[10:11, :], hat, scale1[rows, :])
        gr1[rows, :] = g1
        go = g1.astype(bf16)
        g_small[2:3, :] += column_sum(go.astype(f32))
        g_so[...] += dot(go, ctx[0, rows, :], TN)
        gctx[rows, :] = dot(go, wso[...], NN).astype(bf16)

    blocks(length, big, final)


def self_back_kernel(
    starts, needs, live_blocks, q, k, v, g, ctx, lse, seg_c, seg_r,
    gq, gk_low, gv_low, delta, gk_t, gv_t,
):
    length = q.shape[1]
    size = 128
    gk_t[...] = jnp.zeros_like(gk_t)
    gv_t[...] = jnp.zeros_like(gv_t)
    gq[...] = jnp.zeros_like(gq)

    def step(i, carry):
        rows = pl.ds(pl.multiple_of(i * size, size), size)
        delta[rows, :] = head_sums(g[rows, :].astype(f32) * ctx[0, rows, :].astype(f32))

        def body(keys):
            bias = jnp.where(seg_c[rows, :] == seg_r[:, keys], 0.0, MASKED)
            attend_back_block(
                q.at[0], k.at[0], v.at[0], g, lse, delta, gq, gk_t, gv_t, rows, keys, bias, size
            )

        windowed(starts, needs, i, length, body)
        return carry

    lax.fori_loop(0, live_blocks[0], step, 0)
    gk_low[...] = (gk_t[...] * SCALING).astype(bf16)
    gv_low[...] = gv_t[...].astype(bf16)


def input_kernel(h, gq, gk_low, gv_low, gr1, wq, wk, wv, g_x, g_q, g_k, g_v, sums):
    length = h.shape[1]
    g_q[...] = jnp.zeros_like(g_q)
    g_k[...] = jnp.zeros_like(g_k)
    g_v[...] = jnp.zeros_like(g_v)
    sums[...] = jnp.zeros_like(sums)
    ones = jnp.ones((8, 512), bf16)

    for at in range(0, length, 512):
        rows = pl.ds(at, 512)
        low = h[0, rows, :].astype(bf16)
        part = gq[rows, :]
        g_q[...] += dot(part, low, TN)
        g_k[...] += dot(gk_low[:, rows], low, NN)
        g_v[...] += dot(gv_low[:, rows], low, NN)
        value = gr1[rows, :] + dot(part, wq[...], NN)
        value = value + dot(gk_low[:, rows], wk[...], TN) + dot(gv_low[:, rows], wv[...], TN)
        g_x[rows, :] = value
        sums[0:1, :] += column_sum(part.astype(f32))
        sums[1:2, :] += dot(ones, gv_low[:, rows], NT)[0:1, :]
        sums[2:3, :] += column_sum(value)


def shape(dims, dtype=f32):
    return jax.ShapeDtypeStruct(dims, dtype)


def call(kernel, name, outs, args, scratch=(), scalars=0, specs=None):
    in_specs = [pl.BlockSpec(memory_space=pltpu.SMEM)] * scalars
    for at in range(scalars, len(args)):
        in_specs.append((specs or {}).get(at) or pl.BlockSpec(memory_space=VMEM))
    return pl.pallas_call(
        kernel,
        out_shape=outs,
        in_specs=in_specs,
        out_specs=[pl.BlockSpec(memory_space=VMEM)] * len(outs),
        scratch_shapes=list(scratch),
        name=name,
        compiler_params=pltpu.CompilerParams(vmem_limit_bytes=61 * 2**20),
    )(*args)


def shards(
    n,
    x_copy,
    target_embed,
    memory,
    cotangent,
    segment_ids,
    source_lengths,
    target_lengths,
    hamming,
    priority,
    lang_tag,
    w_self_qkv,
    w_self_out,
    w_cross_q,
    w_cross_kv,
    w_cross_out,
    w_in,
    w_out,
    biases,
    gains,
    b_hidden,
    lang_table,
):
    length, width = x_copy.shape[1:]
    source = memory.shape[1]
    hidden = b_hidden.shape[0] * n
    share = width // n
    fold = hidden // width
    langs = lang_table.shape[0]
    slots = hamming.shape[1]

    table = jnp.concatenate([biases, gains, lang_table, b_hidden.reshape(fold, share)], axis=0)
    kept = table.shape[0]
    table = jnp.pad(table, ((0, 128 - kept), (0, 0)))
    gathered = gather_all(
        n,
        [
            table.T,
            w_cross_kv[0].T,
            w_cross_kv[1].T,
            w_self_qkv[0].T,
            w_self_qkv[1].T,
            w_self_qkv[2].T,
            w_self_out.T,
            w_cross_q.T,
            w_cross_out.T,
            w_in.T,
            w_out.T,
        ],
        0,
    )
    small_t, wck, wcv, wq, wk, wv, wso, wcq, wco, win, wout = gathered
    small = small_t.T.astype(f32)
    first_lang = BIASES + GAINS
    hidden_bias = small[first_lang + langs : first_lang + langs + fold]
    hidden_bias = hidden_bias.reshape(fold, n, share).transpose(1, 0, 2).reshape(1, hidden)
    lang = lax.dynamic_slice_in_dim(small, first_lang + lang_tag[0], 1, 0)
    small = small[:16]

    target_len = target_lengths[0]
    position = jnp.arange(length, dtype=jnp.int32)
    live = position < target_len
    seg = jnp.where(live, segment_ids[0], slots).astype(jnp.int32)
    wanted = jnp.sum(
        jnp.where(seg[:, None] == jnp.arange(slots, dtype=jnp.int32)[None, :], hamming[0][None, :], 0),
        axis=1,
        keepdims=True,
    )
    key = priority[0] * length + (length - 1 - position)
    same_edge = seg.reshape(length // 128, 128)
    first_seg, last_seg = same_edge[:, 0], same_edge[:, -1]
    begin = jnp.sum((seg[None, :] < first_seg[:, None]).astype(jnp.int32), axis=1)
    end = jnp.sum((seg[None, :] <= last_seg[:, None]).astype(jnp.int32), axis=1)
    starts = begin // 128 * 128
    needs = (end + 127) // 128 * 128 - starts
    live_blocks = ((target_len + 127) // 128).reshape(1)
    seg_c, seg_r = seg[:, None], seg[None, :]
    source_bias = jnp.where(
        jnp.arange(source, dtype=jnp.int32) < source_lengths[0], 0.0, MASKED
    ).astype(f32)[None, :]

    mem = memory[0]
    two = (2, length, width)
    h, q, k, v, ck, cv = call(
        prepare_kernel,
        "prepare",
        [shape(two), shape(two, bf16), shape(two, bf16), shape(two, bf16)]
        + [shape((source, width), bf16)] * 2,
        (
            x_copy[0], target_embed[0], mem, seg_c, seg_r, key[:, None], key[None, :], wanted,
            lang, wq, wk, wv, wck, wcv, small,
        ),
    )
    ctx, lse = call(
        self_kernel,
        "self_attention",
        [shape(two, bf16), shape((length, 128))],
        (starts, needs, q, k, v, seg_c, seg_r),
        scalars=2,
    )

    def part(dims, which):
        block = (1,) + dims[1:]
        return pl.BlockSpec(block, lambda i: (which, 0, 0))

    def one(value, which):
        return lax.slice_in_dim(value, which, which + 1, axis=0)

    flat = (length, width)
    (first,) = call(
        first_kernel,
        "first_pass",
        [shape(flat, bf16)],
        (one(h, 0), one(ctx, 0), ck, cv, source_bias, wso, wcq, wco, win, wout, small, hidden_bias),
        scratch=[VMEM(flat, f32), VMEM(flat, bf16), VMEM(flat, bf16)],
    )
    square = shape((width, width))
    h2, ctx_two = one(h, 1), one(ctx, 1)
    big = 512
    (
        final, gr1, gctx, g_mem, g_so, g_cq, g_ck, g_cv, g_co, g_in, g_out, g_small, g_hidden,
    ) = call(
        layer_kernel,
        "second_pass",
        [shape(flat, bf16), shape(flat), shape(flat, bf16), shape((source, width))]
        + [square] * 5
        + [shape((hidden, width)), shape((width, hidden)), shape((16, width)), shape((1, hidden))],
        (
            h2, ctx_two, ck, cv, mem, cotangent[0], live[:, None].astype(f32), source_bias,
            wso, wcq, wck, wcv, wco, win, wout, small, hidden_bias,
        ),
        scratch=[
            VMEM(flat, bf16), VMEM(flat, bf16), VMEM((length, 128), f32),
            VMEM(flat, f32), VMEM((length, 1), f32), VMEM(flat, bf16),
            VMEM((big, hidden), bf16), VMEM((width, max(hidden, 2 * source)), f32),
            VMEM((length, 128), f32), VMEM(flat, bf16),
            VMEM((width, source), bf16), VMEM((width, source), bf16),
            VMEM((big, width), bf16), VMEM((big, width), f32),
        ],
    )
    gq, gk_low, gv_low = call(
        self_back_kernel,
        "self_attention_back",
        [shape(flat, bf16), shape((width, length), bf16), shape((width, length), bf16)],
        (starts, needs, live_blocks, one(q, 1), one(k, 1), one(v, 1), gctx, ctx_two, lse, seg_c, seg_r),
        scratch=[VMEM((length, 128), f32), VMEM((width, length), f32), VMEM((width, length), f32)],
        scalars=3,
    )
    g_x, g_q, g_k, g_v, sums = call(
        input_kernel,
        "input_gradient",
        [shape(flat), square, square, square, shape((8, width))],
        (h2, gq, gk_low, gv_low, gr1, wq, wk, wv),
    )

    tag = jnp.arange(langs, dtype=jnp.int32) == lang_tag[0]
    g_lang = jnp.where(tag[:, None], sums[2:3], 0.0)
    g_fold = g_hidden.reshape(n, fold, share).transpose(1, 0, 2).reshape(fold, width)
    g_table = jnp.concatenate([sums[0:2], g_small[2:13], g_lang, g_fold], axis=0)
    g_table = jnp.pad(g_table, ((0, 128 - kept), (0, 0))).T
    owned = scatter_all(n, [g_in, g_out, g_co, g_ck, g_cv, g_cq, g_so, g_q, g_k, g_v, g_table], 1)
    o_in, o_out, o_co, o_ck, o_cv, o_cq, o_so, o_q, o_k, o_v, o_table = owned
    o_table = o_table.T
    return (
        first[None],
        final[None],
        g_x[None],
        g_mem[None],
        jnp.stack([o_q.T, o_k.T, o_v.T]),
        o_so.T,
        o_cq.T,
        jnp.stack([o_ck.T, o_cv.T]),
        o_co.T,
        o_in.T,
        o_out.T,
        o_table[:BIASES],
        o_table[BIASES:first_lang],
        o_table[first_lang + langs : kept].reshape(hidden // n),
        o_table[first_lang : first_lang + langs],
    )


def solution(mesh):
    n = mesh.shape["dp"]
    row3, row2, row1 = P(("rep", "dp"), None, None), P(("rep", "dp"), None), P(("rep", "dp"))
    wide, tall, flat = P(None, None, "dp"), P(None, "dp"), P("dp")
    parameters = (wide, tall, tall, wide, tall, tall, tall, tall, tall, flat, tall)
    return jax.shard_map(
        functools.partial(shards, n),
        mesh=mesh,
        in_specs=(row3, row3, row3, row3, row2, row1, row1, row2, row2, row1) + parameters,
        out_specs=(row3, row3, row3, row3) + parameters,
        check_vma=False,
    )
```

```python
import functools
import itertools
import math

import jax
import jax.numpy as jnp
from jax import lax
from jax.experimental import pallas as pl
from jax.experimental.pallas import tpu as pltpu
from jax.sharding import PartitionSpec as P

f32, bf16 = jnp.float32, jnp.bfloat16
MESH = pl.DeviceIdType.MESH
VMEM = pltpu.VMEM

HEADS = 8
HD = 64
EPSILON = 1e-05
MASKED = -1000000000.0
LOG2E = 1.4426950408889634
SCORE = LOG2E * HD ** (-0.5)
SCALING = HD ** (-0.5)

NT = (((1,), (1,)), ((), ()))
NN = (((1,), (0,)), ((), ()))
TN = (((0,), (0,)), ((), ()))

BIASES, GAINS = 10, 3


def dot(left, right, form):
    return lax.dot_general(left, right, form, preferred_element_type=f32)


def own_bits(index, depth):
    return [lax.rem(index // (1 << (depth - 1 - j)), 2) for j in range(depth)]


def partner_of(index, bit, depth, j):
    return index + (1 - 2 * bit) * (1 << (depth - 1 - j))


def enter(rep, me, partners, with_rep):
    barrier = pltpu.get_barrier_semaphore()
    for partner in partners:
        pl.semaphore_signal(barrier, inc=1, device_id=(rep, partner), device_id_type=MESH)
    if with_rep:
        pl.semaphore_signal(barrier, inc=1, device_id=(1 - rep, me), device_id_type=MESH)
    pl.semaphore_wait(barrier, len(partners) + int(with_rep))


def gather_kernel(depth, pieces, count, *refs):
    ins, outs = refs[:count], refs[count : 2 * count]
    send, recv, local = refs[2 * count :]
    rep, me = lax.axis_index("rep"), lax.axis_index("dp")
    bits = own_bits(me, depth)
    partners = [partner_of(me, bits[j], depth, j) for j in range(depth)]
    copies = [
        pltpu.make_async_copy(ins[i], outs[i].at[tuple(bits)], local.at[i]) for i in range(count)
    ]
    for copy in copies:
        copy.start()
    enter(rep, me, partners, False)
    for copy in copies:
        copy.wait()
    started = {}
    for tick in range(len(pieces) + depth - 1):
        for j in reversed(range(depth)):
            b = tick - j
            if not 0 <= b < len(pieces):
                continue
            if j > 0:
                started[b, j - 1].wait_recv()
            which, rows, cols = pieces[b]
            part = outs[which].at[(slice(None),) * j + tuple(bits[j:]) + (rows, cols)]
            copy = pltpu.make_async_remote_copy(
                part,
                part,
                send.at[b, j],
                recv.at[b, j],
                device_id=(rep, partners[j]),
                device_id_type=MESH,
            )
            copy.start()
            started[b, j] = copy
    for (b, j), copy in started.items():
        copy.wait_send()
        if j == depth - 1:
            copy.wait_recv()


def gather_all(n, shards, collective_id):
    depth = int(math.log2(n))
    pieces = []
    for i, shard in enumerate(shards):
        r, c = shard.shape
        if c > 512:
            pieces += [(i, slice(None), pl.ds(at, 512)) for at in range(0, c, 512)]
        elif r >= 128:
            pieces += [(i, pl.ds(at, 32), slice(None)) for at in range(0, r, 32)]
        else:
            pieces.append((i, slice(None), slice(None)))
    count = len(shards)
    outs = pl.pallas_call(
        functools.partial(gather_kernel, depth, pieces, count),
        out_shape=[jax.ShapeDtypeStruct((2,) * depth + s.shape, s.dtype) for s in shards],
        in_specs=[pl.BlockSpec(memory_space=pl.ANY)] * count,
        out_specs=[pl.BlockSpec(memory_space=pl.ANY)] * count,
        scratch_shapes=[
            pltpu.SemaphoreType.DMA((len(pieces), depth)),
            pltpu.SemaphoreType.DMA((len(pieces), depth)),
            pltpu.SemaphoreType.DMA((count,)),
        ],
        name="gather_weights",
        compiler_params=pltpu.CompilerParams(collective_id=collective_id, has_side_effects=True),
    )(*shards)
    return [out.reshape(n * s.shape[0], s.shape[1]) for out, s in zip(outs, shards)]


def scatter_kernel(depth, pieces, groups, count, *refs):
    ins, outs = refs[:count], refs[count : 2 * count]
    at = 2 * count
    stages = depth + 1
    gives = {}
    gets = {}
    for group in groups:
        gives[group] = refs[at : at + stages]
        gets[group] = refs[at + stages : at + 2 * stages]
        at += 2 * stages
    send, recv = refs[at:]
    rep, me = lax.axis_index("rep"), lax.axis_index("dp")
    bits = own_bits(me, depth)
    partners = [partner_of(me, bits[j], depth, j) for j in range(depth)]
    enter(rep, me, partners, True)
    started = {}
    for tick in range(len(pieces) + depth + 1):
        for s in reversed(range(depth + 2)):
            b = tick - s
            if not 0 <= b < len(pieces):
                continue
            which, rows, cols, group, slot = pieces[b]
            source = ins[which]
            j = depth - 1 - s
            if s > 0:
                started[b, s - 1].wait_recv()
            if s == depth + 1:
                mine = gives[group][depth][slot].astype(f32)
                outs[which][rows, cols] = mine + gets[group][depth][slot].astype(f32)
                continue
            if j >= 0:
                head = (slice(None),) * j
                tail = tuple(bits[j + 1 :]) + (rows, cols)
                give = head + (1 - bits[j],) + tail
                keep = head + (bits[j],) + tail
                if s == 0:
                    gives[group][0][slot] = source[give].astype(bf16)
                else:
                    got = gets[group][s - 1].at[slot]
                    gives[group][s][slot] = (
                        source[give] + got[head + (1 - bits[j],)].astype(f32)
                    ).astype(bf16)
                    source[keep] = source[keep] + got[head + (bits[j],)].astype(f32)
                target = (rep, partners[j])
            else:
                got = gets[group][s - 1][slot].astype(f32)
                gives[group][s][slot] = (source[tuple(bits) + (rows, cols)] + got).astype(bf16)
                target = (1 - rep, me)
            copy = pltpu.make_async_remote_copy(
                gives[group][s].at[slot],
                gets[group][s].at[slot],
                send.at[b, s],
                recv.at[b, s],
                device_id=target,
                device_id_type=MESH,
            )
            copy.start()
            started[b, s] = copy
    for copy in started.values():
        copy.wait_send()


def scatter_all(n, grads, collective_id):
    depth = int(math.log2(n))
    pieces, views, shapes, sizes = [], [], [], {}
    for i, grad in enumerate(grads):
        r, c = grad.shape[0] // n, grad.shape[1]
        views.append(grad.reshape((2,) * depth + (r, c)))
        shapes.append((r, c))
        high, wide = min(r, 32), min(c, 512)
        for a in range(0, r, high):
            for q in range(0, c, wide):
                slot = sizes.get((high, wide), 0)
                sizes[high, wide] = slot + 1
                pieces.append((i, pl.ds(a, high), pl.ds(q, wide), (high, wide), slot))
    count = len(grads)
    groups = sorted(sizes)
    scratch = []
    for group in groups:
        buffers = [
            VMEM((sizes[group],) + (2,) * max(depth - 1 - s, 0) + group, bf16)
            for s in range(depth + 1)
        ]
        scratch += buffers + buffers
    return pl.pallas_call(
        functools.partial(scatter_kernel, depth, pieces, groups, count),
        out_shape=[jax.ShapeDtypeStruct(s, f32) for s in shapes],
        in_specs=[pl.BlockSpec(memory_space=VMEM)] * count,
        out_specs=[pl.BlockSpec(memory_space=VMEM)] * count,
        scratch_shapes=scratch
        + [
            pltpu.SemaphoreType.DMA((len(pieces), depth + 1)),
            pltpu.SemaphoreType.DMA((len(pieces), depth + 1)),
        ],
        name="scatter_gradients",
        compiler_params=pltpu.CompilerParams(
            collective_id=collective_id, has_side_effects=True, vmem_limit_bytes=60 * 2**20
        ),
    )(*views)


class Gather:
    lag = 2

    def __init__(self, depth, buffers, pieces, send, recv):
        self.depth, self.buffers, self.pieces = depth, buffers, pieces
        self.send, self.recv = send, recv
        self.rep, self.me = lax.axis_index("rep"), lax.axis_index("dp")
        self.bits = own_bits(self.me, depth)
        self.partners = [partner_of(self.me, self.bits[j], depth, j) for j in range(depth)]
        self.time, self.arrived = 0, set()

    def enter(self):
        enter(self.rep, self.me, self.partners, False)

    def own(self, which):
        return self.buffers[which].at[tuple(self.bits)]

    def transfer(self, b, j):
        which, rows, cols = self.pieces[b]
        part = self.buffers[which].at[(slice(None),) * j + tuple(self.bits[j:]) + (rows, cols)]
        return pltpu.make_async_remote_copy(
            part,
            part,
            self.send.at[b, j],
            self.recv.at[b, j],
            device_id=(self.rep, self.partners[j]),
            device_id_type=MESH,
        )

    def tick(self):
        for j in reversed(range(self.depth)):
            b = self.time - self.lag * j
            if 0 <= b < len(self.pieces):
                if j > 0:
                    self.transfer(b, j - 1).wait_recv()
                self.transfer(b, j).start()
        self.time += 1

    def need(self, count):
        for b in range(count):
            if b in self.arrived:
                continue
            while self.time <= b + self.lag * (self.depth - 1):
                self.tick()
            self.transfer(b, self.depth - 1).wait_recv()
            self.arrived.add(b)

    def finish(self):
        self.need(len(self.pieces))
        for b in range(len(self.pieces)):
            for j in range(self.depth):
                self.transfer(b, j).wait_send()


class Agenda:
    def __init__(self, gap):
        self.gap, self.time, self.flows = gap, 0, []

    def add(self, *flows):
        for steps in flows:
            steps.pop(0)()
            self.flows.append([steps, self.time + self.gap])

    def step(self, *fresh):
        self.time += 1
        for flow in self.flows:
            if flow[0] and flow[1] <= self.time:
                flow[0].pop(0)()
                flow[1] = self.time + self.gap
        self.add(*fresh)

    def busy(self):
        return any(flow[0] for flow in self.flows)

    def round(self):
        for flow in self.flows:
            if flow[0]:
                flow[0].pop(0)()


class Scatter:
    def __init__(self, depth, units, refs, send, recv):
        self.planes, self.units = 1 << (depth - 2), units
        self.rep, self.me = lax.axis_index("rep"), lax.axis_index("dp")
        self.core = lax.rem(self.me, 2)
        self.x = lax.rem(self.me // 2, 2)
        self.plane = self.me // 4
        self.send, self.recv = send, recv
        at, mark = 0, 0
        for unit in units:
            unit["parts"] = []
            planes = list(range(self.planes))
            for part in [[p] for p in planes] if unit["apart"] else [planes]:
                steps = []
                for _ in range(3):
                    steps.append((refs[at], refs[at + 1], mark))
                    at, mark = at + 2, mark + 1
                unit["parts"].append((part, steps))
            unit["across"], unit["last"] = (refs[at], refs[at + 1], mark), (refs[at + 2], refs[at + 3], mark + self.planes - 1)
            at, mark = at + 4, mark + self.planes

    @staticmethod
    def scratch(depth, kinds):
        planes, buffers, marks = 1 << (depth - 2), [], 0
        for wide, kind, apart in kinds:
            half = wide // 2
            for count in [1] * planes if apart else [planes]:
                middle = (count, 32, wide) if kind == 0 else (2 * count, 32, half)
                for dims in [(2 * count, 32, wide), middle, (count, 32, half)]:
                    buffers += [VMEM(dims, bf16)] * 2
                    marks += 1
            buffers += [VMEM((planes, 32, half), bf16), VMEM((planes - 1, 32, half), bf16)]
            buffers += [VMEM((32, half), bf16)] * 2
            marks += planes
        return buffers + [pltpu.SemaphoreType.DMA((marks,))] * 2

    def enter(self):
        barrier = pltpu.get_barrier_semaphore()
        targets = [self.near(dim) for dim in ("core", "x", "rep")]
        targets += [self.far(k)[1] for k in range(1, self.planes)]
        for target in targets:
            pl.semaphore_signal(barrier, inc=1, device_id=target, device_id_type=MESH)
        pl.semaphore_wait(barrier, len(targets))

    def near(self, dim):
        if dim == "rep":
            return (1 - self.rep, self.me)
        if dim == "x":
            return (self.rep, self.me + 2 * (1 - 2 * self.x))
        return (self.rep, self.me + 1 - 2 * self.core)

    def far(self, k):
        plane = lax.rem(self.plane + k, self.planes)
        return plane, (self.rep, plane * 4 + lax.rem(self.me, 4))

    def transfer(self, give, get, mark, target):
        return pltpu.make_async_remote_copy(
            give,
            get,
            self.send.at[mark],
            self.recv.at[mark],
            device_id=target,
            device_id_type=MESH,
        )

    def part(self, which, index):
        unit = self.units[which]
        planes, buffers = unit["parts"][index]
        source, r, a, c0, wide = (unit[name] for name in ("source", "r", "a", "c0", "wide"))
        half, count = wide // 2, len(planes)
        dims = ["core", "x", "rep"] if unit["kind"] == 0 else ["core", "rep", "x"]
        whole = pl.ds(c0, wide)
        mine = pl.ds(pl.multiple_of(c0 + half * self.rep, 128), half)
        other = pl.ds(pl.multiple_of(c0 + half * (1 - self.rep), 128), half)
        mine_got = pl.ds(pl.multiple_of(half * self.rep, 128), half)
        other_got = pl.ds(pl.multiple_of(half * (1 - self.rep), 128), half)

        def rows(plane, x, core):
            return pl.ds(pl.multiple_of((plane * 4 + x * 2 + core) * r + a, 32), 32)

        def moved(step):
            give, get, mark = buffers[step]
            return self.transfer(give, get, mark, self.near(dims[step]))

        def first():
            give = buffers[0][0]
            for x in range(2):
                for i, plane in enumerate(planes):
                    give[x * count + i] = source[rows(plane, x, 1 - self.core), whole].astype(bf16)
            moved(0).start()

        def over_x(step, columns):
            moved(step - 1).wait_recv()
            give, got = buffers[step][0], buffers[step - 1][1]
            for i, plane in enumerate(planes):
                away = rows(plane, 1 - self.x, self.core)
                here = rows(plane, self.x, self.core)
                give[i] = (
                    source[away, columns] + got[(1 - self.x) * count + i].astype(f32)
                ).astype(bf16)
                source[here, columns] = source[here, columns] + got[self.x * count + i].astype(f32)
            moved(step).start()

        def over_rep(step):
            moved(step - 1).wait_recv()
            give, got = buffers[step][0], buffers[step - 1][1]
            for x in range(2) if step == 1 else [self.x]:
                for i, plane in enumerate(planes):
                    at = x * count + i if step == 1 else i
                    here = rows(plane, x, self.core)
                    give[at] = (source[here, other] + got[at, :, other_got].astype(f32)).astype(bf16)
                    source[here, mine] = source[here, mine] + got[at, :, mine_got].astype(f32)
            moved(step).start()

        def summed():
            moved(2).wait_recv()
            got, across = buffers[2][1], unit["across"][0]
            for i, plane in enumerate(planes):
                here = rows(plane, self.x, self.core)
                total = source[here, mine] + got[i].astype(f32)
                source[here, mine] = total
                across[plane] = total.astype(bf16)

        if unit["kind"] == 0:
            return [first, lambda: over_x(1, whole), lambda: over_rep(2), summed]
        return [first, lambda: over_rep(1), lambda: over_x(2, mine), summed]

    def ending(self, which):
        unit = self.units[which]
        source, r, a, c0, wide = (unit[name] for name in ("source", "r", "a", "c0", "wide"))
        out, out_col = unit["out"], unit["out_col"]
        half = wide // 2
        give, get, mark = unit["across"]
        last = self.transfer(*unit["last"], self.near("rep"))
        mine = pl.ds(pl.multiple_of(c0 + half * self.rep, 128), half)

        def sent(k):
            plane, target = self.far(k)
            return self.transfer(give.at[plane], get.at[k - 1], mark + k - 1, target)

        def across():
            for k in range(1, self.planes):
                sent(k).start()

        def total():
            value = source[pl.ds(pl.multiple_of(self.me * r + a, 32), 32), mine]
            for k in range(1, self.planes):
                sent(k).wait_recv()
                value = value + get[k - 1].astype(f32)
            value = value.astype(bf16)
            unit["last"][0][...] = value
            own = pl.ds(pl.multiple_of(out_col + half * self.rep, 128), half)
            out[pl.ds(a, 32), own] = value.astype(f32)
            last.start()

        def rest():
            last.wait_recv()
            other = pl.ds(pl.multiple_of(out_col + half * (1 - self.rep), 128), half)
            out[pl.ds(a, 32), other] = unit["last"][1][...].astype(f32)

        return [across, total, rest]

    def flow(self, which):
        return self.part(which, 0) + self.ending(which)

    def sent(self):
        for which, unit in enumerate(self.units):
            dims = ["core", "x", "rep"] if unit["kind"] == 0 else ["core", "rep", "x"]
            for _, buffers in unit["parts"]:
                for step, (give, get, mark) in enumerate(buffers):
                    self.transfer(give, get, mark, self.near(dims[step])).wait_send()
            give, get, mark = unit["across"]
            for k in range(1, self.planes):
                plane, target = self.far(k)
                self.transfer(give.at[plane], get.at[k - 1], mark + k - 1, target).wait_send()
            self.transfer(*unit["last"], self.near("rep")).wait_send()


def units_of(source, r, out, wide, kinds, apart=False):
    units = []
    for a in range(0, r, 32):
        for c0 in range(0, wide, 512):
            units.append(
                dict(
                    source=source, r=r, a=a, c0=c0, wide=min(512, wide - c0), out=out, out_col=c0,
                    kind=next(kinds) % 2, apart=apart,
                )
            )
    return units


def both_heads(pair, low):
    zero = jnp.zeros_like(pair)
    return jnp.concatenate([jnp.where(low, pair, zero), jnp.where(low, zero, pair)], axis=0)


def twice(bias):
    return bias if bias.shape[0] == 1 else jnp.concatenate([bias, bias], axis=0)


def attend_block(q, k, v, ctx, lse, rows, key_rows, keys, bias, size, after=None):
    low = lax.broadcasted_iota(jnp.int32, (size, 128), 1) < HD
    lanes = lax.broadcasted_iota(jnp.int32, (size, 128), 1)
    bias = twice(bias)
    log_sums = jnp.zeros((size, 128), f32)
    for pair in range(HEADS // 2):
        cols = pl.ds(128 * pair, 128)
        s = dot(both_heads(q[rows, cols], low), k[keys, cols], NT) * SCORE + bias
        largest = jnp.max(s, axis=1, keepdims=True)
        powers = jnp.exp2(s - largest)
        total = jnp.sum(powers, axis=1, keepdims=True)
        c = dot(powers.astype(bf16), v[keys, cols], NN) * (1.0 / total)
        ctx[rows, cols] = jnp.where(low, c[:size], c[size:]).astype(bf16)
        if lse is not None:
            log_sum = largest + jnp.log2(total)
            log_sums = jnp.where(lanes == 2 * pair, log_sum[:size], log_sums)
            log_sums = jnp.where(lanes == 2 * pair + 1, log_sum[size:], log_sums)
        if after is not None:
            after()
    if lse is not None:
        lse[key_rows, :] = log_sums


def column_pair(table, rows, pair):
    return jnp.concatenate(
        [table[rows, 2 * pair : 2 * pair + 1], table[rows, 2 * pair + 1 : 2 * pair + 2]], axis=0
    )


def attend_back_pair(q, k, v, g, lse, delta, gq, gk_t, gv_t, rows, keys, bias, size, pair):
    low = lax.broadcasted_iota(jnp.int32, (size, 128), 1) < HD
    cols = pl.ds(128 * pair, 128)
    q_two = both_heads(q[rows, cols], low)
    g_two = both_heads(g[rows, cols], low)
    k_pair, v_pair = k[keys, cols], v[keys, cols]
    scores = dot(q_two, k_pair, NT) * SCORE + twice(bias)
    probs = jnp.exp2(scores - column_pair(lse, rows, pair))
    grad_s = (probs * (dot(g_two, v_pair, NT) - column_pair(delta, rows, pair))).astype(bf16)
    gv_t[cols, keys] += dot(g_two, probs.astype(bf16), TN)
    gk_t[cols, keys] += dot(q_two, grad_s, TN)
    d = dot(grad_s, k_pair, NN)
    gq[rows, cols] = (jnp.where(low, d[:size], d[size:]) * SCALING).astype(bf16)


def attend_back_block(
    q, k, v, g, lse, delta, gq, gk_t, gv_t, rows, keys, bias, size, after=None
):
    for pair in range(HEADS // 2):
        attend_back_pair(q, k, v, g, lse, delta, gq, gk_t, gv_t, rows, keys, bias, size, pair)
        if after is not None:
            after()


def head_sums(value):
    rows = value.shape[0]
    lanes = lax.broadcasted_iota(jnp.int32, (rows, 128), 1)
    low = lanes < HD
    result = jnp.zeros((rows, 128), f32)
    for pair in range(HEADS // 2):
        part = value[:, 128 * pair : 128 * pair + 128]
        first = jnp.sum(jnp.where(low, part, 0.0), axis=1, keepdims=True)
        second = jnp.sum(jnp.where(low, 0.0, part), axis=1, keepdims=True)
        result = jnp.where(lanes == 2 * pair, first, result)
        result = jnp.where(lanes == 2 * pair + 1, second, result)
    return result


def blocks(total, size, body):
    def step(i, carry):
        body(pl.ds(pl.multiple_of(i * size, size), size))
        return carry

    lax.fori_loop(0, total // size, step, 0)


def normalise(value):
    average = jnp.mean(value, axis=1, keepdims=True)
    centred = value - average
    scale = lax.rsqrt(jnp.mean(centred * centred, axis=1, keepdims=True) + EPSILON)
    return centred * scale, scale


def normalise_back(grad, gain, hat, scale):
    g = grad * gain
    first = jnp.mean(g, axis=1, keepdims=True)
    second = jnp.mean(g * hat, axis=1, keepdims=True)
    return scale * (g - first - hat * second)


def column_sum(value):
    return jnp.sum(value, axis=0, keepdims=True)


def mat(ref):
    value = ref[...]
    return value if value.ndim == 2 else value.reshape(-1, value.shape[-1])


def up_part(win, j):
    if len(win.shape) == 2:
        return win[512 * j : 512 * j + 512, :]
    depth = len(win.shape) - 2
    lead = depth - int(math.log2(512 // win.shape[-2]))
    part = win[tuple((j >> (lead - 1 - i)) & 1 for i in range(lead))]
    return part.reshape(512, part.shape[-1])


def down_part(wout, j):
    if len(wout.shape) == 2:
        return wout[:, 512 * j : 512 * j + 512]
    part = wout[(slice(None),) * (len(wout.shape) - 1) + (slice(512 * j, 512 * j + 512),)]
    return part.reshape(-1, 512)


def prepare_kernel(
    x, t, mem, seg_c, seg_r, key_c, key_r, want_c, lang, wq, wk, wv, wck, wcv, small,
    h, q, k, v, ck, cv,
):
    length = x.shape[0]

    def glanced(rows):
        same = seg_c[rows, :] == seg_r[...]
        doc_length = jnp.sum(same.astype(f32), axis=1, keepdims=True)
        ahead = jnp.logical_and(same, key_r[...] > key_c[rows, :])
        rank = jnp.sum(ahead.astype(f32), axis=1, keepdims=True)
        wanted = jnp.minimum(want_c[rows, :], doc_length.astype(jnp.int32))
        count = lax.shift_right_logical(wanted + 1, jnp.int32(1))
        glance = rank < count.astype(f32)
        plain = x[rows, :].astype(f32)
        h[0, rows, :] = plain + lang[...]
        h[1, rows, :] = jnp.where(glance, t[rows, :].astype(f32), plain) + lang[...]

    blocks(length, 128, glanced)

    def cross(rows):
        m = mem[rows, :]
        ck[rows, :] = dot(m, wck[...], NT).astype(bf16)
        cv[rows, :] = (dot(m, wcv[...], NT) + small[4:5, :]).astype(bf16)

    blocks(mem.shape[0], 512, cross)
    for which in range(2):

        def project(rows):
            low = h[which, rows, :].astype(bf16)
            q[which, rows, :] = (dot(low, wq[...], NT) + small[0:1, :]).astype(bf16)
            k[which, rows, :] = dot(low, wk[...], NT).astype(bf16)
            v[which, rows, :] = (dot(low, wv[...], NT) + small[1:2, :]).astype(bf16)

        blocks(length, 512, project)


def windows(length):
    return [w for w in (256, 384, 512, 640) if w < length] + [length]


def windowed(starts, needs, i, length, body):
    need, begin = needs[i], starts[i]
    sizes = windows(length)
    for at, size in enumerate(sizes):
        fits = need <= size
        if at > 0:
            fits = jnp.logical_and(fits, need > sizes[at - 1])

        @pl.when(fits)
        def _():
            start = pl.multiple_of(jnp.minimum(begin, length - size), 128)
            body(pl.ds(start, size))


def self_kernel(starts, needs, q, k, v, seg_c, seg_r, ctx, lse):
    length = q.shape[1]
    size = 128

    def step(i, carry):
        rows = pl.ds(pl.multiple_of(i * size, size), size)

        def body(keys):
            bias = jnp.where(seg_c[rows, :] == seg_r[:, keys], 0.0, MASKED)
            for which in range(2):
                attend_block(
                    q.at[which], k.at[which], v.at[which], ctx.at[which],
                    lse if which == 1 else None, rows, rows, keys, bias, size,
                )

        windowed(starts, needs, i, length, body)
        return carry

    lax.fori_loop(0, length // size, step, 0)


def after_self(ctx, h, wso, wcq, small, a, cq, rows):
    r1 = h + dot(ctx, mat(wso), NT) + small[2:3, :]
    hat, scale = normalise(r1)
    value = hat * small[10:11, :] + small[7:8, :]
    if a is not None:
        a[rows, :] = value
    low = value.astype(bf16)
    cq[rows, :] = (dot(low, mat(wcq), NT) + small[3:4, :]).astype(bf16)
    return hat, scale, low


def after_cross(a, ctx2, wco, win, wout, small, hidden_bias, hid, slope):
    r2 = a + dot(ctx2, mat(wco), NT) + small[5:6, :]
    hat2, scale2 = normalise(r2)
    b = hat2 * small[11:12, :] + small[8:9, :]
    low = b.astype(bf16)
    total = b + small[6:7, :]
    for j in range(hidden_bias.shape[1] // 512):
        cols = pl.ds(512 * j, 512)
        z = dot(low, up_part(win, j), NT) + hidden_bias[:, cols]
        half = 0.5 + 0.5 * lax.erf(z * 0.7071067811865476)
        hidden = (z * half).astype(bf16)
        if hid is not None:
            hid[:, cols] = hidden
            bell = jnp.exp2(z * z * (-0.5 * LOG2E)) * 0.3989422804014327
            slope[:, cols] = half + z * bell
        total = total + dot(hidden, down_part(wout, j), NT)
    hat3, scale3 = normalise(total)
    y = hat3 * small[12:13, :] + small[9:10, :]
    return y, (hat2, scale2, low, hat3, scale3)


def first_kernel(
    h, ctx, ck, cv, source_bias, wso, wcq, wco, win, wout, small, hidden_bias,
    out, a, cq, ctx2,
):
    length = h.shape[1]

    def before(rows):
        after_self(ctx[0, rows, :], h[0, rows, :], wso, wcq, small, a, cq, rows)

    blocks(length, 512, before)
    every = pl.ds(0, ck.shape[0])
    blocks(
        length,
        256,
        lambda rows: attend_block(cq, ck, cv, ctx2, None, rows, rows, every, source_bias[...], 256),
    )

    def last(rows):
        y, _ = after_cross(
            a[rows, :], ctx2[rows, :], wco, win, wout, small, hidden_bias, None, None
        )
        out[rows, :] = y.astype(bf16)

    blocks(length, 512, last)


def layer_kernel(
    h, ctx, ck, cv, mem, cot, live, source_bias,
    wso, wcq, wck, wcv, wco, win, wout, small, hidden_bias,
    out, gr1, gctx, g_mem,
    g_so, g_cq, g_ck, g_cv, g_co, g_in, g_out, g_small, g_hidden,
    cq, ctx2, lse2, hat1, scale1, low1, hid, slope, delta, gcq, gk_low, gv_low, low2, hat2s,
):
    length = h.shape[1]
    big = 512
    a, gctx2 = gr1, gctx
    for ref in (g_so, g_cq, g_co, g_in, g_out, g_small, g_hidden):
        ref[...] = jnp.zeros_like(ref)

    def before(rows):
        hat, scale, low = after_self(ctx[0, rows, :], h[0, rows, :], wso, wcq, small, a, cq, rows)
        hat1[rows, :] = hat
        scale1[rows, :] = scale
        low1[rows, :] = low

    blocks(length, big, before)
    every = pl.ds(0, ck.shape[0])
    blocks(
        length,
        256,
        lambda rows: attend_block(cq, ck, cv, ctx2, lse2, rows, rows, every, source_bias[...], 256),
    )

    def turn(rows):
        y, (hat2, scale2, low, hat3, scale3) = after_cross(
            a[rows, :], ctx2[rows, :], wco, win, wout, small, hidden_bias, hid, slope
        )
        out[rows, :] = y.astype(bf16)
        low2[...] = low
        hat2s[...] = hat2
        gy = cot[rows, :].astype(f32) * live[rows, :]
        g_small[12:13, :] += column_sum(gy * hat3)
        g_small[9:10, :] += column_sum(gy)
        gr3 = normalise_back(gy, small[12:13, :], hat3, scale3)
        gf = gr3.astype(bf16)
        g_small[6:7, :] += column_sum(gf.astype(f32))
        gb = gr3
        for j in range(win.shape[0] // 512):
            cols = pl.ds(512 * j, 512)
            gz = (dot(gf, wout[:, cols], NN) * slope[:, cols]).astype(bf16)
            g_out[:, cols] += dot(gf, hid[:, cols], TN)
            g_in[cols, :] += dot(gz, low2[...], TN)
            g_hidden[:, cols] += column_sum(gz.astype(f32))
            gb = gb + dot(gz, win[cols, :], NN)
        hat2 = hat2s[...]
        g_small[11:12, :] += column_sum(gb * hat2)
        g_small[8:9, :] += column_sum(gb)
        gr2 = normalise_back(gb, small[11:12, :], hat2, scale2)
        a[rows, :] = gr2
        go2 = gr2.astype(bf16)
        g_small[5:6, :] += column_sum(go2.astype(f32))
        context = ctx2[rows, :]
        g_co[...] += dot(go2, context, TN)
        back = dot(go2, wco[...], NN).astype(bf16)
        gctx2[rows, :] = back
        delta[rows, :] = head_sums(back.astype(f32) * context.astype(f32))

    blocks(length, big, turn)
    gk_t, gv_t = slope.at[:, pl.ds(0, ck.shape[0])], slope.at[:, pl.ds(ck.shape[0], ck.shape[0])]
    slope[...] = jnp.zeros_like(slope)
    blocks(
        length,
        256,
        lambda rows: attend_back_block(
            cq, ck, cv, gctx2, lse2, delta, gcq, gk_t, gv_t, rows, every, source_bias[...], 256
        ),
    )
    gk_low[...] = (gk_t[...] * SCALING).astype(bf16)
    gv_low[...] = gv_t[...].astype(bf16)
    g_ck[...] = dot(gk_low[...], mem[...], NN)
    g_cv[...] = dot(gv_low[...], mem[...], NN)
    ones = jnp.ones((8, mem.shape[0]), bf16)
    g_small[4:5, :] = dot(ones, gv_low[...], NT)[0:1, :]
    for at in range(0, mem.shape[0], 512):
        cols = pl.ds(at, 512)
        g_mem[cols, :] = dot(gk_low[:, cols], wck[...], TN) + dot(gv_low[:, cols], wcv[...], TN)

    def final(rows):
        gq = gcq[rows, :]
        g_small[3:4, :] += column_sum(gq.astype(f32))
        g_cq[...] += dot(gq, low1[rows, :], TN)
        ga = a[rows, :] + dot(gq, wcq[...], NN)
        hat = hat1[rows, :]
        g_small[10:11, :] += column_sum(ga * hat)
        g_small[7:8, :] += column_sum(ga)
        g1 = normalise_back(ga, small[10:11, :], hat, scale1[rows, :])
        gr1[rows, :] = g1
        go = g1.astype(bf16)
        g_small[2:3, :] += column_sum(go.astype(f32))
        g_so[...] += dot(go, ctx[0, rows, :], TN)
        gctx[rows, :] = dot(go, wso[...], NN).astype(bf16)

    blocks(length, big, final)


def self_back_kernel(
    starts, needs, live_blocks, q, k, v, g, ctx, lse, seg_c, seg_r,
    gq, gk_low, gv_low, delta, gk_t, gv_t,
):
    length = q.shape[1]
    size = 128
    gk_t[...] = jnp.zeros_like(gk_t)
    gv_t[...] = jnp.zeros_like(gv_t)
    gq[...] = jnp.zeros_like(gq)

    def step(i, carry):
        rows = pl.ds(pl.multiple_of(i * size, size), size)
        delta[rows, :] = head_sums(g[rows, :].astype(f32) * ctx[0, rows, :].astype(f32))

        def body(keys):
            bias = jnp.where(seg_c[rows, :] == seg_r[:, keys], 0.0, MASKED)
            attend_back_block(
                q.at[0], k.at[0], v.at[0], g, lse, delta, gq, gk_t, gv_t, rows, keys, bias, size
            )

        windowed(starts, needs, i, length, body)
        return carry

    lax.fori_loop(0, live_blocks[0], step, 0)
    gk_low[...] = (gk_t[...] * SCALING).astype(bf16)
    gv_low[...] = gv_t[...].astype(bf16)


def input_kernel(h, gq, gk_low, gv_low, gr1, wq, wk, wv, g_x, g_q, g_k, g_v, sums):
    length = h.shape[1]
    g_q[...] = jnp.zeros_like(g_q)
    g_k[...] = jnp.zeros_like(g_k)
    g_v[...] = jnp.zeros_like(g_v)
    sums[...] = jnp.zeros_like(sums)
    ones = jnp.ones((8, 512), bf16)

    for at in range(0, length, 512):
        rows = pl.ds(at, 512)
        low = h[0, rows, :].astype(bf16)
        part = gq[rows, :]
        g_q[...] += dot(part, low, TN)
        g_k[...] += dot(gk_low[:, rows], low, NN)
        g_v[...] += dot(gv_low[:, rows], low, NN)
        value = gr1[rows, :] + dot(part, wq[...], NN)
        value = value + dot(gk_low[:, rows], wk[...], TN) + dot(gv_low[:, rows], wv[...], TN)
        g_x[rows, :] = value
        sums[0:1, :] += column_sum(part.astype(f32))
        sums[1:2, :] += dot(ones, gv_low[:, rows], NT)[0:1, :]
        sums[2:3, :] += column_sum(value)


def shape(dims, dtype=f32):
    return jax.ShapeDtypeStruct(dims, dtype)


def call(kernel, name, outs, args, scratch=(), scalars=0, specs=None):
    in_specs = [pl.BlockSpec(memory_space=pltpu.SMEM)] * scalars
    for at in range(scalars, len(args)):
        in_specs.append((specs or {}).get(at) or pl.BlockSpec(memory_space=VMEM))
    return pl.pallas_call(
        kernel,
        out_shape=outs,
        in_specs=in_specs,
        out_specs=[pl.BlockSpec(memory_space=VMEM)] * len(outs),
        scratch_shapes=list(scratch),
        name=name,
        compiler_params=pltpu.CompilerParams(vmem_limit_bytes=61 * 2**20),
    )(*args)


def shards_apart(
    n,
    x_copy,
    target_embed,
    memory,
    cotangent,
    segment_ids,
    source_lengths,
    target_lengths,
    hamming,
    priority,
    lang_tag,
    w_self_qkv,
    w_self_out,
    w_cross_q,
    w_cross_kv,
    w_cross_out,
    w_in,
    w_out,
    biases,
    gains,
    b_hidden,
    lang_table,
):
    length, width = x_copy.shape[1:]
    source = memory.shape[1]
    hidden = b_hidden.shape[0] * n
    share = width // n
    fold = hidden // width
    langs = lang_table.shape[0]
    slots = hamming.shape[1]

    table = jnp.concatenate([biases, gains, lang_table, b_hidden.reshape(fold, share)], axis=0)
    kept = table.shape[0]
    table = jnp.pad(table, ((0, 128 - kept), (0, 0)))
    gathered = gather_all(
        n,
        [
            table.T,
            w_cross_kv[0].T,
            w_cross_kv[1].T,
            w_self_qkv[0].T,
            w_self_qkv[1].T,
            w_self_qkv[2].T,
            w_self_out.T,
            w_cross_q.T,
            w_cross_out.T,
            w_in.T,
            w_out.T,
        ],
        0,
    )
    small_t, wck, wcv, wq, wk, wv, wso, wcq, wco, win, wout = gathered
    small = small_t.T.astype(f32)
    first_lang = BIASES + GAINS
    hidden_bias = small[first_lang + langs : first_lang + langs + fold]
    hidden_bias = hidden_bias.reshape(fold, n, share).transpose(1, 0, 2).reshape(1, hidden)
    lang = lax.dynamic_slice_in_dim(small, first_lang + lang_tag[0], 1, 0)
    small = small[:16]

    target_len = target_lengths[0]
    position = jnp.arange(length, dtype=jnp.int32)
    live = position < target_len
    seg = jnp.where(live, segment_ids[0], slots).astype(jnp.int32)
    wanted = jnp.sum(
        jnp.where(seg[:, None] == jnp.arange(slots, dtype=jnp.int32)[None, :], hamming[0][None, :], 0),
        axis=1,
        keepdims=True,
    )
    key = priority[0] * length + (length - 1 - position)
    same_edge = seg.reshape(length // 128, 128)
    first_seg, last_seg = same_edge[:, 0], same_edge[:, -1]
    begin = jnp.sum((seg[None, :] < first_seg[:, None]).astype(jnp.int32), axis=1)
    end = jnp.sum((seg[None, :] <= last_seg[:, None]).astype(jnp.int32), axis=1)
    starts = begin // 128 * 128
    needs = (end + 127) // 128 * 128 - starts
    live_blocks = ((target_len + 127) // 128).reshape(1)
    seg_c, seg_r = seg[:, None], seg[None, :]
    source_bias = jnp.where(
        jnp.arange(source, dtype=jnp.int32) < source_lengths[0], 0.0, MASKED
    ).astype(f32)[None, :]

    mem = memory[0]
    two = (2, length, width)
    h, q, k, v, ck, cv = call(
        prepare_kernel,
        "prepare",
        [shape(two), shape(two, bf16), shape(two, bf16), shape(two, bf16)]
        + [shape((source, width), bf16)] * 2,
        (
            x_copy[0], target_embed[0], mem, seg_c, seg_r, key[:, None], key[None, :], wanted,
            lang, wq, wk, wv, wck, wcv, small,
        ),
    )
    ctx, lse = call(
        self_kernel,
        "self_attention",
        [shape(two, bf16), shape((length, 128))],
        (starts, needs, q, k, v, seg_c, seg_r),
        scalars=2,
    )

    def part(dims, which):
        block = (1,) + dims[1:]
        return pl.BlockSpec(block, lambda i: (which, 0, 0))

    def one(value, which):
        return lax.slice_in_dim(value, which, which + 1, axis=0)

    flat = (length, width)
    (first,) = call(
        first_kernel,
        "first_pass",
        [shape(flat, bf16)],
        (one(h, 0), one(ctx, 0), ck, cv, source_bias, wso, wcq, wco, win, wout, small, hidden_bias),
        scratch=[VMEM(flat, f32), VMEM(flat, bf16), VMEM(flat, bf16)],
    )
    square = shape((width, width))
    h2, ctx_two = one(h, 1), one(ctx, 1)
    big = 512
    (
        final, gr1, gctx, g_mem, g_so, g_cq, g_ck, g_cv, g_co, g_in, g_out, g_small, g_hidden,
    ) = call(
        layer_kernel,
        "second_pass",
        [shape(flat, bf16), shape(flat), shape(flat, bf16), shape((source, width))]
        + [square] * 5
        + [shape((hidden, width)), shape((width, hidden)), shape((16, width)), shape((1, hidden))],
        (
            h2, ctx_two, ck, cv, mem, cotangent[0], live[:, None].astype(f32), source_bias,
            wso, wcq, wck, wcv, wco, win, wout, small, hidden_bias,
        ),
        scratch=[
            VMEM(flat, bf16), VMEM(flat, bf16), VMEM((length, 128), f32),
            VMEM(flat, f32), VMEM((length, 1), f32), VMEM(flat, bf16),
            VMEM((big, hidden), bf16), VMEM((width, max(hidden, 2 * source)), f32),
            VMEM((length, 128), f32), VMEM(flat, bf16),
            VMEM((width, source), bf16), VMEM((width, source), bf16),
            VMEM((big, width), bf16), VMEM((big, width), f32),
        ],
    )
    gq, gk_low, gv_low = call(
        self_back_kernel,
        "self_attention_back",
        [shape(flat, bf16), shape((width, length), bf16), shape((width, length), bf16)],
        (starts, needs, live_blocks, one(q, 1), one(k, 1), one(v, 1), gctx, ctx_two, lse, seg_c, seg_r),
        scratch=[VMEM((length, 128), f32), VMEM((width, length), f32), VMEM((width, length), f32)],
        scalars=3,
    )
    g_x, g_q, g_k, g_v, sums = call(
        input_kernel,
        "input_gradient",
        [shape(flat), square, square, square, shape((8, width))],
        (h2, gq, gk_low, gv_low, gr1, wq, wk, wv),
    )

    tag = jnp.arange(langs, dtype=jnp.int32) == lang_tag[0]
    g_lang = jnp.where(tag[:, None], sums[2:3], 0.0)
    g_fold = g_hidden.reshape(n, fold, share).transpose(1, 0, 2).reshape(fold, width)
    g_table = jnp.concatenate([sums[0:2], g_small[2:13], g_lang, g_fold], axis=0)
    g_table = jnp.pad(g_table, ((0, 128 - kept), (0, 0))).T
    owned = scatter_all(n, [g_in, g_out, g_co, g_ck, g_cv, g_cq, g_so, g_q, g_k, g_v, g_table], 1)
    o_in, o_out, o_co, o_ck, o_cv, o_cq, o_so, o_q, o_k, o_v, o_table = owned
    o_table = o_table.T
    return (
        first[None],
        final[None],
        g_x[None],
        g_mem[None],
        jnp.stack([o_q.T, o_k.T, o_v.T]),
        o_so.T,
        o_cq.T,
        jnp.stack([o_ck.T, o_cv.T]),
        o_co.T,
        o_in.T,
        o_out.T,
        o_table[:BIASES],
        o_table[BIASES:first_lang],
        o_table[first_lang + langs : kept].reshape(hidden // n),
        o_table[first_lang : first_lang + langs],
    )


class Copies:
    def __init__(self, semaphores):
        self.semaphores, self.pending, self.count = semaphores, {}, 0

    def start(self, source, target):
        copy = pltpu.make_async_copy(source, target, self.semaphores.at[self.count])
        copy.start()
        self.pending[self.count] = copy
        self.count += 1
        return self.count - 1

    def wait(self, *which):
        for at in which:
            if at in self.pending:
                self.pending.pop(at).wait()

    def wait_all(self):
        self.wait(*list(self.pending))


def column(row, rows):
    size = 128
    down = lax.broadcasted_iota(jnp.int32, (size, size), 0)
    across = lax.broadcasted_iota(jnp.int32, (size, size), 1)
    return jnp.sum(jnp.where(down == across, row[:, rows], 0.0), axis=1, keepdims=True)


def placed(height, offset):
    down = lax.broadcasted_iota(jnp.int32, (height, 128), 0)
    across = lax.broadcasted_iota(jnp.int32, (height, 128), 1)
    return (across == down + offset).astype(bf16)


def apart(body):
    once = jnp.minimum(lax.axis_index("dp") + 1, 1)

    def step(i, carry):
        body()
        return carry

    lax.fori_loop(0, once, step, 0)


def source_row(source_len, count):
    position = lax.broadcasted_iota(jnp.int32, (1, count), 1)
    return jnp.where(position < source_len[0], 0.0, MASKED)


def forward_kernel(
    depth, target_len, tag, hamming, source_len,
    raw, priority, biases, gains, lang_t, w_in, b_mid,
    x_ref, t_ref, mem_ref, qkv_t, ckv_t, so_t, cq_t, co_t, out_t,
    first, small, seg_c, seg_r, hidden_bias, scale1,
    hat1_ref, low2_ref, q2_ref, k2_ref, v2_ref, lse_ref, ctx2_ref, ck_ref, cv_ref, cq_ref,
    ctxb_ref, lse_cross_ref,
    wq_ref, wk_ref, wv_ref, wck_ref, wcv_ref, wso_ref, wcq_ref, wco_ref, win_ref, wout_ref,
    x, t, mem, small_t, mids, wq, wk, wv, wck, wcv, wso, wcq, wco, win, wout,
    h1, h2, low1, low2, q1, k1, v1, q2, k2, v2, lse, ctx1, ctx2, ck, cv, a1, hat1, cq1, cq,
    ctxb1, ctxb, lse_cross, glance, send, recv, local,
):
    length, count = x.shape[0], mem.shape[0]
    slots, langs = hamming.shape[1], lang_t.shape[1]
    every = (slice(None), slice(None))
    buffers = [small_t, wq, wk, wv, wck, wcv, wso, wcq, mids, wco, win, wout]
    pieces = [(i,) + every for i in range(10)]
    pieces += [(10, pl.ds(at, 32), slice(None)) for at in range(0, w_in.shape[1], 32)]
    pieces += [(11, slice(None), pl.ds(at, 512)) for at in range(0, out_t.shape[1], 512)]
    gather = Gather(depth, buffers, pieces, send, recv)
    copies = Copies(local)
    shares = [qkv_t.at[0], qkv_t.at[1], qkv_t.at[2], ckv_t.at[0], ckv_t.at[1], so_t, cq_t]
    owned = [copies.start(share, gather.own(i + 1)) for i, share in enumerate(shares)]
    owned += [copies.start(co_t, gather.own(9)), copies.start(out_t, gather.own(11))]
    rows_in = [copies.start(a, b) for a, b in ((x_ref, x), (t_ref, t), (mem_ref, mem))]
    table = dot(biases[...], placed(BIASES, langs), TN)
    table = table + dot(gains[...], placed(GAINS, langs + BIASES), TN)
    table = table + dot(lang_t[...], placed(langs, 0), NN)
    small_t[tuple(gather.bits)] = table.astype(bf16)
    win[tuple(gather.bits)] = w_in[...].astype(f32).T.astype(bf16)
    mids[tuple(gather.bits)] = jnp.broadcast_to(b_mid[...], mids.shape[-2:])
    gather.enter()
    copies.wait(*owned)
    gather.tick()
    gather.tick()

    position = lax.broadcasted_iota(jnp.int32, (1, length), 1)
    segments = jnp.where(position < target_len[0], raw[...], slots).astype(f32)
    seg_r[...] = segments
    rank_key = priority[...].astype(f32)
    place = position.astype(f32)

    def glanced(at):
        rows = pl.ds(at, 128)
        seg = column(segments, slice(at, at + 128))
        key = column(rank_key, slice(at, at + 128))
        here = (lax.broadcasted_iota(jnp.int32, (128, 1), 0) + at).astype(f32)
        seg_c[rows, :] = seg
        same = segments == seg
        doc_length = jnp.sum(same.astype(f32), axis=1, keepdims=True)
        ahead = (rank_key > key) | ((rank_key == key) & (place < here))
        rank = jnp.sum((same & ahead).astype(f32), axis=1, keepdims=True)
        wanted = jnp.zeros((128, 1), f32)
        for slot in range(slots):
            wanted = jnp.where(seg == float(slot), hamming[0, slot].astype(f32), wanted)
        glance[rows, :] = (2.0 * rank + 1.0 <= jnp.minimum(wanted, doc_length)).astype(f32)

    for at in range(0, length, 128):
        glanced(at)
        if at % 256 == 128:
            gather.tick()
    gather.need(1)
    items = mat(small_t)
    small[...] = dot(placed(16, langs), items, NT)
    choice = lax.broadcasted_iota(jnp.int32, (8, 128), 1) == tag[0]
    lang = dot(choice.astype(bf16), items, NT)[0:1, :]
    copies.wait(*rows_in)

    def combine(rows):
        plain = x[rows, :].astype(f32)
        one = plain + lang
        two = jnp.where(glance[rows, :] > 0.5, t[rows, :].astype(f32), plain) + lang
        h1[rows, :] = one
        h2[rows, :] = two
        low1[rows, :] = one.astype(bf16)
        low2[rows, :] = two.astype(bf16)

    blocks(length, 256, combine)
    copies.start(low2, low2_ref)

    def project(source, weight, bias, out):
        def step(rows):
            value = dot(source[rows, :], mat(weight), NT)
            if bias is not None:
                value = value + small[bias : bias + 1, :]
            out[rows, :] = value.astype(bf16)

        blocks(source.shape[0], 512, step)

    for at, (weight, bias, one, two) in enumerate(
        [(wq, 0, q1, q2), (wk, None, k1, k2), (wv, 1, v1, v2)]
    ):
        gather.need(2 + at)
        project(low1, weight, bias, one)
        project(low2, weight, bias, two)
    for source, target in ((q2, q2_ref), (k2, k2_ref), (v2, v2_ref)):
        copies.start(source, target)

    def pause():
        gather.tick()
        gather.tick()

    every_row = pl.ds(0, length)
    for q, k, v, ctx, log_sums in ((q1, k1, v1, ctx1, None), (q2, k2, v2, ctx2, lse)):
        for at in range(0, length, 256):

            def one_block():
                rows = pl.ds(at, 256)
                masked = jnp.where(seg_c[rows, :] == seg_r[...], 0.0, MASKED)
                attend_block(q, k, v, ctx, log_sums, rows, rows, every_row, masked, 256)

            apart(one_block)
            pause()
    copies.start(ctx2, ctx2_ref)
    copies.start(lse, lse_ref)
    gather.need(8)
    project(mem, wck, None, ck)
    project(mem, wcv, 4, cv)
    copies.start(ck, ck_ref)
    copies.start(cv, cv_ref)
    pause()

    def start_one(rows):
        after_self(ctx1[rows, :], h1[rows, :], wso, wcq, small, a1, cq1, rows)

    def start_two(rows):
        hat, scale, _ = after_self(ctx2[rows, :], h2[rows, :], wso, wcq, small, None, cq, rows)
        hat1[rows, :] = hat
        scale1[rows, :] = scale

    blocks(length, 512, start_one)
    pause()
    blocks(length, 512, start_two)
    copies.start(hat1, hat1_ref)
    copies.start(cq, cq_ref)
    pause()
    every_key = pl.ds(0, count)
    source_bias = source_row(source_len, count)
    for query, context, log_sums in ((cq, ctxb, lse_cross), (cq1, ctxb1, None)):
        for at in range(0, length, 256):

            def one_block():
                rows = pl.ds(at, 256)
                attend_block(
                    query, ck, cv, context, log_sums, rows, rows, every_key, source_bias, 256
                )

            apart(one_block)
            pause()
        if log_sums is not None:
            copies.start(ctxb, ctxb_ref)
            copies.start(lse_cross, lse_cross_ref)
    gather.finish()
    for source, target in (
        (wq, wq_ref), (wk, wk_ref), (wv, wv_ref), (wck, wck_ref), (wcv, wcv_ref), (wso, wso_ref),
        (wcq, wcq_ref), (wco, wco_ref), (win, win_ref), (wout, wout_ref),
    ):
        copies.start(source, target)
    for i in range(2**depth):
        owner = mids.at[tuple((i >> (depth - 1 - j)) & 1 for j in range(depth))]
        hidden_bias[:, 128 * i : 128 * i + 128] = owner[0:1, :].astype(f32)

    def last(rows):
        y, _ = after_cross(
            a1[rows, :], ctxb1[rows, :], wco, win, wout, small, hidden_bias, None, None
        )
        first[rows, :] = y.astype(bf16)

    blocks(length, 512, last)
    copies.wait_all()


def turn_kernel(
    depth, slots, source_len,
    scale1, seg_c, small, hidden_bias,
    hat1_ref, ctxb_ref, wco_ref, win_ref, wout_ref, cot_ref,
    cq_ref, ck_ref, cv_ref, lse_ref, mem_ref, wck_ref, wcv_ref, wcq_ref, wso_ref, ctx_ref,
    gr1, gctx, g_so, g_cq, g_ck, g_cv, g_small, g_hidden, o_in, o_out, o_co, out_ref, g_mem_ref,
    hat1, ctxb, wco, win, wout, cq, ck, cv, lse, mem, wck, wcv, wcq, wso, ctx,
    g_in, g_out, g_co, hid, slope, delta, gcq, low2, hat2s, *rest,
):
    length, count = cq.shape[0], ck.shape[0]
    big = 512
    send, recv, local = rest[-3:]
    kinds = itertools.count()
    units = (
        units_of(g_out, g_out.shape[0] >> depth, o_out, g_out.shape[1], kinds)
        + units_of(g_in, g_in.shape[0] >> depth, o_in, g_in.shape[1], kinds)
        + units_of(g_co, g_co.shape[0] >> depth, o_co, g_co.shape[1], kinds)
    )
    downs = g_out.shape[1] // 512
    scatter = Scatter(depth, units, rest[:-3], send, recv)
    agenda = Agenda(3)
    copies = Copies(local)
    pairs = [
        (hat1_ref, hat1), (ctxb_ref, ctxb), (wco_ref, wco), (win_ref, win), (wout_ref, wout),
        (cot_ref, gctx),
        (cq_ref, cq), (ck_ref, ck), (cv_ref, cv), (lse_ref, lse),
        (mem_ref, mem), (wck_ref, wck), (wcv_ref, wcv), (wcq_ref, wcq), (wso_ref, wso), (ctx_ref, ctx),
    ]
    fetched = [copies.start(source, target) for source, target in pairs]
    for ref in (g_so, g_cq, g_co, g_in, g_out, g_small, g_hidden):
        ref[...] = jnp.zeros_like(ref)
    scatter.enter()
    copies.wait(*fetched[:3])

    out = gcq
    for at in range(0, length, big):
        rows = pl.ds(at, big)
        final = at + big == length
        a = hat1[rows, :] * small[10:11, :] + small[7:8, :]
        copies.wait(*fetched[3:6])
        y, (hat2, scale2, low, hat3, scale3) = after_cross(
            a, ctxb[rows, :], wco, win, wout, small, hidden_bias, hid, slope
        )
        out[rows, :] = y.astype(bf16)
        low2[...] = low
        hat2s[...] = hat2
        live = (seg_c[rows, :] < slots - 0.5).astype(f32)
        gy = gctx[rows, :].astype(f32) * live
        g_small[12:13, :] += column_sum(gy * hat3)
        g_small[9:10, :] += column_sum(gy)
        gr3 = normalise_back(gy, small[12:13, :], hat3, scale3)
        gf = gr3.astype(bf16)
        g_small[6:7, :] += column_sum(gf.astype(f32))
        gb = gr3
        for j in range(downs):
            cols = pl.ds(512 * j, 512)
            gz = (dot(gf, down_part(wout, j), NN) * slope[:, cols]).astype(bf16)
            g_out[:, cols] += dot(gf, hid[:, cols], TN)
            g_in[cols, :] += dot(gz, low2[...], TN)
            g_hidden[:, cols] += column_sum(gz.astype(f32))
            gb = gb + dot(gz, up_part(win, j), NN)
            if final:
                agenda.step(scatter.flow(j))
        hat2 = hat2s[...]
        g_small[11:12, :] += column_sum(gb * hat2)
        g_small[8:9, :] += column_sum(gb)
        gr2 = normalise_back(gb, small[11:12, :], hat2, scale2)
        gr1[rows, :] = gr2
        go2 = gr2.astype(bf16)
        g_small[5:6, :] += column_sum(go2.astype(f32))
        context = ctxb[rows, :]
        g_co[...] += dot(go2, context, TN)
        back = dot(go2, mat(wco), NN).astype(bf16)
        gctx[rows, :] = back
        delta[rows, :] = head_sums(back.astype(f32) * context.astype(f32))

    keep_out = copies.start(out, out_ref)
    waiting = list(range(downs, len(units)))
    agenda.step(scatter.flow(waiting.pop(0)))
    gk_t, gv_t = slope.at[:, pl.ds(0, count)], slope.at[:, pl.ds(count, count)]
    slope[...] = jnp.zeros_like(slope)
    copies.wait(keep_out, *fetched[6:10])
    every = pl.ds(0, count)
    source_bias = source_row(source_len, count)

    def pause():
        agenda.step(*([scatter.flow(waiting.pop(0))] if waiting else []))

    for at in range(0, length, 256):
        attend_back_block(
            cq, ck, cv, gctx, lse, delta, gcq, gk_t, gv_t, pl.ds(at, 256), every, source_bias, 256,
            pause,
        )
    copies.wait(*fetched[10:])
    gk_low, gv_low = hid.at[:, pl.ds(0, count)], hid.at[:, pl.ds(count, count)]
    gk_low[...] = (gk_t[...] * SCALING).astype(bf16)
    gv_low[...] = gv_t[...].astype(bf16)
    g_ck[...] = dot(gk_low[...], mem[...], NN)
    agenda.step()
    g_cv[...] = dot(gv_low[...], mem[...], NN)
    agenda.step()
    ones = jnp.ones((8, count), bf16)
    g_small[4:5, :] = dot(ones, gv_low[...], NT)[0:1, :]
    for i, at in enumerate(range(0, count, 512)):
        cols = pl.ds(at, 512)
        place = slope.at[:, pl.ds(512 * i, 512)]
        place[...] = dot(gk_low[:, cols], mat(wck), TN) + dot(gv_low[:, cols], mat(wcv), TN)
        copies.start(place, g_mem_ref.at[cols, :])
        agenda.step()
    for at in range(0, length, big):
        rows = pl.ds(at, big)
        gq = gcq[rows, :]
        hat = hat1[rows, :]
        low = (hat * small[10:11, :] + small[7:8, :]).astype(bf16)
        g_small[3:4, :] += column_sum(gq.astype(f32))
        g_cq[...] += dot(gq, low, TN)
        ga = gr1[rows, :] + dot(gq, mat(wcq), NN)
        g_small[10:11, :] += column_sum(ga * hat)
        g_small[7:8, :] += column_sum(ga)
        g1 = normalise_back(ga, small[10:11, :], hat, scale1[rows, :])
        gr1[rows, :] = g1
        go = g1.astype(bf16)
        g_small[2:3, :] += column_sum(go.astype(f32))
        agenda.step()
        g_so[...] += dot(go, ctx[rows, :], TN)
        gctx[rows, :] = dot(go, mat(wso), NN).astype(bf16)
        agenda.step()
    while agenda.busy():
        agenda.round()
    scatter.sent()
    copies.wait_all()


def close_kernel(
    depth, most, tag,
    seg_c, seg_r, g_small, g_hidden,
    gctx_ref, ctx_ref, q_ref, k_ref, v_ref, lse_ref, ck_ref, cv_ref, cq_ref, so_ref, low_ref,
    gr1_ref, wq_ref, wk_ref, wv_ref,
    g_x, o_qkv, o_ckv, o_cq, o_so, o_table,
    gctx, ctx, q, k, v, lse, g_ck, g_cv, g_cq, g_so, low, wq, wk, wv,
    g_q, g_k, g_v, gq, gk_t, gv_t, gk_low, gv_low, delta, lines, table, *rest,
):
    length = q.shape[0]
    size = 256
    send, recv, local = rest[-3:]
    kinds = itertools.count()
    width = g_q.shape[0]
    share = width >> depth
    units = []
    for source, out in [(g_ck, o_ckv.at[0]), (g_cv, o_ckv.at[1]), (g_cq, o_cq), (g_so, o_so)]:
        units += units_of(source, share, out, width, kinds)
    for i, source in enumerate((g_q, g_k, g_v)):
        units += units_of(source, share, o_qkv.at[i], width, kinds, apart=True)
    units += units_of(table, share, o_table, table.shape[1], kinds)
    scatter = Scatter(depth, units, rest[:-3], send, recv)
    agenda = Agenda(4)
    copies = Copies(local)
    pairs = [
        (gctx_ref, gctx), (ctx_ref, ctx), (q_ref, q), (k_ref, k), (v_ref, v), (lse_ref, lse),
        (ck_ref, g_ck), (cv_ref, g_cv), (cq_ref, g_cq), (so_ref, g_so),
        (low_ref, low), (gr1_ref, g_x), (wq_ref, wq), (wk_ref, wk), (wv_ref, wv),
    ]
    fetched = [copies.start(source, target) for source, target in pairs]
    scatter.enter()
    for ref in (gk_t, gv_t, lines, table):
        ref[...] = jnp.zeros_like(ref)
    copies.wait(*fetched[:2])
    for at in range(0, length, 512):
        rows = pl.ds(at, 512)
        delta[rows, :] = head_sums(gctx[rows, :].astype(f32) * ctx[rows, :].astype(f32))
    copies.wait(*fetched[2:10])
    agenda.add(scatter.flow(0), scatter.flow(1))
    early = [2, 3]
    for pair in range(HEADS // 2):
        cols = pl.ds(128 * pair, 128)
        for at in range(0, length, size):
            begin = max(0, (at - most + 1) // 128 * 128)
            end = min(length, (at + size + most - 1 + 127) // 128 * 128)
            rows, keys = pl.ds(at, size), pl.ds(begin, end - begin)
            masked = jnp.where(seg_c[rows, :] == seg_r[:, keys], 0.0, MASKED)
            attend_back_pair(
                q, k, v, gctx, lse, delta, gq, gk_t, gv_t, rows, keys, masked, size, pair
            )
            agenda.step(*([scatter.flow(early.pop(0))] if early and at > 0 else []))
        copies.wait(*fetched[10:])
        gk_low[cols, :] = (gk_t[cols, :] * SCALING).astype(bf16)
        gv_low[cols, :] = gv_t[cols, :].astype(bf16)
        g_q[cols, :] = dot(gq[:, cols], low[...], TN)
        g_k[cols, :] = dot(gk_low[cols, :], low[...], NN)
        g_v[cols, :] = dot(gv_low[cols, :], low[...], NN)
        agenda.step(*[scatter.part(4 + i, pair) for i in range(3)])
    ones = jnp.ones((8, length), bf16)
    sums = [
        dot(ones, gq[...], NN)[0:1, :],
        dot(ones, gk_low[...], NT)[0:1, :],
        dot(ones, gv_low[...], NT)[0:1, :],
    ]
    total = column_sum(g_x[...])
    down = lax.broadcasted_iota(jnp.int32, (8, width), 0)
    for value, weight in zip(sums, (wq, wk, wv)):
        top = value.astype(bf16)
        middle = (value - top.astype(f32)).astype(bf16)
        bottom = (value - top.astype(f32) - middle.astype(f32)).astype(bf16)
        split = jnp.where(down == 0, top.astype(f32), jnp.where(down == 1, middle.astype(f32), 0.0))
        split = jnp.where(down == 2, bottom.astype(f32), split).astype(bf16)
        total = total + column_sum(dot(split, mat(weight), NN))
    langs = lines.shape[0] // 2
    lines[langs : langs + 16, :] = g_small[...]
    lines[langs : langs + 1, :] = sums[0]
    lines[langs + 1 : langs + 2, :] = sums[2]
    down = lax.broadcasted_iota(jnp.int32, lines.shape, 0)
    table[:, 0:128] = jnp.where(down == tag[0], total, lines[...]).T
    for owner in range(2**depth):
        table[share * owner : share * owner + 1, 128:256] = g_hidden[:, 128 * owner : 128 * owner + 128]
    agenda.step(scatter.flow(7))
    for at in range(0, length, 256):
        rows = pl.ds(at, 256)
        value = g_x[rows, :] + dot(gq[rows, :], mat(wq), NN)
        value = value + dot(gk_low[:, rows], mat(wk), TN) + dot(gv_low[:, rows], mat(wv), TN)
        g_x[rows, :] = value
        agenda.round()
    while agenda.busy():
        agenda.round()
    endings = [scatter.ending(4 + i) for i in range(3)]
    while endings[0]:
        for steps in endings:
            steps.pop(0)()
    scatter.sent()


def finish_kernel(langs, qkv, ckv, cq, so, co, up, down, table, *outs):
    for source, out in zip((qkv, ckv, cq, so, co, down), outs):
        out[...] = source[...]
    outs[6][...] = up[...].T
    items = table[:, 0:128]
    lines = items.T
    outs[7][...] = lines[langs : langs + BIASES, :]
    outs[8][...] = lines[langs + BIASES : langs + BIASES + GAINS, :]
    outs[9][...] = table[0:1, 128:256]
    outs[10][...] = items[:, 0:langs]


def transfer_call(kernel, name, collective_id, outs, args, scratch, scalars, away, away_out):
    in_specs = [pl.BlockSpec(memory_space=pltpu.SMEM)] * scalars
    for at in range(scalars, len(args)):
        in_specs.append(pl.BlockSpec(memory_space=pl.ANY if at >= away else VMEM))
    out_specs = [
        pl.BlockSpec(memory_space=pl.ANY if at >= away_out else VMEM) for at in range(len(outs))
    ]
    return pl.pallas_call(
        kernel,
        out_shape=outs,
        in_specs=in_specs,
        out_specs=out_specs,
        scratch_shapes=list(scratch),
        name=name,
        compiler_params=pltpu.CompilerParams(
            collective_id=collective_id, has_side_effects=True, vmem_limit_bytes=62 * 2**20
        ),
    )(*args)


def shards(
    n,
    x_copy,
    target_embed,
    memory,
    cotangent,
    segment_ids,
    source_lengths,
    target_lengths,
    hamming,
    priority,
    lang_tag,
    w_self_qkv,
    w_self_out,
    w_cross_q,
    w_cross_kv,
    w_cross_out,
    w_in,
    w_out,
    biases,
    gains,
    b_hidden,
    lang_table,
):
    depth = int(math.log2(n))
    length, width = x_copy.shape[1:]
    source = memory.shape[1]
    hidden = b_hidden.shape[0] * n
    share = width // n
    langs = lang_table.shape[0]
    most = 256
    bits = (2,) * depth
    flat, side = (length, width), (source, width)
    lse = (length, 128)
    whole, up, down = bits + (share, width), bits + (hidden // n, width), bits + (share, hidden)
    square = (width, width)
    mem = memory[0]

    def low(dims):
        return shape(dims, bf16)

    def scratch(*all_dims, dtype=bf16):
        return [VMEM(dims, dtype) for dims in all_dims]

    kept = [
        shape(flat), low(flat), low(flat), low(flat), low(flat), shape(lse), low(flat), low(side),
        low(side), low(flat), low(flat), shape(lse),
    ]
    weights = [low(whole)] * 8 + [low(up), low(down)]
    pieces = 10 + hidden // n // 32 + hidden // 512
    (
        first, small, seg_c, seg_r, hidden_bias, scale1,
        hat1, low2, q, k, v, lse_self, ctx, ck, cv, cq, ctxb, lse_cross,
        wq, wk, wv, wck, wcv, wso, wcq, wco, win, wout,
    ) = transfer_call(
        functools.partial(forward_kernel, depth),
        "forward",
        2,
        [
            low(flat), shape((16, width)), shape((length, 1)), shape((1, length)),
            shape((1, hidden)), shape((length, 1)),
        ]
        + kept
        + weights,
        (
            target_lengths, lang_tag, hamming, source_lengths, segment_ids, priority, biases, gains,
            lang_table.T, w_in, b_hidden[None], x_copy[0], target_embed[0], mem,
            w_self_qkv.transpose(0, 2, 1), w_cross_kv.transpose(0, 2, 1), w_self_out.T,
            w_cross_q.T, w_cross_out.T, w_out.T,
        ),
        scratch(flat, flat, side, bits + (share, 128), bits + (16, 128), *[whole] * 8, up, down)
        + scratch(flat, flat, dtype=f32)
        + scratch(*[flat] * 8)
        + scratch(lse, dtype=f32)
        + scratch(flat, flat, side, side)
        + scratch(flat, flat, dtype=f32)
        + scratch(*[flat] * 4)
        + scratch(lse, (length, 1), dtype=f32)
        + [pltpu.SemaphoreType.DMA((pieces, depth))] * 2
        + [pltpu.SemaphoreType.DMA((40,))],
        4,
        11,
        6,
    )
    big = 512
    blocks_in, blocks_out = hidden // n // 32, hidden // 512
    kinds = [(512, i % 2, False) for i in range(blocks_in + blocks_out + 1)]
    (
        gr1, gctx, g_so, g_cq, g_ck, g_cv, g_small, g_hidden, o_in, o_out, o_co, out, g_mem,
    ) = transfer_call(
        functools.partial(turn_kernel, depth, hamming.shape[1]),
        "turn",
        3,
        [shape(flat), low(flat)]
        + [shape(square)] * 4
        + [
            shape((16, width)), shape((1, hidden)), shape((hidden // n, width)),
            shape((share, hidden)), shape((share, width)), low(flat), shape(side),
        ],
        (
            source_lengths, scale1, seg_c, small, hidden_bias,
            hat1, ctxb, wco, win, wout, cotangent[0], cq, ck, cv, lse_cross, mem, wck, wcv, wcq,
            wso, ctx,
        ),
        scratch(flat, dtype=f32)
        + scratch(flat, whole, up, down, flat, side, side)
        + scratch(lse, dtype=f32)
        + scratch(side, whole, whole, whole, whole, flat)
        + scratch((hidden, width), (width, hidden), square, dtype=f32)
        + scratch((big, hidden))
        + scratch((width, max(hidden, 2 * source)), lse, dtype=f32)
        + scratch(flat, (big, width))
        + scratch((big, width), dtype=f32)
        + Scatter.scratch(depth, kinds)
        + [pltpu.SemaphoreType.DMA((24,))],
        1,
        5,
        11,
    )
    kinds = [(512, i % 2, i >= 4) for i in range(7)] + [(256, 1, False)]
    turned = (width, length)
    g_x, o_qkv, o_ckv, o_cq, o_so, o_table = transfer_call(
        functools.partial(close_kernel, depth, most),
        "close",
        4,
        [
            shape(flat), shape((3, share, width)), shape((2, share, width)),
            shape((share, width)), shape((share, width)), shape((share, 256)),
        ],
        (
            lang_tag, seg_c, seg_r, g_small, g_hidden,
            gctx, ctx, q, k, v, lse_self, g_ck, g_cv, g_cq, g_so, low2, gr1, wq, wk, wv,
        ),
        scratch(*[flat] * 5)
        + scratch(lse, *[square] * 4, dtype=f32)
        + scratch(flat, whole, whole, whole)
        + scratch(*[square] * 3, dtype=f32)
        + scratch(flat)
        + scratch(turned, turned, dtype=f32)
        + scratch(turned, turned)
        + scratch(lse, (2 * langs, width), (width, 256), dtype=f32)
        + Scatter.scratch(depth, kinds)
        + [pltpu.SemaphoreType.DMA((16,))],
        1,
        5,
        6,
    )
    own = shape((share, width))
    g_qkv, g_ckv, g_cq, g_so, g_co, g_out, g_in, g_bias, g_gain, g_mid, g_lang = call(
        functools.partial(finish_kernel, langs),
        "finish",
        [
            shape((3, share, width)), shape((2, share, width)), own, own, own,
            shape((share, hidden)), shape((width, hidden // n)), shape((BIASES, share)),
            shape((GAINS, share)), shape((1, hidden // n)), shape((share, langs)),
        ],
        (o_qkv, o_ckv, o_cq, o_so, o_co, o_in, o_out, o_table),
    )
    return (
        first[None],
        out[None],
        g_x[None],
        g_mem[None],
        g_qkv.transpose(0, 2, 1),
        g_so.T,
        g_cq.T,
        g_ckv.transpose(0, 2, 1),
        g_co.T,
        g_in,
        g_out.T,
        g_bias,
        g_gain,
        g_mid[0],
        g_lang.T,
    )


def choose(n):
    return shards if n * 32 == 512 else shards_apart


def solution(mesh):
    n = mesh.shape["dp"]
    row3, row2, row1 = P(("rep", "dp"), None, None), P(("rep", "dp"), None), P(("rep", "dp"))
    wide, tall, flat = P(None, None, "dp"), P(None, "dp"), P("dp")
    parameters = (wide, tall, tall, wide, tall, tall, tall, tall, tall, flat, tall)
    return jax.shard_map(
        functools.partial(choose(n), n),
        mesh=mesh,
        in_specs=(row3, row3, row3, row3, row2, row1, row1, row2, row2, row1) + parameters,
        out_specs=(row3, row3, row3, row3) + parameters,
        check_vma=False,
    )
```

```python
import functools
import itertools
import math

import jax
import jax.numpy as jnp
from jax import lax
from jax.experimental import pallas as pl
from jax.experimental.pallas import tpu as pltpu
from jax.sharding import PartitionSpec as P

f32, bf16 = jnp.float32, jnp.bfloat16
MESH = pl.DeviceIdType.MESH
VMEM = pltpu.VMEM

HEADS = 8
HD = 64
EPSILON = 1e-05
MASKED = -1000000000.0
LOG2E = 1.4426950408889634
SCORE = LOG2E * HD ** (-0.5)
SCALING = HD ** (-0.5)

NT = (((1,), (1,)), ((), ()))
NN = (((1,), (0,)), ((), ()))
TN = (((0,), (0,)), ((), ()))

BIASES, GAINS = 10, 3


def dot(left, right, form):
    return lax.dot_general(left, right, form, preferred_element_type=f32)


def own_bits(index, depth):
    return [lax.rem(index // (1 << (depth - 1 - j)), 2) for j in range(depth)]


def partner_of(index, bit, depth, j):
    return index + (1 - 2 * bit) * (1 << (depth - 1 - j))


def enter(rep, me, partners, with_rep):
    barrier = pltpu.get_barrier_semaphore()
    for partner in partners:
        pl.semaphore_signal(barrier, inc=1, device_id=(rep, partner), device_id_type=MESH)
    if with_rep:
        pl.semaphore_signal(barrier, inc=1, device_id=(1 - rep, me), device_id_type=MESH)
    pl.semaphore_wait(barrier, len(partners) + int(with_rep))


def gather_kernel(depth, pieces, count, *refs):
    ins, outs = refs[:count], refs[count : 2 * count]
    send, recv, local = refs[2 * count :]
    rep, me = lax.axis_index("rep"), lax.axis_index("dp")
    bits = own_bits(me, depth)
    partners = [partner_of(me, bits[j], depth, j) for j in range(depth)]
    copies = [
        pltpu.make_async_copy(ins[i], outs[i].at[tuple(bits)], local.at[i]) for i in range(count)
    ]
    for copy in copies:
        copy.start()
    enter(rep, me, partners, False)
    for copy in copies:
        copy.wait()
    started = {}
    for tick in range(len(pieces) + depth - 1):
        for j in reversed(range(depth)):
            b = tick - j
            if not 0 <= b < len(pieces):
                continue
            if j > 0:
                started[b, j - 1].wait_recv()
            which, rows, cols = pieces[b]
            part = outs[which].at[(slice(None),) * j + tuple(bits[j:]) + (rows, cols)]
            copy = pltpu.make_async_remote_copy(
                part,
                part,
                send.at[b, j],
                recv.at[b, j],
                device_id=(rep, partners[j]),
                device_id_type=MESH,
            )
            copy.start()
            started[b, j] = copy
    for (b, j), copy in started.items():
        copy.wait_send()
        if j == depth - 1:
            copy.wait_recv()


def gather_all(n, shards, collective_id):
    depth = int(math.log2(n))
    pieces = []
    for i, shard in enumerate(shards):
        r, c = shard.shape
        if c > 512:
            pieces += [(i, slice(None), pl.ds(at, 512)) for at in range(0, c, 512)]
        elif r >= 128:
            pieces += [(i, pl.ds(at, 32), slice(None)) for at in range(0, r, 32)]
        else:
            pieces.append((i, slice(None), slice(None)))
    count = len(shards)
    outs = pl.pallas_call(
        functools.partial(gather_kernel, depth, pieces, count),
        out_shape=[jax.ShapeDtypeStruct((2,) * depth + s.shape, s.dtype) for s in shards],
        in_specs=[pl.BlockSpec(memory_space=pl.ANY)] * count,
        out_specs=[pl.BlockSpec(memory_space=pl.ANY)] * count,
        scratch_shapes=[
            pltpu.SemaphoreType.DMA((len(pieces), depth)),
            pltpu.SemaphoreType.DMA((len(pieces), depth)),
            pltpu.SemaphoreType.DMA((count,)),
        ],
        name="gather_weights",
        compiler_params=pltpu.CompilerParams(collective_id=collective_id, has_side_effects=True),
    )(*shards)
    return [out.reshape(n * s.shape[0], s.shape[1]) for out, s in zip(outs, shards)]


def scatter_kernel(depth, pieces, groups, count, *refs):
    ins, outs = refs[:count], refs[count : 2 * count]
    at = 2 * count
    stages = depth + 1
    gives = {}
    gets = {}
    for group in groups:
        gives[group] = refs[at : at + stages]
        gets[group] = refs[at + stages : at + 2 * stages]
        at += 2 * stages
    send, recv = refs[at:]
    rep, me = lax.axis_index("rep"), lax.axis_index("dp")
    bits = own_bits(me, depth)
    partners = [partner_of(me, bits[j], depth, j) for j in range(depth)]
    enter(rep, me, partners, True)
    started = {}
    for tick in range(len(pieces) + depth + 1):
        for s in reversed(range(depth + 2)):
            b = tick - s
            if not 0 <= b < len(pieces):
                continue
            which, rows, cols, group, slot = pieces[b]
            source = ins[which]
            j = depth - 1 - s
            if s > 0:
                started[b, s - 1].wait_recv()
            if s == depth + 1:
                mine = gives[group][depth][slot].astype(f32)
                outs[which][rows, cols] = mine + gets[group][depth][slot].astype(f32)
                continue
            if j >= 0:
                head = (slice(None),) * j
                tail = tuple(bits[j + 1 :]) + (rows, cols)
                give = head + (1 - bits[j],) + tail
                keep = head + (bits[j],) + tail
                if s == 0:
                    gives[group][0][slot] = source[give].astype(bf16)
                else:
                    got = gets[group][s - 1].at[slot]
                    gives[group][s][slot] = (
                        source[give] + got[head + (1 - bits[j],)].astype(f32)
                    ).astype(bf16)
                    source[keep] = source[keep] + got[head + (bits[j],)].astype(f32)
                target = (rep, partners[j])
            else:
                got = gets[group][s - 1][slot].astype(f32)
                gives[group][s][slot] = (source[tuple(bits) + (rows, cols)] + got).astype(bf16)
                target = (1 - rep, me)
            copy = pltpu.make_async_remote_copy(
                gives[group][s].at[slot],
                gets[group][s].at[slot],
                send.at[b, s],
                recv.at[b, s],
                device_id=target,
                device_id_type=MESH,
            )
            copy.start()
            started[b, s] = copy
    for copy in started.values():
        copy.wait_send()


def scatter_all(n, grads, collective_id):
    depth = int(math.log2(n))
    pieces, views, shapes, sizes = [], [], [], {}
    for i, grad in enumerate(grads):
        r, c = grad.shape[0] // n, grad.shape[1]
        views.append(grad.reshape((2,) * depth + (r, c)))
        shapes.append((r, c))
        high, wide = min(r, 32), min(c, 512)
        for a in range(0, r, high):
            for q in range(0, c, wide):
                slot = sizes.get((high, wide), 0)
                sizes[high, wide] = slot + 1
                pieces.append((i, pl.ds(a, high), pl.ds(q, wide), (high, wide), slot))
    count = len(grads)
    groups = sorted(sizes)
    scratch = []
    for group in groups:
        buffers = [
            VMEM((sizes[group],) + (2,) * max(depth - 1 - s, 0) + group, bf16)
            for s in range(depth + 1)
        ]
        scratch += buffers + buffers
    return pl.pallas_call(
        functools.partial(scatter_kernel, depth, pieces, groups, count),
        out_shape=[jax.ShapeDtypeStruct(s, f32) for s in shapes],
        in_specs=[pl.BlockSpec(memory_space=VMEM)] * count,
        out_specs=[pl.BlockSpec(memory_space=VMEM)] * count,
        scratch_shapes=scratch
        + [
            pltpu.SemaphoreType.DMA((len(pieces), depth + 1)),
            pltpu.SemaphoreType.DMA((len(pieces), depth + 1)),
        ],
        name="scatter_gradients",
        compiler_params=pltpu.CompilerParams(
            collective_id=collective_id, has_side_effects=True, vmem_limit_bytes=60 * 2**20
        ),
    )(*views)


class Gather:
    lag, steps = 2, 3

    def __init__(self, depth, buffers, pieces, send, recv):
        self.depth, self.buffers, self.pieces = depth, buffers, pieces
        self.send, self.recv = send, recv
        self.rep, self.me = lax.axis_index("rep"), lax.axis_index("dp")
        self.bits = own_bits(self.me, depth)
        self.planes = 1 << (depth - 2)
        self.far = [
            (self.rep, lax.rem(self.me + 4 * k, 4 * self.planes)) for k in range(1, self.planes)
        ]
        self.near = [
            (self.rep, partner_of(self.me, self.bits[j], depth, j)) for j in (depth - 2, depth - 1)
        ]
        self.time, self.arrived = 0, set()

    def enter(self):
        barrier = pltpu.get_barrier_semaphore()
        for target in self.far + self.near:
            pl.semaphore_signal(barrier, inc=1, device_id=target, device_id_type=MESH)
        pl.semaphore_wait(barrier, len(self.far) + len(self.near))

    def own(self, which):
        return self.buffers[which].at[tuple(self.bits)]

    def transfers(self, b, j):
        which, rows, cols = self.pieces[b]
        fixed = [0, self.depth - 2, self.depth - 1][j]
        part = self.buffers[which].at[(slice(None),) * fixed + tuple(self.bits[fixed:]) + (rows, cols)]
        targets = self.far if j == 0 else [self.near[j - 1]]
        first = [0, len(self.far), len(self.far) + 1][j]
        return [
            pltpu.make_async_remote_copy(
                part,
                part,
                self.send.at[b, first + i],
                self.recv.at[b, first + i],
                device_id=target,
                device_id_type=MESH,
            )
            for i, target in enumerate(targets)
        ]

    def tick(self):
        for j in reversed(range(self.steps)):
            b = self.time - self.lag * j
            if 0 <= b < len(self.pieces):
                if j > 0:
                    for copy in self.transfers(b, j - 1):
                        copy.wait_recv()
                for copy in self.transfers(b, j):
                    copy.start()
        self.time += 1

    def need(self, count):
        for b in range(count):
            if b in self.arrived:
                continue
            while self.time <= b + self.lag * (self.steps - 1):
                self.tick()
            for copy in self.transfers(b, self.steps - 1):
                copy.wait_recv()
            self.arrived.add(b)

    def finish(self):
        self.need(len(self.pieces))
        for b in range(len(self.pieces)):
            for j in range(self.steps):
                for copy in self.transfers(b, j):
                    copy.wait_send()


class Agenda:
    def __init__(self):
        self.flows = []

    def round(self, *fresh):
        for steps in self.flows:
            if steps:
                steps.pop(0)()
        for steps in fresh:
            steps.pop(0)()
            self.flows.append(steps)

    def busy(self):
        return any(self.flows)


class Scatter:
    def __init__(self, depth, units, refs, send, recv):
        self.planes, self.units = 1 << (depth - 2), units
        self.rep, self.me = lax.axis_index("rep"), lax.axis_index("dp")
        self.core = lax.rem(self.me, 2)
        self.x = lax.rem(self.me // 2, 2)
        self.plane = self.me // 4
        self.send, self.recv = send, recv
        at, mark = 0, 0
        for unit in units:
            unit["parts"] = []
            planes = list(range(self.planes))
            turns = [[lax.rem(self.plane + 1 + p, self.planes)] for p in planes]
            for part in turns if unit["apart"] else [planes]:
                steps = []
                for _ in range(3):
                    steps.append((refs[at], refs[at + 1], mark))
                    at, mark = at + 2, mark + 1
                unit["parts"].append((part, steps))
            unit["across"], unit["last"] = (refs[at], refs[at + 1], mark), (refs[at + 2], refs[at + 3], mark + self.planes - 1)
            at, mark = at + 4, mark + self.planes

    @staticmethod
    def scratch(depth, kinds):
        planes, buffers, marks = 1 << (depth - 2), [], 0
        for wide, kind, apart in kinds:
            half = wide // 2
            for count in [1] * planes if apart else [planes]:
                middle = (count, 32, wide) if kind == 0 else (2 * count, 32, half)
                for dims in [(2 * count, 32, wide), middle, (count, 32, half)]:
                    buffers += [VMEM(dims, bf16)] * 2
                    marks += 1
            buffers += [VMEM((planes, 32, half), bf16), VMEM((planes - 1, 32, half), bf16)]
            buffers += [VMEM((32, half), bf16)] * 2
            marks += planes
        return buffers + [pltpu.SemaphoreType.DMA((marks,))] * 2

    def enter(self, steps=()):
        barrier = pltpu.get_barrier_semaphore()
        targets = [self.near("rep")]
        if steps:
            devices = 4 * self.planes
            targets += [(self.rep, lax.rem(self.me + k, devices)) for k in steps]
        else:
            targets += [self.near("core"), self.near("x")]
            targets += [self.far(k)[1] for k in range(1, self.planes)]
        for target in targets:
            pl.semaphore_signal(barrier, inc=1, device_id=target, device_id_type=MESH)
        pl.semaphore_wait(barrier, len(targets))

    def near(self, dim):
        if dim == "rep":
            return (1 - self.rep, self.me)
        if dim == "x":
            return (self.rep, self.me + 2 * (1 - 2 * self.x))
        return (self.rep, self.me + 1 - 2 * self.core)

    def far(self, k):
        plane = lax.rem(self.plane + k, self.planes)
        return plane, (self.rep, plane * 4 + lax.rem(self.me, 4))

    def transfer(self, give, get, mark, target):
        return pltpu.make_async_remote_copy(
            give,
            get,
            self.send.at[mark],
            self.recv.at[mark],
            device_id=target,
            device_id_type=MESH,
        )

    def part(self, which, index):
        unit = self.units[which]
        planes, buffers = unit["parts"][index]
        source, r, a, c0, wide = (unit[name] for name in ("source", "r", "a", "c0", "wide"))
        half, count = wide // 2, len(planes)
        dims = ["core", "x", "rep"] if unit["kind"] == 0 else ["core", "rep", "x"]
        whole = pl.ds(c0, wide)
        mine = pl.ds(pl.multiple_of(c0 + half * self.rep, 128), half)
        other = pl.ds(pl.multiple_of(c0 + half * (1 - self.rep), 128), half)
        mine_got = pl.ds(pl.multiple_of(half * self.rep, 128), half)
        other_got = pl.ds(pl.multiple_of(half * (1 - self.rep), 128), half)

        def rows(plane, x, core):
            return pl.ds(pl.multiple_of((plane * 4 + x * 2 + core) * r + a, 32), 32)

        def moved(step):
            give, get, mark = buffers[step]
            return self.transfer(give, get, mark, self.near(dims[step]))

        def first():
            give = buffers[0][0]
            for x in range(2):
                for i, plane in enumerate(planes):
                    give[x * count + i] = source[rows(plane, x, 1 - self.core), whole].astype(bf16)
            moved(0).start()

        def over_x(step, columns):
            moved(step - 1).wait_recv()
            give, got = buffers[step][0], buffers[step - 1][1]
            for i, plane in enumerate(planes):
                away = rows(plane, 1 - self.x, self.core)
                here = rows(plane, self.x, self.core)
                give[i] = (
                    source[away, columns] + got[(1 - self.x) * count + i].astype(f32)
                ).astype(bf16)
                source[here, columns] = source[here, columns] + got[self.x * count + i].astype(f32)
            moved(step).start()

        def over_rep(step):
            moved(step - 1).wait_recv()
            give, got = buffers[step][0], buffers[step - 1][1]
            for x in range(2) if step == 1 else [self.x]:
                for i, plane in enumerate(planes):
                    at = x * count + i if step == 1 else i
                    here = rows(plane, x, self.core)
                    give[at] = (source[here, other] + got[at, :, other_got].astype(f32)).astype(bf16)
                    source[here, mine] = source[here, mine] + got[at, :, mine_got].astype(f32)
            moved(step).start()

        def summed():
            moved(2).wait_recv()
            got, across = buffers[2][1], unit["across"][0]
            for i, plane in enumerate(planes):
                here = rows(plane, self.x, self.core)
                total = source[here, mine] + got[i].astype(f32)
                source[here, mine] = total
                across[plane] = total.astype(bf16)
            if unit["apart"] and index + 1 < self.planes:
                self.sent(which, index + 1).start()

        if unit["kind"] == 0:
            return [first, lambda: over_x(1, whole), lambda: over_rep(2), summed]
        return [first, lambda: over_rep(1), lambda: over_x(2, mine), summed]

    def ending(self, which):
        unit = self.units[which]
        source, r, a, c0, wide = (unit[name] for name in ("source", "r", "a", "c0", "wide"))
        out, out_col = unit["out"], unit["out_col"]
        half = wide // 2
        get = unit["across"][1]
        last = self.transfer(*unit["last"], self.near("rep"))
        mine = pl.ds(pl.multiple_of(c0 + half * self.rep, 128), half)

        def across():
            for k in range(1, self.planes):
                self.sent(which, k).start()

        def total():
            value = source[pl.ds(pl.multiple_of(self.me * r + a, 32), 32), mine]
            for k in range(1, self.planes):
                self.sent(which, k).wait_recv()
                value = value + get[k - 1].astype(f32)
            value = value.astype(bf16)
            unit["last"][0][...] = value
            own = pl.ds(pl.multiple_of(out_col + half * self.rep, 128), half)
            out[pl.ds(a, 32), own] = value.astype(f32)
            last.start()

        def rest():
            last.wait_recv()
            other = pl.ds(pl.multiple_of(out_col + half * (1 - self.rep), 128), half)
            out[pl.ds(a, 32), other] = unit["last"][1][...].astype(f32)

        return [total, rest] if unit["apart"] else [across, total, rest]

    def flow(self, which):
        steps, (across, *rest) = self.part(which, 0), self.ending(which)

        def summed():
            steps[-1]()
            across()

        return steps[:-1] + [summed] + rest

    def sent(self, which, k):
        give, get, mark = self.units[which]["across"]
        plane, target = self.far(k)
        return self.transfer(give.at[plane], get.at[k - 1], mark + k - 1, target)

    def leave(self):
        for which, unit in enumerate(self.units):
            dims = ["core", "x", "rep"] if unit["kind"] == 0 else ["core", "rep", "x"]
            for _, buffers in unit["parts"]:
                for step, (give, get, mark) in enumerate(buffers):
                    self.transfer(give, get, mark, self.near(dims[step])).wait_send()
            for k in range(1, self.planes):
                self.sent(which, k).wait_send()
            self.transfer(*unit["last"], self.near("rep")).wait_send()


def units_of(source, r, out, wide, kinds, apart=False):
    units = []
    for a in range(0, r, 32):
        for c0 in range(0, wide, 512):
            units.append(
                dict(
                    source=source, r=r, a=a, c0=c0, wide=min(512, wide - c0), out=out, out_col=c0,
                    kind=next(kinds) % 2, apart=apart,
                )
            )
    return units


def both_heads(pair, low):
    zero = jnp.zeros_like(pair)
    return jnp.concatenate([jnp.where(low, pair, zero), jnp.where(low, zero, pair)], axis=0)


def twice(bias):
    return bias if bias.shape[0] == 1 else jnp.concatenate([bias, bias], axis=0)


def attend_block(q, k, v, ctx, lse, rows, key_rows, keys, bias, size, after=None):
    low = lax.broadcasted_iota(jnp.int32, (size, 128), 1) < HD
    lanes = lax.broadcasted_iota(jnp.int32, (size, 128), 1)
    bias = twice(bias)
    log_sums = jnp.zeros((size, 128), f32)

    def scores(pair):
        cols = pl.ds(128 * pair, 128)
        return dot(both_heads(q[rows, cols], low), k[keys, cols], NT) * SCORE + bias

    following = scores(0)
    for pair in range(HEADS // 2):
        cols = pl.ds(128 * pair, 128)
        s = following
        if pair + 1 < HEADS // 2:
            following = scores(pair + 1)
        largest = jnp.max(s, axis=1, keepdims=True)
        powers = jnp.exp2(s - largest)
        total = jnp.sum(powers, axis=1, keepdims=True)
        c = dot(powers.astype(bf16), v[keys, cols], NN) * (1.0 / total)
        ctx[rows, cols] = jnp.where(low, c[:size], c[size:]).astype(bf16)
        if lse is not None:
            log_sum = largest + jnp.log2(total)
            log_sums = jnp.where(lanes == 2 * pair, log_sum[:size], log_sums)
            log_sums = jnp.where(lanes == 2 * pair + 1, log_sum[size:], log_sums)
        if after is not None:
            after()
    if lse is not None:
        lse[key_rows, :] = log_sums


def column_pair(table, rows, pair):
    return jnp.concatenate(
        [table[rows, 2 * pair : 2 * pair + 1], table[rows, 2 * pair + 1 : 2 * pair + 2]], axis=0
    )


def head_columns(table, pair):
    lanes = lax.broadcasted_iota(jnp.int32, table.shape, 1)
    parts = [jnp.where(lanes == 2 * pair + head, table, 0.0) for head in range(2)]
    return jnp.concatenate([jnp.sum(part, axis=1, keepdims=True) for part in parts], axis=0)


def head_products(left, right):
    value = left.astype(f32) * right.astype(f32)
    low = lax.broadcasted_iota(jnp.int32, value.shape, 1) < HD
    parts = [jnp.where(low, value, 0.0), jnp.where(low, 0.0, value)]
    return jnp.concatenate([jnp.sum(part, axis=1, keepdims=True) for part in parts], axis=0)


def attend_back_pair(q, k, v, g, lse, delta, gq, gk_t, gv_t, rows, keys, bias, size, cols):
    low = lax.broadcasted_iota(jnp.int32, (size, 128), 1) < HD
    q_two = both_heads(q[rows, cols], low)
    g_two = both_heads(g[rows, cols], low)
    k_pair, v_pair = k[keys, cols], v[keys, cols]
    probs = jnp.exp2(dot(q_two, k_pair, NT) * SCORE + twice(bias) - lse)
    grad_s = (probs * (dot(g_two, v_pair, NT) - delta)).astype(bf16)
    gv_t[cols, keys] += dot(g_two, probs.astype(bf16), TN)
    gk_t[cols, keys] += dot(q_two, grad_s, TN)
    d = dot(grad_s, k_pair, NN)
    gq[rows, cols] = (jnp.where(low, d[:size], d[size:]) * SCALING).astype(bf16)


def attend_back_block(
    q, k, v, g, lse, delta, gq, gk_t, gv_t, rows, keys, bias, size, after=None
):
    for pair in range(HEADS // 2):
        attend_back_pair(
            q, k, v, g, column_pair(lse, rows, pair), column_pair(delta, rows, pair),
            gq, gk_t, gv_t, rows, keys, bias, size, pl.ds(128 * pair, 128),
        )
        if after is not None:
            after()


def head_sums(value):
    rows = value.shape[0]
    lanes = lax.broadcasted_iota(jnp.int32, (rows, 128), 1)
    low = lanes < HD
    result = jnp.zeros((rows, 128), f32)
    for pair in range(HEADS // 2):
        part = value[:, 128 * pair : 128 * pair + 128]
        first = jnp.sum(jnp.where(low, part, 0.0), axis=1, keepdims=True)
        second = jnp.sum(jnp.where(low, 0.0, part), axis=1, keepdims=True)
        result = jnp.where(lanes == 2 * pair, first, result)
        result = jnp.where(lanes == 2 * pair + 1, second, result)
    return result


def blocks(total, size, body):
    def step(i, carry):
        body(pl.ds(pl.multiple_of(i * size, size), size))
        return carry

    lax.fori_loop(0, total // size, step, 0)


def normalise(value):
    average = jnp.mean(value, axis=1, keepdims=True)
    centred = value - average
    scale = lax.rsqrt(jnp.mean(centred * centred, axis=1, keepdims=True) + EPSILON)
    return centred * scale, scale


def normalise_back(grad, gain, hat, scale):
    g = grad * gain
    first = jnp.mean(g, axis=1, keepdims=True)
    second = jnp.mean(g * hat, axis=1, keepdims=True)
    return scale * (g - first - hat * second)


def column_sum(value):
    return jnp.sum(value, axis=0, keepdims=True)


def mat(ref):
    value = ref[...]
    return value if value.ndim == 2 else value.reshape(-1, value.shape[-1])


def up_part(win, j):
    if len(win.shape) == 2:
        return win[512 * j : 512 * j + 512, :]
    depth = len(win.shape) - 2
    lead = depth - int(math.log2(512 // win.shape[-2]))
    part = win[tuple((j >> (lead - 1 - i)) & 1 for i in range(lead))]
    return part.reshape(512, part.shape[-1])


def down_part(wout, j):
    if len(wout.shape) == 2:
        return wout[:, 512 * j : 512 * j + 512]
    part = wout[(slice(None),) * (len(wout.shape) - 1) + (slice(512 * j, 512 * j + 512),)]
    return part.reshape(-1, 512)


def prepare_kernel(
    x, t, mem, seg_c, seg_r, key_c, key_r, want_c, lang, wq, wk, wv, wck, wcv, small,
    h, q, k, v, ck, cv,
):
    length = x.shape[0]

    def glanced(rows):
        same = seg_c[rows, :] == seg_r[...]
        doc_length = jnp.sum(same.astype(f32), axis=1, keepdims=True)
        ahead = jnp.logical_and(same, key_r[...] > key_c[rows, :])
        rank = jnp.sum(ahead.astype(f32), axis=1, keepdims=True)
        wanted = jnp.minimum(want_c[rows, :], doc_length.astype(jnp.int32))
        count = lax.shift_right_logical(wanted + 1, jnp.int32(1))
        glance = rank < count.astype(f32)
        plain = x[rows, :].astype(f32)
        h[0, rows, :] = plain + lang[...]
        h[1, rows, :] = jnp.where(glance, t[rows, :].astype(f32), plain) + lang[...]

    blocks(length, 128, glanced)

    def cross(rows):
        m = mem[rows, :]
        ck[rows, :] = dot(m, wck[...], NT).astype(bf16)
        cv[rows, :] = (dot(m, wcv[...], NT) + small[4:5, :]).astype(bf16)

    blocks(mem.shape[0], 512, cross)
    for which in range(2):

        def project(rows):
            low = h[which, rows, :].astype(bf16)
            q[which, rows, :] = (dot(low, wq[...], NT) + small[0:1, :]).astype(bf16)
            k[which, rows, :] = dot(low, wk[...], NT).astype(bf16)
            v[which, rows, :] = (dot(low, wv[...], NT) + small[1:2, :]).astype(bf16)

        blocks(length, 512, project)


def windows(length):
    return [w for w in (256, 384, 512, 640) if w < length] + [length]


def windowed(starts, needs, i, length, body):
    need, begin = needs[i], starts[i]
    sizes = windows(length)
    for at, size in enumerate(sizes):
        fits = need <= size
        if at > 0:
            fits = jnp.logical_and(fits, need > sizes[at - 1])

        @pl.when(fits)
        def _():
            start = pl.multiple_of(jnp.minimum(begin, length - size), 128)
            body(pl.ds(start, size))


def self_kernel(starts, needs, q, k, v, seg_c, seg_r, ctx, lse):
    length = q.shape[1]
    size = 128

    def step(i, carry):
        rows = pl.ds(pl.multiple_of(i * size, size), size)

        def body(keys):
            bias = jnp.where(seg_c[rows, :] == seg_r[:, keys], 0.0, MASKED)
            for which in range(2):
                attend_block(
                    q.at[which], k.at[which], v.at[which], ctx.at[which],
                    lse if which == 1 else None, rows, rows, keys, bias, size,
                )

        windowed(starts, needs, i, length, body)
        return carry

    lax.fori_loop(0, length // size, step, 0)


def after_self(ctx, h, wso, wcq, small, a, cq, rows):
    r1 = h + dot(ctx, mat(wso), NT) + small[2:3, :]
    hat, scale = normalise(r1)
    value = hat * small[10:11, :] + small[7:8, :]
    if a is not None:
        a[rows, :] = value
    low = value.astype(bf16)
    cq[rows, :] = (dot(low, mat(wcq), NT) + small[3:4, :]).astype(bf16)
    return hat, scale, low


def after_cross(a, ctx2, wco, win, wout, small, hidden_bias, hid, slope):
    r2 = a + dot(ctx2, mat(wco), NT) + small[5:6, :]
    hat2, scale2 = normalise(r2)
    b = hat2 * small[11:12, :] + small[8:9, :]
    low = b.astype(bf16)
    total = b + small[6:7, :]
    for j in range(hidden_bias.shape[1] // 512):
        cols = pl.ds(512 * j, 512)
        z = dot(low, up_part(win, j), NT) + hidden_bias[:, cols]
        half = 0.5 + 0.5 * lax.erf(z * 0.7071067811865476)
        hidden = (z * half).astype(bf16)
        if hid is not None:
            hid[:, cols] = hidden
            bell = jnp.exp2(z * z * (-0.5 * LOG2E)) * 0.3989422804014327
            slope[:, cols] = half + z * bell
        total = total + dot(hidden, down_part(wout, j), NT)
    hat3, scale3 = normalise(total)
    y = hat3 * small[12:13, :] + small[9:10, :]
    return y, (hat2, scale2, low, hat3, scale3)


def first_kernel(
    h, ctx, ck, cv, source_bias, wso, wcq, wco, win, wout, small, hidden_bias,
    out, a, cq, ctx2,
):
    length = h.shape[1]

    def before(rows):
        after_self(ctx[0, rows, :], h[0, rows, :], wso, wcq, small, a, cq, rows)

    blocks(length, 512, before)
    every = pl.ds(0, ck.shape[0])
    blocks(
        length,
        256,
        lambda rows: attend_block(cq, ck, cv, ctx2, None, rows, rows, every, source_bias[...], 256),
    )

    def last(rows):
        y, _ = after_cross(
            a[rows, :], ctx2[rows, :], wco, win, wout, small, hidden_bias, None, None
        )
        out[rows, :] = y.astype(bf16)

    blocks(length, 512, last)


def layer_kernel(
    h, ctx, ck, cv, mem, cot, live, source_bias,
    wso, wcq, wck, wcv, wco, win, wout, small, hidden_bias,
    out, gr1, gctx, g_mem,
    g_so, g_cq, g_ck, g_cv, g_co, g_in, g_out, g_small, g_hidden,
    cq, ctx2, lse2, hat1, scale1, low1, hid, slope, delta, gcq, gk_low, gv_low, low2, hat2s,
):
    length = h.shape[1]
    big = 512
    a, gctx2 = gr1, gctx
    for ref in (g_so, g_cq, g_co, g_in, g_out, g_small, g_hidden):
        ref[...] = jnp.zeros_like(ref)

    def before(rows):
        hat, scale, low = after_self(ctx[0, rows, :], h[0, rows, :], wso, wcq, small, a, cq, rows)
        hat1[rows, :] = hat
        scale1[rows, :] = scale
        low1[rows, :] = low

    blocks(length, big, before)
    every = pl.ds(0, ck.shape[0])
    blocks(
        length,
        256,
        lambda rows: attend_block(cq, ck, cv, ctx2, lse2, rows, rows, every, source_bias[...], 256),
    )

    def turn(rows):
        y, (hat2, scale2, low, hat3, scale3) = after_cross(
            a[rows, :], ctx2[rows, :], wco, win, wout, small, hidden_bias, hid, slope
        )
        out[rows, :] = y.astype(bf16)
        low2[...] = low
        hat2s[...] = hat2
        gy = cot[rows, :].astype(f32) * live[rows, :]
        g_small[12:13, :] += column_sum(gy * hat3)
        g_small[9:10, :] += column_sum(gy)
        gr3 = normalise_back(gy, small[12:13, :], hat3, scale3)
        gf = gr3.astype(bf16)
        g_small[6:7, :] += column_sum(gf.astype(f32))
        gb = gr3
        for j in range(win.shape[0] // 512):
            cols = pl.ds(512 * j, 512)
            gz = (dot(gf, wout[:, cols], NN) * slope[:, cols]).astype(bf16)
            g_out[:, cols] += dot(gf, hid[:, cols], TN)
            g_in[cols, :] += dot(gz, low2[...], TN)
            g_hidden[:, cols] += column_sum(gz.astype(f32))
            gb = gb + dot(gz, win[cols, :], NN)
        hat2 = hat2s[...]
        g_small[11:12, :] += column_sum(gb * hat2)
        g_small[8:9, :] += column_sum(gb)
        gr2 = normalise_back(gb, small[11:12, :], hat2, scale2)
        a[rows, :] = gr2
        go2 = gr2.astype(bf16)
        g_small[5:6, :] += column_sum(go2.astype(f32))
        context = ctx2[rows, :]
        g_co[...] += dot(go2, context, TN)
        back = dot(go2, wco[...], NN).astype(bf16)
        gctx2[rows, :] = back
        delta[rows, :] = head_sums(back.astype(f32) * context.astype(f32))

    blocks(length, big, turn)
    gk_t, gv_t = slope.at[:, pl.ds(0, ck.shape[0])], slope.at[:, pl.ds(ck.shape[0], ck.shape[0])]
    slope[...] = jnp.zeros_like(slope)
    blocks(
        length,
        256,
        lambda rows: attend_back_block(
            cq, ck, cv, gctx2, lse2, delta, gcq, gk_t, gv_t, rows, every, source_bias[...], 256
        ),
    )
    gk_low[...] = (gk_t[...] * SCALING).astype(bf16)
    gv_low[...] = gv_t[...].astype(bf16)
    g_ck[...] = dot(gk_low[...], mem[...], NN)
    g_cv[...] = dot(gv_low[...], mem[...], NN)
    ones = jnp.ones((8, mem.shape[0]), bf16)
    g_small[4:5, :] = dot(ones, gv_low[...], NT)[0:1, :]
    for at in range(0, mem.shape[0], 512):
        cols = pl.ds(at, 512)
        g_mem[cols, :] = dot(gk_low[:, cols], wck[...], TN) + dot(gv_low[:, cols], wcv[...], TN)

    def final(rows):
        gq = gcq[rows, :]
        g_small[3:4, :] += column_sum(gq.astype(f32))
        g_cq[...] += dot(gq, low1[rows, :], TN)
        ga = a[rows, :] + dot(gq, wcq[...], NN)
        hat = hat1[rows, :]
        g_small[10:11, :] += column_sum(ga * hat)
        g_small[7:8, :] += column_sum(ga)
        g1 = normalise_back(ga, small[10:11, :], hat, scale1[rows, :])
        gr1[rows, :] = g1
        go = g1.astype(bf16)
        g_small[2:3, :] += column_sum(go.astype(f32))
        g_so[...] += dot(go, ctx[0, rows, :], TN)
        gctx[rows, :] = dot(go, wso[...], NN).astype(bf16)

    blocks(length, big, final)


def self_back_kernel(
    starts, needs, live_blocks, q, k, v, g, ctx, lse, seg_c, seg_r,
    gq, gk_low, gv_low, delta, gk_t, gv_t,
):
    length = q.shape[1]
    size = 128
    gk_t[...] = jnp.zeros_like(gk_t)
    gv_t[...] = jnp.zeros_like(gv_t)
    gq[...] = jnp.zeros_like(gq)

    def step(i, carry):
        rows = pl.ds(pl.multiple_of(i * size, size), size)
        delta[rows, :] = head_sums(g[rows, :].astype(f32) * ctx[0, rows, :].astype(f32))

        def body(keys):
            bias = jnp.where(seg_c[rows, :] == seg_r[:, keys], 0.0, MASKED)
            attend_back_block(
                q.at[0], k.at[0], v.at[0], g, lse, delta, gq, gk_t, gv_t, rows, keys, bias, size
            )

        windowed(starts, needs, i, length, body)
        return carry

    lax.fori_loop(0, live_blocks[0], step, 0)
    gk_low[...] = (gk_t[...] * SCALING).astype(bf16)
    gv_low[...] = gv_t[...].astype(bf16)


def input_kernel(h, gq, gk_low, gv_low, gr1, wq, wk, wv, g_x, g_q, g_k, g_v, sums):
    length = h.shape[1]
    g_q[...] = jnp.zeros_like(g_q)
    g_k[...] = jnp.zeros_like(g_k)
    g_v[...] = jnp.zeros_like(g_v)
    sums[...] = jnp.zeros_like(sums)
    ones = jnp.ones((8, 512), bf16)

    for at in range(0, length, 512):
        rows = pl.ds(at, 512)
        low = h[0, rows, :].astype(bf16)
        part = gq[rows, :]
        g_q[...] += dot(part, low, TN)
        g_k[...] += dot(gk_low[:, rows], low, NN)
        g_v[...] += dot(gv_low[:, rows], low, NN)
        value = gr1[rows, :] + dot(part, wq[...], NN)
        value = value + dot(gk_low[:, rows], wk[...], TN) + dot(gv_low[:, rows], wv[...], TN)
        g_x[rows, :] = value
        sums[0:1, :] += column_sum(part.astype(f32))
        sums[1:2, :] += dot(ones, gv_low[:, rows], NT)[0:1, :]
        sums[2:3, :] += column_sum(value)


def shape(dims, dtype=f32):
    return jax.ShapeDtypeStruct(dims, dtype)


def call(kernel, name, outs, args, scratch=(), scalars=0, specs=None):
    in_specs = [pl.BlockSpec(memory_space=pltpu.SMEM)] * scalars
    for at in range(scalars, len(args)):
        in_specs.append((specs or {}).get(at) or pl.BlockSpec(memory_space=VMEM))
    return pl.pallas_call(
        kernel,
        out_shape=outs,
        in_specs=in_specs,
        out_specs=[pl.BlockSpec(memory_space=VMEM)] * len(outs),
        scratch_shapes=list(scratch),
        name=name,
        compiler_params=pltpu.CompilerParams(vmem_limit_bytes=61 * 2**20),
    )(*args)


def shards_apart(
    n,
    x_copy,
    target_embed,
    memory,
    cotangent,
    segment_ids,
    source_lengths,
    target_lengths,
    hamming,
    priority,
    lang_tag,
    w_self_qkv,
    w_self_out,
    w_cross_q,
    w_cross_kv,
    w_cross_out,
    w_in,
    w_out,
    biases,
    gains,
    b_hidden,
    lang_table,
):
    length, width = x_copy.shape[1:]
    source = memory.shape[1]
    hidden = b_hidden.shape[0] * n
    share = width // n
    fold = hidden // width
    langs = lang_table.shape[0]
    slots = hamming.shape[1]

    table = jnp.concatenate([biases, gains, lang_table, b_hidden.reshape(fold, share)], axis=0)
    kept = table.shape[0]
    table = jnp.pad(table, ((0, 128 - kept), (0, 0)))
    gathered = gather_all(
        n,
        [
            table.T,
            w_cross_kv[0].T,
            w_cross_kv[1].T,
            w_self_qkv[0].T,
            w_self_qkv[1].T,
            w_self_qkv[2].T,
            w_self_out.T,
            w_cross_q.T,
            w_cross_out.T,
            w_in.T,
            w_out.T,
        ],
        0,
    )
    small_t, wck, wcv, wq, wk, wv, wso, wcq, wco, win, wout = gathered
    small = small_t.T.astype(f32)
    first_lang = BIASES + GAINS
    hidden_bias = small[first_lang + langs : first_lang + langs + fold]
    hidden_bias = hidden_bias.reshape(fold, n, share).transpose(1, 0, 2).reshape(1, hidden)
    lang = lax.dynamic_slice_in_dim(small, first_lang + lang_tag[0], 1, 0)
    small = small[:16]

    target_len = target_lengths[0]
    position = jnp.arange(length, dtype=jnp.int32)
    live = position < target_len
    seg = jnp.where(live, segment_ids[0], slots).astype(jnp.int32)
    wanted = jnp.sum(
        jnp.where(seg[:, None] == jnp.arange(slots, dtype=jnp.int32)[None, :], hamming[0][None, :], 0),
        axis=1,
        keepdims=True,
    )
    key = priority[0] * length + (length - 1 - position)
    same_edge = seg.reshape(length // 128, 128)
    first_seg, last_seg = same_edge[:, 0], same_edge[:, -1]
    begin = jnp.sum((seg[None, :] < first_seg[:, None]).astype(jnp.int32), axis=1)
    end = jnp.sum((seg[None, :] <= last_seg[:, None]).astype(jnp.int32), axis=1)
    starts = begin // 128 * 128
    needs = (end + 127) // 128 * 128 - starts
    live_blocks = ((target_len + 127) // 128).reshape(1)
    seg_c, seg_r = seg[:, None], seg[None, :]
    source_bias = jnp.where(
        jnp.arange(source, dtype=jnp.int32) < source_lengths[0], 0.0, MASKED
    ).astype(f32)[None, :]

    mem = memory[0]
    two = (2, length, width)
    h, q, k, v, ck, cv = call(
        prepare_kernel,
        "prepare",
        [shape(two), shape(two, bf16), shape(two, bf16), shape(two, bf16)]
        + [shape((source, width), bf16)] * 2,
        (
            x_copy[0], target_embed[0], mem, seg_c, seg_r, key[:, None], key[None, :], wanted,
            lang, wq, wk, wv, wck, wcv, small,
        ),
    )
    ctx, lse = call(
        self_kernel,
        "self_attention",
        [shape(two, bf16), shape((length, 128))],
        (starts, needs, q, k, v, seg_c, seg_r),
        scalars=2,
    )

    def part(dims, which):
        block = (1,) + dims[1:]
        return pl.BlockSpec(block, lambda i: (which, 0, 0))

    def one(value, which):
        return lax.slice_in_dim(value, which, which + 1, axis=0)

    flat = (length, width)
    (first,) = call(
        first_kernel,
        "first_pass",
        [shape(flat, bf16)],
        (one(h, 0), one(ctx, 0), ck, cv, source_bias, wso, wcq, wco, win, wout, small, hidden_bias),
        scratch=[VMEM(flat, f32), VMEM(flat, bf16), VMEM(flat, bf16)],
    )
    square = shape((width, width))
    h2, ctx_two = one(h, 1), one(ctx, 1)
    big = 512
    (
        final, gr1, gctx, g_mem, g_so, g_cq, g_ck, g_cv, g_co, g_in, g_out, g_small, g_hidden,
    ) = call(
        layer_kernel,
        "second_pass",
        [shape(flat, bf16), shape(flat), shape(flat, bf16), shape((source, width))]
        + [square] * 5
        + [shape((hidden, width)), shape((width, hidden)), shape((16, width)), shape((1, hidden))],
        (
            h2, ctx_two, ck, cv, mem, cotangent[0], live[:, None].astype(f32), source_bias,
            wso, wcq, wck, wcv, wco, win, wout, small, hidden_bias,
        ),
        scratch=[
            VMEM(flat, bf16), VMEM(flat, bf16), VMEM((length, 128), f32),
            VMEM(flat, f32), VMEM((length, 1), f32), VMEM(flat, bf16),
            VMEM((big, hidden), bf16), VMEM((width, max(hidden, 2 * source)), f32),
            VMEM((length, 128), f32), VMEM(flat, bf16),
            VMEM((width, source), bf16), VMEM((width, source), bf16),
            VMEM((big, width), bf16), VMEM((big, width), f32),
        ],
    )
    gq, gk_low, gv_low = call(
        self_back_kernel,
        "self_attention_back",
        [shape(flat, bf16), shape((width, length), bf16), shape((width, length), bf16)],
        (starts, needs, live_blocks, one(q, 1), one(k, 1), one(v, 1), gctx, ctx_two, lse, seg_c, seg_r),
        scratch=[VMEM((length, 128), f32), VMEM((width, length), f32), VMEM((width, length), f32)],
        scalars=3,
    )
    g_x, g_q, g_k, g_v, sums = call(
        input_kernel,
        "input_gradient",
        [shape(flat), square, square, square, shape((8, width))],
        (h2, gq, gk_low, gv_low, gr1, wq, wk, wv),
    )

    tag = jnp.arange(langs, dtype=jnp.int32) == lang_tag[0]
    g_lang = jnp.where(tag[:, None], sums[2:3], 0.0)
    g_fold = g_hidden.reshape(n, fold, share).transpose(1, 0, 2).reshape(fold, width)
    g_table = jnp.concatenate([sums[0:2], g_small[2:13], g_lang, g_fold], axis=0)
    g_table = jnp.pad(g_table, ((0, 128 - kept), (0, 0))).T
    owned = scatter_all(n, [g_in, g_out, g_co, g_ck, g_cv, g_cq, g_so, g_q, g_k, g_v, g_table], 1)
    o_in, o_out, o_co, o_ck, o_cv, o_cq, o_so, o_q, o_k, o_v, o_table = owned
    o_table = o_table.T
    return (
        first[None],
        final[None],
        g_x[None],
        g_mem[None],
        jnp.stack([o_q.T, o_k.T, o_v.T]),
        o_so.T,
        o_cq.T,
        jnp.stack([o_ck.T, o_cv.T]),
        o_co.T,
        o_in.T,
        o_out.T,
        o_table[:BIASES],
        o_table[BIASES:first_lang],
        o_table[first_lang + langs : kept].reshape(hidden // n),
        o_table[first_lang : first_lang + langs],
    )


def add_to(ref, index, value, fresh):
    ref[index] = value if fresh else ref[index] + value


class Copies:
    def __init__(self, semaphores):
        self.semaphores, self.pending, self.count = semaphores, {}, 0

    def start(self, source, target):
        copy = pltpu.make_async_copy(source, target, self.semaphores.at[self.count])
        copy.start()
        self.pending[self.count] = copy
        self.count += 1
        return self.count - 1

    def wait(self, *which):
        for at in which:
            if at in self.pending:
                self.pending.pop(at).wait()

    def wait_all(self):
        self.wait(*list(self.pending))


def column(row, rows):
    size = 128
    down = lax.broadcasted_iota(jnp.int32, (size, size), 0)
    across = lax.broadcasted_iota(jnp.int32, (size, size), 1)
    return jnp.sum(jnp.where(down == across, row[:, rows], 0.0), axis=1, keepdims=True)


def placed(height, offset):
    down = lax.broadcasted_iota(jnp.int32, (height, 128), 0)
    across = lax.broadcasted_iota(jnp.int32, (height, 128), 1)
    return (across == down + offset).astype(bf16)


def apart(body):
    once = jnp.minimum(lax.axis_index("dp") + 1, 1)

    def step(i, carry):
        body()
        return carry

    lax.fori_loop(0, once, step, 0)


def source_row(source_len, count):
    position = lax.broadcasted_iota(jnp.int32, (1, count), 1)
    return jnp.where(position < source_len[0], 0.0, MASKED)


def forward_kernel(
    depth, most, fewest, target_len, tag, hamming, source_len,
    raw, priority, biases, gains, lang_t, w_in, b_mid,
    x_ref, t_ref, mem_ref, qkv_t, ckv_t, so_t, cq_t, co_t, out_t,
    small, seg_c, seg_r, hidden_bias, scale1,
    a1_ref, ctxb1_ref, hat1_ref, low2_ref, q2_ref, k2_ref, v2_ref, lse_ref, ctx2_ref, ck_ref, cv_ref, cq_ref,
    ctxb_ref, lse_cross_ref,
    wq_ref, wk_ref, wv_ref, wck_ref, wcv_ref, wso_ref, wcq_ref, wco_ref, win_ref, wout_ref,
    x, t, mem, small_t, mids, wq, wk, wv, wck, wcv, wso, wcq, wco, win, wout,
    h1, h2, low1, low2, q1, k1, v1, q2, k2, v2, lse, ctx1, ctx2, ck, cv, a1, hat1, cq1, cq,
    ctxb1, ctxb, lse_cross, glance, send, recv, local,
):
    length, count = x.shape[0], mem.shape[0]
    slots, langs = hamming.shape[1], lang_t.shape[1]
    every = (slice(None), slice(None))
    buffers = [small_t, wq, wk, wv, wck, wcv, wso, wcq, mids, wco, win, wout]
    pieces = [(i,) + every for i in range(10)]
    pieces += [(10, pl.ds(at, 32), slice(None)) for at in range(0, w_in.shape[1], 32)]
    pieces += [(11, slice(None), pl.ds(at, 512)) for at in range(0, out_t.shape[1], 512)]
    gather = Gather(depth, buffers, pieces, send, recv)
    copies = Copies(local)
    shares = [qkv_t.at[0], qkv_t.at[1], qkv_t.at[2], ckv_t.at[0], ckv_t.at[1], so_t, cq_t]
    owned = [copies.start(share, gather.own(i + 1)) for i, share in enumerate(shares)]
    owned += [copies.start(co_t, gather.own(9)), copies.start(out_t, gather.own(11))]
    rows_in = [copies.start(a, b) for a, b in ((x_ref, x), (t_ref, t), (mem_ref, mem))]
    table = dot(biases[...], placed(BIASES, langs), TN)
    table = table + dot(gains[...], placed(GAINS, langs + BIASES), TN)
    table = table + dot(lang_t[...], placed(langs, 0), NN)
    small_t[tuple(gather.bits)] = table.astype(bf16)
    win[tuple(gather.bits)] = w_in[...].astype(f32).T.astype(bf16)
    mids[tuple(gather.bits)] = jnp.broadcast_to(b_mid[...], mids.shape[-2:])
    gather.enter()
    gather.tick()
    copies.wait(*owned)
    gather.tick()

    position = lax.broadcasted_iota(jnp.int32, (1, length), 1)
    segments = jnp.where(position < target_len[0], raw[...], slots).astype(f32)
    seg_r[...] = segments
    rank_key = priority[...].astype(f32)
    place = position.astype(f32)

    def glanced(at):
        rows = pl.ds(at, 128)
        seg = column(segments, slice(at, at + 128))
        key = column(rank_key, slice(at, at + 128))
        here = (lax.broadcasted_iota(jnp.int32, (128, 1), 0) + at).astype(f32)
        seg_c[rows, :] = seg
        same = segments == seg
        doc_length = jnp.sum(same.astype(f32), axis=1, keepdims=True)
        ahead = (rank_key > key) | ((rank_key == key) & (place < here))
        rank = jnp.sum((same & ahead).astype(f32), axis=1, keepdims=True)
        wanted = jnp.zeros((128, 1), f32)
        for slot in range(slots):
            wanted = jnp.where(seg == float(slot), hamming[0, slot].astype(f32), wanted)
        glance[rows, :] = (2.0 * rank + 1.0 <= jnp.minimum(wanted, doc_length)).astype(f32)

    for at in range(0, length, 128):
        glanced(at)
        if at % 512 == 384:
            gather.tick()
    gather.need(1)
    items = mat(small_t)
    small[...] = dot(placed(16, langs), items, NT)
    choice = lax.broadcasted_iota(jnp.int32, (8, 128), 1) == tag[0]
    lang = dot(choice.astype(bf16), items, NT)[0:1, :]
    copies.wait(*rows_in)

    def combine(rows):
        plain = x[rows, :].astype(f32)
        one = plain + lang
        two = jnp.where(glance[rows, :] > 0.5, t[rows, :].astype(f32), plain) + lang
        h1[rows, :] = one
        h2[rows, :] = two
        low1[rows, :] = one.astype(bf16)
        low2[rows, :] = two.astype(bf16)

    blocks(length, 256, combine)
    copies.start(low2, low2_ref)

    def project(source, weight, bias, out):
        def step(rows):
            value = dot(source[rows, :], mat(weight), NT)
            if bias is not None:
                value = value + small[bias : bias + 1, :]
            out[rows, :] = value.astype(bf16)

        blocks(source.shape[0], 512, step)

    for at, (weight, bias, one, two) in enumerate(
        [(wq, 0, q1, q2), (wk, None, k1, k2), (wv, 1, v1, v2)]
    ):
        gather.need(2 + at)
        project(low1, weight, bias, one)
        project(low2, weight, bias, two)
    for source, target in ((q2, q2_ref), (k2, k2_ref), (v2, v2_ref)):
        copies.start(source, target)

    pause = gather.tick
    for q, k, v, ctx, log_sums in ((q1, k1, v1, ctx1, None), (q2, k2, v2, ctx2, lse)):
        for at in range(0, length, 256):

            def one_block():
                begin, end = max(0, at - most + 1), min(length, at + 256 + most - 1)
                if at + 256 > fewest:
                    begin, end = min(begin, fewest), length
                begin, end = begin // 128 * 128, (end + 127) // 128 * 128
                rows, keys = pl.ds(at, 256), pl.ds(begin, end - begin)
                masked = jnp.where(seg_c[rows, :] == seg_r[:, keys], 0.0, MASKED)
                attend_block(q, k, v, ctx, log_sums, rows, rows, keys, masked, 256)

            apart(one_block)
            pause()
    copies.start(ctx2, ctx2_ref)
    copies.start(lse, lse_ref)
    gather.need(8)
    project(mem, wck, None, ck)
    project(mem, wcv, 4, cv)
    copies.start(ck, ck_ref)
    copies.start(cv, cv_ref)
    pause()

    def start_one(rows):
        after_self(ctx1[rows, :], h1[rows, :], wso, wcq, small, a1, cq1, rows)

    def start_two(rows):
        hat, scale, _ = after_self(ctx2[rows, :], h2[rows, :], wso, wcq, small, None, cq, rows)
        hat1[rows, :] = hat
        scale1[rows, :] = scale

    blocks(length, 512, start_one)
    copies.start(a1, a1_ref)
    pause()
    blocks(length, 512, start_two)
    copies.start(hat1, hat1_ref)
    copies.start(cq, cq_ref)
    pause()
    every_key = pl.ds(0, count)
    source_bias = source_row(source_len, count)
    for query, context, log_sums in ((cq, ctxb, lse_cross), (cq1, ctxb1, None)):
        for at in range(0, length, 256):

            def one_block():
                rows = pl.ds(at, 256)
                attend_block(
                    query, ck, cv, context, log_sums, rows, rows, every_key, source_bias, 256
                )

            apart(one_block)
            if log_sums is not None:
                pause()
            elif at == 0:
                gather.finish()
                for source, target in (
                    (wq, wq_ref), (wk, wk_ref), (wv, wv_ref), (wck, wck_ref), (wcv, wcv_ref),
                    (wso, wso_ref), (wcq, wcq_ref), (wco, wco_ref), (win, win_ref),
                    (wout, wout_ref),
                ):
                    copies.start(source, target)
        if log_sums is not None:
            copies.start(ctxb, ctxb_ref)
            copies.start(lse_cross, lse_cross_ref)
    copies.start(ctxb1, ctxb1_ref)
    for i in range(2**depth):
        owner = mids.at[tuple((i >> (depth - 1 - j)) & 1 for j in range(depth))]
        hidden_bias[:, 128 * i : 128 * i + 128] = owner[0:1, :].astype(f32)
    copies.wait_all()


def turn_kernel(
    depth, slots, source_len,
    scale1, seg_c, small, hidden_bias,
    hat1_ref, ctxb_ref, wco_ref, win_ref, wout_ref, cot_ref,
    cq_ref, ck_ref, cv_ref, lse_ref, mem_ref, wck_ref, wcv_ref, wcq_ref, wso_ref, ctx_ref,
    gr1, gctx, g_so, g_cq, g_ck, g_cv, g_small, g_hidden, o_in, o_out, o_co, out_ref, g_mem_ref,
    hat1, ctxb, wco, win, wout, cq, ck, cv, lse, mem, wck, wcv, wcq, wso, ctx,
    g_in, g_out, g_co, hid, slope, delta, gcq, low2, hat2s, *rest,
):
    length, count = cq.shape[0], ck.shape[0]
    big = 512
    send, recv, local = rest[-3:]
    kinds = itertools.count()
    units = (
        units_of(g_out, g_out.shape[0] >> depth, o_out, g_out.shape[1], kinds)
        + units_of(g_in, g_in.shape[0] >> depth, o_in, g_in.shape[1], kinds)
        + units_of(g_co, g_co.shape[0] >> depth, o_co, g_co.shape[1], kinds)
    )
    downs = g_out.shape[1] // 512
    scatter = Scatter(depth, units, rest[:-3], send, recv)
    agenda = Agenda()
    copies = Copies(local)
    pairs = [
        (hat1_ref, hat1), (ctxb_ref, ctxb), (wco_ref, wco), (win_ref, win), (wout_ref, wout),
        (cot_ref, gctx),
        (cq_ref, cq), (ck_ref, ck), (cv_ref, cv), (lse_ref, lse),
        (mem_ref, mem), (wck_ref, wck), (wcv_ref, wcv), (wcq_ref, wcq), (wso_ref, wso), (ctx_ref, ctx),
    ]
    fetched = [copies.start(source, target) for source, target in pairs]
    for ref in (g_small, g_hidden):
        ref[...] = jnp.zeros_like(ref)
    scatter.enter()
    copies.wait(*fetched[:3])

    out = gcq
    for at in range(0, length, big):
        rows = pl.ds(at, big)
        final = at + big == length
        a = hat1[rows, :] * small[10:11, :] + small[7:8, :]
        copies.wait(*fetched[3:6])
        y, (hat2, scale2, low, hat3, scale3) = after_cross(
            a, ctxb[rows, :], wco, win, wout, small, hidden_bias, hid, slope
        )
        out[rows, :] = y.astype(bf16)
        low2[...] = low
        hat2s[...] = hat2
        live = (seg_c[rows, :] < slots - 0.5).astype(f32)
        gy = gctx[rows, :].astype(f32) * live
        g_small[12:13, :] += column_sum(gy * hat3)
        g_small[9:10, :] += column_sum(gy)
        gr3 = normalise_back(gy, small[12:13, :], hat3, scale3)
        gf = gr3.astype(bf16)
        g_small[6:7, :] += column_sum(gf.astype(f32))
        gb = gr3
        for j in range(downs):
            cols = pl.ds(512 * j, 512)
            gz = (dot(gf, down_part(wout, j), NN) * slope[:, cols]).astype(bf16)
            add_to(g_out, (slice(None), cols), dot(gf, hid[:, cols], TN), at == 0)
            add_to(g_in, (cols, slice(None)), dot(gz, low2[...], TN), at == 0)
            g_hidden[:, cols] += column_sum(gz.astype(f32))
            gb = gb + dot(gz, up_part(win, j), NN)
            if final and j % 2 == 1:
                agenda.round(*[scatter.flow(i) for i in range(j // 2, j)])
        hat2 = hat2s[...]
        g_small[11:12, :] += column_sum(gb * hat2)
        g_small[8:9, :] += column_sum(gb)
        gr2 = normalise_back(gb, small[11:12, :], hat2, scale2)
        gr1[rows, :] = gr2
        go2 = gr2.astype(bf16)
        g_small[5:6, :] += column_sum(go2.astype(f32))
        context = ctxb[rows, :]
        add_to(g_co, ..., dot(go2, context, TN), at == 0)
        back = dot(go2, mat(wco), NN).astype(bf16)
        gctx[rows, :] = back
        delta[rows, :] = head_sums(back.astype(f32) * context.astype(f32))

    keep_out = copies.start(out, out_ref)
    waiting = list(range(downs - 1, len(units)))

    def onward(count):
        fresh = waiting[:count]
        del waiting[:count]
        agenda.round(*[scatter.flow(which) for which in fresh])

    onward(2)
    gk_t, gv_t = slope.at[:, pl.ds(0, count)], slope.at[:, pl.ds(count, count)]
    slope[...] = jnp.zeros_like(slope)
    copies.wait(keep_out, *fetched[6:10])
    every = pl.ds(0, count)
    source_bias = source_row(source_len, count)

    for at in range(0, length, 256):
        attend_back_block(
            cq, ck, cv, gctx, lse, delta, gcq, gk_t, gv_t, pl.ds(at, 256), every, source_bias, 256
        )
        onward(2)
    copies.wait(*fetched[10:])
    gk_low, gv_low = hid.at[:, pl.ds(0, count)], hid.at[:, pl.ds(count, count)]
    gk_low[...] = (gk_t[...] * SCALING).astype(bf16)
    gv_low[...] = gv_t[...].astype(bf16)
    g_ck[...] = dot(gk_low[...], mem[...], NN)
    g_cv[...] = dot(gv_low[...], mem[...], NN)
    ones = jnp.ones((8, count), bf16)
    g_small[4:5, :] = dot(ones, gv_low[...], NT)[0:1, :]
    for i, at in enumerate(range(0, count, 512)):
        cols = pl.ds(at, 512)
        place = slope.at[:, pl.ds(512 * i, 512)]
        place[...] = dot(gk_low[:, cols], mat(wck), TN) + dot(gv_low[:, cols], mat(wcv), TN)
        copies.start(place, g_mem_ref.at[cols, :])
    agenda.round()
    for at in range(0, length, big):
        rows = pl.ds(at, big)
        gq = gcq[rows, :]
        hat = hat1[rows, :]
        low = (hat * small[10:11, :] + small[7:8, :]).astype(bf16)
        g_small[3:4, :] += column_sum(gq.astype(f32))
        add_to(g_cq, ..., dot(gq, low, TN), at == 0)
        ga = gr1[rows, :] + dot(gq, mat(wcq), NN)
        g_small[10:11, :] += column_sum(ga * hat)
        g_small[7:8, :] += column_sum(ga)
        g1 = normalise_back(ga, small[10:11, :], hat, scale1[rows, :])
        gr1[rows, :] = g1
        go = g1.astype(bf16)
        g_small[2:3, :] += column_sum(go.astype(f32))
        add_to(g_so, ..., dot(go, ctx[rows, :], TN), at == 0)
        gctx[rows, :] = dot(go, mat(wso), NN).astype(bf16)
        agenda.round()
    while agenda.busy():
        agenda.round()
    scatter.leave()
    copies.wait_all()


def close_kernel(
    depth, most, tag,
    seg_c, seg_r, g_small, g_hidden, small, hidden_bias,
    gctx_ref, ctx_ref, q_ref, k_ref, v_ref, lse_ref, ck_ref, cv_ref, cq_ref, so_ref, low_ref,
    gr1_ref, wq_ref, wk_ref, wv_ref, a1_ref, ctxb1_ref, wco_ref, win_ref, wout_ref,
    g_x, first, o_qkv, o_ckv, o_cq, o_so, o_table, o_late,
    gctx, ctx, q, k, v, lse, g_ck, g_cv, g_cq, g_so, low, wq, wk, wv, a1, ctxb1, wco, win, wout,
    g_q, g_k, g_v, gq, gk_t, gv_t, gk_low, gv_low, lines, table, late, late_low, late_got,
    late_give, late_get, *rest,
):
    length = q.shape[0]
    size = 256
    send, recv, late_send, late_recv, local = rest[-5:]
    kinds = itertools.count()
    width = g_q.shape[0]
    share, devices = width >> depth, 1 << depth
    units = []
    for source, out in [(g_ck, o_ckv.at[0]), (g_cv, o_ckv.at[1]), (g_cq, o_cq), (g_so, o_so)]:
        units += units_of(source, share, out, width, kinds)
    units += units_of(table, share, o_table, table.shape[1], kinds)
    for i, source in enumerate((g_q, g_k, g_v)):
        units += units_of(source, share, o_qkv.at[i], width, kinds, apart=True)
    scatter = Scatter(depth, units, rest[:-5], send, recv)
    agenda = Agenda()
    copies = Copies(local)
    pairs = [
        (gctx_ref, gctx), (ctx_ref, ctx), (q_ref, q), (k_ref, k), (v_ref, v), (lse_ref, lse),
        (ck_ref, g_ck), (cv_ref, g_cv), (cq_ref, g_cq), (so_ref, g_so),
        (low_ref, low), (gr1_ref, g_x), (wq_ref, wq), (wk_ref, wk), (wv_ref, wv),
        (a1_ref, a1), (ctxb1_ref, ctxb1), (wco_ref, wco), (win_ref, win), (wout_ref, wout),
    ]
    fetched = [copies.start(source, target) for source, target in pairs]
    scatter.enter(range(1, devices))
    for ref in (gk_t, gv_t, lines, table):
        ref[...] = jnp.zeros_like(ref)
    langs = lines.shape[0] // 2
    lines[langs : langs + 16, :] = g_small[...]
    table[:, 0:128] = lines[...].T
    for owner in range(devices):
        table[share * owner : share * owner + 1, 128:256] = g_hidden[:, 128 * owner : 128 * owner + 128]
    copies.wait(*fetched[:6])
    early = [[0, 1], [2, 3], [4], []]
    for turn in range(HEADS // 2):
        pair = lax.rem(scatter.plane + 1 + turn, HEADS // 2)
        cols = pl.ds(pl.multiple_of(128 * pair, 128), 128)
        for at in range(0, length, size):
            begin = max(0, (at - most + 1) // 128 * 128)
            end = min(length, (at + size + most - 1 + 127) // 128 * 128)
            rows, keys = pl.ds(at, size), pl.ds(begin, end - begin)
            masked = jnp.where(seg_c[rows, :] == seg_r[:, keys], 0.0, MASKED)
            attend_back_pair(
                q, k, v, gctx, head_columns(lse[rows, :], pair),
                head_products(gctx[rows, cols], ctx[rows, cols]),
                gq, gk_t, gv_t, rows, keys, masked, size, cols,
            )
        copies.wait(*fetched[6:15])
        gk_low[cols, :] = (gk_t[cols, :] * SCALING).astype(bf16)
        gv_low[cols, :] = gv_t[cols, :].astype(bf16)
        g_q[cols, :] = dot(gq[:, cols], low[...], TN)
        g_k[cols, :] = dot(gk_low[cols, :], low[...], NN)
        g_v[cols, :] = dot(gv_low[cols, :], low[...], NN)
        fresh = [scatter.part(5 + i, turn) for i in range(3)]
        agenda.round(*[scatter.flow(which) for which in early[turn]], *fresh)
    ones = jnp.ones((8, length), bf16)
    sums = [
        dot(ones, gq[...], NN)[0:1, :],
        dot(ones, gk_low[...], NT)[0:1, :],
        dot(ones, gv_low[...], NT)[0:1, :],
    ]
    total = column_sum(g_x[...])
    down = lax.broadcasted_iota(jnp.int32, (8, width), 0)
    for value, weight in zip(sums, (wq, wk, wv)):
        top = value.astype(bf16)
        middle = (value - top.astype(f32)).astype(bf16)
        bottom = (value - top.astype(f32) - middle.astype(f32)).astype(bf16)
        split = jnp.where(down == 0, top.astype(f32), jnp.where(down == 1, middle.astype(f32), 0.0))
        split = jnp.where(down == 2, bottom.astype(f32), split).astype(bf16)
        total = total + column_sum(dot(split, mat(weight), NN))
    down = lax.broadcasted_iota(jnp.int32, lines.shape, 0)
    value = jnp.where(down == tag[0], total, 0.0)
    value = jnp.where(down == langs, sums[0], jnp.where(down == langs + 1, sums[2], value))
    late[...] = value.T
    late_low[...] = late[...].astype(bf16)

    def own_rows(owner):
        return pl.ds(pl.multiple_of(owner * share, share), share)

    def straight(step):
        target = lax.rem(scatter.me + step, devices)
        return pltpu.make_async_remote_copy(
            late_low.at[own_rows(target), :],
            late_got.at[step - 1],
            late_send.at[step],
            late_recv.at[step],
            device_id=(scatter.rep, target),
            device_id_type=MESH,
        )

    def hand_over():
        return pltpu.make_async_remote_copy(
            late_give,
            late_get,
            late_send.at[0],
            late_recv.at[0],
            device_id=scatter.near("rep"),
            device_id_type=MESH,
        )

    for step in range(1, devices):
        straight(step).start()
    agenda.round()
    for at in range(0, length, 512):
        rows = pl.ds(at, 512)
        value = g_x[rows, :] + dot(gq[rows, :], mat(wq), NN)
        value = value + dot(gk_low[:, rows], mat(wk), TN) + dot(gv_low[:, rows], mat(wv), TN)
        g_x[rows, :] = value
        agenda.round()
    copies.wait_all()
    endings = [scatter.ending(5 + i) for i in range(3)]
    for at in range(0, length, 512):
        rows = pl.ds(at, 512)
        y, _ = after_cross(
            a1[rows, :], ctxb1[rows, :], wco, win, wout, small, hidden_bias, None, None
        )
        first[rows, :] = y.astype(bf16)
        if at > 0:
            continue
        while agenda.busy():
            agenda.round()
        for steps in endings:
            steps.pop(0)()
        value = late[own_rows(scatter.me), :]
        for step in range(1, devices):
            straight(step).wait_recv()
            value = value + late_got[step - 1].astype(f32)
        value = value.astype(bf16)
        late_give[...] = value
        hand_over().start()
    for steps in endings:
        steps.pop(0)()
    hand_over().wait_recv()
    o_late[...] = value.astype(f32) + late_get[...].astype(f32)
    scatter.leave()
    for step in range(1, devices):
        straight(step).wait_send()
    hand_over().wait_send()


def finish_kernel(langs, qkv, ckv, cq, so, co, up, down, table, late, *refs):
    large, outs, held, semaphores = refs[:4], refs[4:-5], refs[-5:-1], refs[-1]
    copies = Copies(semaphores)
    moves = []
    for source, place, out in zip(large, held, outs[11:]):
        for at in range(0, source.shape[0], 512):
            rows = pl.ds(at, 512)
            inward = copies.start(source.at[rows, :], place.at[rows, :])
            moves.append((inward, place.at[rows, :], out.at[rows, :]))
    for inward, place, out in moves:
        copies.wait(inward)
        copies.start(place, out)
    for source, out in zip((qkv, ckv, cq, so, co, down), outs):
        out[...] = source[...]
    outs[6][...] = up[...].T
    items = late[...]
    lines, soon = table[:, 0:128].T, items.T
    outs[7][...] = lines[langs : langs + BIASES, :]
    outs[7][0:2, :] = soon[langs : langs + 2, :]
    outs[8][...] = lines[langs + BIASES : langs + BIASES + GAINS, :]
    outs[9][...] = table[0:1, 128:256]
    outs[10][...] = items[:, 0:langs]
    copies.wait_all()


def transfer_call(kernel, name, collective_id, outs, args, scratch, scalars, away, away_out):
    in_specs = [pl.BlockSpec(memory_space=pltpu.SMEM)] * scalars
    for at in range(scalars, len(args)):
        in_specs.append(pl.BlockSpec(memory_space=pl.ANY if at >= away else VMEM))
    out_specs = [
        pl.BlockSpec(memory_space=pl.ANY if at >= away_out else VMEM) for at in range(len(outs))
    ]
    return pl.pallas_call(
        kernel,
        out_shape=outs,
        in_specs=in_specs,
        out_specs=out_specs,
        scratch_shapes=list(scratch),
        name=name,
        compiler_params=pltpu.CompilerParams(
            collective_id=collective_id, has_side_effects=True, vmem_limit_bytes=62 * 2**20
        ),
    )(*args)


def shards(
    n,
    x_copy,
    target_embed,
    memory,
    cotangent,
    segment_ids,
    source_lengths,
    target_lengths,
    hamming,
    priority,
    lang_tag,
    w_self_qkv,
    w_self_out,
    w_cross_q,
    w_cross_kv,
    w_cross_out,
    w_in,
    w_out,
    biases,
    gains,
    b_hidden,
    lang_table,
):
    depth = int(math.log2(n))
    length, width = x_copy.shape[1:]
    source = memory.shape[1]
    hidden = b_hidden.shape[0] * n
    share = width // n
    langs = lang_table.shape[0]
    most, fewest = 256, 384
    bits = (2,) * depth
    flat, side = (length, width), (source, width)
    lse = (length, 128)
    whole, up, down = bits + (share, width), bits + (hidden // n, width), bits + (share, hidden)
    square = (width, width)
    mem = memory[0]

    def low(dims):
        return shape(dims, bf16)

    def scratch(*all_dims, dtype=bf16):
        return [VMEM(dims, dtype) for dims in all_dims]

    kept = [
        shape(flat), low(flat), shape(flat), low(flat), low(flat), low(flat), low(flat), shape(lse), low(flat), low(side),
        low(side), low(flat), low(flat), shape(lse),
    ]
    weights = [low(whole)] * 8 + [low(up), low(down)]
    pieces = 10 + hidden // n // 32 + hidden // 512
    (
        small, seg_c, seg_r, hidden_bias, scale1,
        a1, ctxb1, hat1, low2, q, k, v, lse_self, ctx, ck, cv, cq, ctxb, lse_cross,
        wq, wk, wv, wck, wcv, wso, wcq, wco, win, wout,
    ) = transfer_call(
        functools.partial(forward_kernel, depth, most, fewest),
        "forward",
        2,
        [
            shape((16, width)), shape((length, 1)), shape((1, length)), shape((1, hidden)),
            shape((length, 1)),
        ]
        + kept
        + weights,
        (
            target_lengths, lang_tag, hamming, source_lengths, segment_ids, priority, biases, gains,
            lang_table.T, w_in, b_hidden[None], x_copy[0], target_embed[0], mem,
            w_self_qkv.transpose(0, 2, 1), w_cross_kv.transpose(0, 2, 1), w_self_out.T,
            w_cross_q.T, w_cross_out.T, w_out.T,
        ),
        scratch(flat, flat, side, bits + (share, 128), bits + (16, 128), *[whole] * 8, up, down)
        + scratch(flat, flat, dtype=f32)
        + scratch(*[flat] * 8)
        + scratch(lse, dtype=f32)
        + scratch(flat, flat, side, side)
        + scratch(flat, flat, dtype=f32)
        + scratch(*[flat] * 4)
        + scratch(lse, (length, 1), dtype=f32)
        + [pltpu.SemaphoreType.DMA((pieces, n // 4 + 1))] * 2
        + [pltpu.SemaphoreType.DMA((40,))],
        4,
        11,
        5,
    )
    big = 512
    blocks_in, blocks_out = hidden // n // 32, hidden // 512
    kinds = [(512, i % 2, False) for i in range(blocks_in + blocks_out + 1)]
    (
        gr1, gctx, g_so, g_cq, g_ck, g_cv, g_small, g_hidden, o_in, o_out, o_co, out, g_mem,
    ) = transfer_call(
        functools.partial(turn_kernel, depth, hamming.shape[1]),
        "turn",
        3,
        [shape(flat), low(flat)]
        + [shape(square)] * 4
        + [
            shape((16, width)), shape((1, hidden)), shape((hidden // n, width)),
            shape((share, hidden)), shape((share, width)), low(flat), shape(side),
        ],
        (
            source_lengths, scale1, seg_c, small, hidden_bias,
            hat1, ctxb, wco, win, wout, cotangent[0], cq, ck, cv, lse_cross, mem, wck, wcv, wcq,
            wso, ctx,
        ),
        scratch(flat, dtype=f32)
        + scratch(flat, whole, up, down, flat, side, side)
        + scratch(lse, dtype=f32)
        + scratch(side, whole, whole, whole, whole, flat)
        + scratch((hidden, width), (width, hidden), square, dtype=f32)
        + scratch((big, hidden))
        + scratch((width, max(hidden, 2 * source)), lse, dtype=f32)
        + scratch(flat, (big, width))
        + scratch((big, width), dtype=f32)
        + Scatter.scratch(depth, kinds)
        + [pltpu.SemaphoreType.DMA((24,))],
        1,
        5,
        11,
    )
    kinds = [(512, i % 2, False) for i in range(4)] + [(256, 0, False)]
    kinds += [(512, i % 2, True) for i in range(5, 8)]
    turned = (width, length)
    g_x, first, o_qkv, o_ckv, o_cq, o_so, o_table, o_late = transfer_call(
        functools.partial(close_kernel, depth, most),
        "close",
        4,
        [
            shape(flat), low(flat), shape((3, share, width)), shape((2, share, width)),
            shape((share, width)), shape((share, width)), shape((share, 256)), shape((share, 128)),
        ],
        (
            lang_tag, seg_c, seg_r, g_small, g_hidden, small, hidden_bias,
            gctx, ctx, q, k, v, lse_self, g_ck, g_cv, g_cq, g_so, low2, gr1, wq, wk, wv,
            a1, ctxb1, wco, win, wout,
        ),
        scratch(*[flat] * 5)
        + scratch(lse, *[square] * 4, dtype=f32)
        + scratch(flat, whole, whole, whole)
        + scratch(flat, dtype=f32)
        + scratch(flat, whole, up, down)
        + scratch(*[square] * 3, dtype=f32)
        + scratch(flat)
        + scratch(turned, turned, dtype=f32)
        + scratch(turned, turned)
        + scratch((2 * langs, width), (width, 256), (width, 128), dtype=f32)
        + scratch((width, 128), (n - 1, share, 128), (share, 128), (share, 128))
        + Scatter.scratch(depth, kinds)
        + [pltpu.SemaphoreType.DMA((n,))] * 2
        + [pltpu.SemaphoreType.DMA((24,))],
        1,
        7,
        8,
    )
    own = shape((share, width))
    large = (first, out, g_x, g_mem)
    small_outs = [
        shape((3, share, width)), shape((2, share, width)), own, own, own,
        shape((share, hidden)), shape((width, hidden // n)), shape((BIASES, share)),
        shape((GAINS, share)), shape((1, hidden // n)), shape((share, langs)),
    ]
    here, there = pl.BlockSpec(memory_space=VMEM), pl.BlockSpec(memory_space=pl.ANY)
    g_qkv, g_ckv, g_cq, g_so, g_co, g_out, g_in, g_bias, g_gain, g_mid, g_lang, *large = (
        pl.pallas_call(
            functools.partial(finish_kernel, langs),
            out_shape=small_outs + [jax.ShapeDtypeStruct(v.shape, v.dtype) for v in large],
            in_specs=[here] * 9 + [there] * 4,
            out_specs=[here] * 11 + [there] * 4,
            scratch_shapes=[VMEM(v.shape, v.dtype) for v in large]
            + [pltpu.SemaphoreType.DMA((16,))],
            name="finish",
            compiler_params=pltpu.CompilerParams(vmem_limit_bytes=61 * 2**20),
        )(o_qkv, o_ckv, o_cq, o_so, o_co, o_in, o_out, o_table, o_late, *large)
    )
    first, out, g_x, g_mem = large
    return (
        first[None],
        out[None],
        g_x[None],
        g_mem[None],
        g_qkv.transpose(0, 2, 1),
        g_so.T,
        g_cq.T,
        g_ckv.transpose(0, 2, 1),
        g_co.T,
        g_in,
        g_out.T,
        g_bias,
        g_gain,
        g_mid[0],
        g_lang.T,
    )


def choose(n):
    return shards if n * 32 == 512 else shards_apart


def solution(mesh):
    n = mesh.shape["dp"]
    row3, row2, row1 = P(("rep", "dp"), None, None), P(("rep", "dp"), None), P(("rep", "dp"))
    wide, tall, flat = P(None, None, "dp"), P(None, "dp"), P("dp")
    parameters = (wide, tall, tall, wide, tall, tall, tall, tall, tall, flat, tall)
    return jax.shard_map(
        functools.partial(choose(n), n),
        mesh=mesh,
        in_specs=(row3, row3, row3, row3, row2, row1, row1, row2, row2, row1) + parameters,
        out_specs=(row3, row3, row3, row3) + parameters,
        check_vma=False,
    )
```

```python
import functools
import itertools
import math

import jax
import jax.numpy as jnp
from jax import lax
from jax.experimental import pallas as pl
from jax.experimental.pallas import tpu as pltpu
from jax.sharding import PartitionSpec as P

f32, bf16 = jnp.float32, jnp.bfloat16
MESH = pl.DeviceIdType.MESH
VMEM = pltpu.VMEM

HEADS = 8
HD = 64
EPSILON = 1e-05
MASKED = -1000000000.0
LOG2E = 1.4426950408889634
SCORE = LOG2E * HD ** (-0.5)
SCALING = HD ** (-0.5)

NT = (((1,), (1,)), ((), ()))
NN = (((1,), (0,)), ((), ()))
TN = (((0,), (0,)), ((), ()))

BIASES, GAINS = 10, 3


def dot(left, right, form):
    return lax.dot_general(left, right, form, preferred_element_type=f32)


def own_bits(index, depth):
    return [lax.rem(index // (1 << (depth - 1 - j)), 2) for j in range(depth)]


def partner_of(index, bit, depth, j):
    return index + (1 - 2 * bit) * (1 << (depth - 1 - j))


def enter(rep, me, partners, with_rep):
    barrier = pltpu.get_barrier_semaphore()
    for partner in partners:
        pl.semaphore_signal(barrier, inc=1, device_id=(rep, partner), device_id_type=MESH)
    if with_rep:
        pl.semaphore_signal(barrier, inc=1, device_id=(1 - rep, me), device_id_type=MESH)
    pl.semaphore_wait(barrier, len(partners) + int(with_rep))


def gather_kernel(depth, pieces, count, *refs):
    ins, outs = refs[:count], refs[count : 2 * count]
    send, recv, local = refs[2 * count :]
    rep, me = lax.axis_index("rep"), lax.axis_index("dp")
    bits = own_bits(me, depth)
    partners = [partner_of(me, bits[j], depth, j) for j in range(depth)]
    copies = [
        pltpu.make_async_copy(ins[i], outs[i].at[tuple(bits)], local.at[i]) for i in range(count)
    ]
    for copy in copies:
        copy.start()
    enter(rep, me, partners, False)
    for copy in copies:
        copy.wait()
    started = {}
    for tick in range(len(pieces) + depth - 1):
        for j in reversed(range(depth)):
            b = tick - j
            if not 0 <= b < len(pieces):
                continue
            if j > 0:
                started[b, j - 1].wait_recv()
            which, rows, cols = pieces[b]
            part = outs[which].at[(slice(None),) * j + tuple(bits[j:]) + (rows, cols)]
            copy = pltpu.make_async_remote_copy(
                part,
                part,
                send.at[b, j],
                recv.at[b, j],
                device_id=(rep, partners[j]),
                device_id_type=MESH,
            )
            copy.start()
            started[b, j] = copy
    for (b, j), copy in started.items():
        copy.wait_send()
        if j == depth - 1:
            copy.wait_recv()


def gather_all(n, shards, collective_id):
    depth = int(math.log2(n))
    pieces = []
    for i, shard in enumerate(shards):
        r, c = shard.shape
        if c > 512:
            pieces += [(i, slice(None), pl.ds(at, 512)) for at in range(0, c, 512)]
        elif r >= 128:
            pieces += [(i, pl.ds(at, 32), slice(None)) for at in range(0, r, 32)]
        else:
            pieces.append((i, slice(None), slice(None)))
    count = len(shards)
    outs = pl.pallas_call(
        functools.partial(gather_kernel, depth, pieces, count),
        out_shape=[jax.ShapeDtypeStruct((2,) * depth + s.shape, s.dtype) for s in shards],
        in_specs=[pl.BlockSpec(memory_space=pl.ANY)] * count,
        out_specs=[pl.BlockSpec(memory_space=pl.ANY)] * count,
        scratch_shapes=[
            pltpu.SemaphoreType.DMA((len(pieces), depth)),
            pltpu.SemaphoreType.DMA((len(pieces), depth)),
            pltpu.SemaphoreType.DMA((count,)),
        ],
        name="gather_weights",
        compiler_params=pltpu.CompilerParams(collective_id=collective_id, has_side_effects=True),
    )(*shards)
    return [out.reshape(n * s.shape[0], s.shape[1]) for out, s in zip(outs, shards)]


def scatter_kernel(depth, pieces, groups, count, *refs):
    ins, outs = refs[:count], refs[count : 2 * count]
    at = 2 * count
    stages = depth + 1
    gives = {}
    gets = {}
    for group in groups:
        gives[group] = refs[at : at + stages]
        gets[group] = refs[at + stages : at + 2 * stages]
        at += 2 * stages
    send, recv = refs[at:]
    rep, me = lax.axis_index("rep"), lax.axis_index("dp")
    bits = own_bits(me, depth)
    partners = [partner_of(me, bits[j], depth, j) for j in range(depth)]
    enter(rep, me, partners, True)
    started = {}
    for tick in range(len(pieces) + depth + 1):
        for s in reversed(range(depth + 2)):
            b = tick - s
            if not 0 <= b < len(pieces):
                continue
            which, rows, cols, group, slot = pieces[b]
            source = ins[which]
            j = depth - 1 - s
            if s > 0:
                started[b, s - 1].wait_recv()
            if s == depth + 1:
                mine = gives[group][depth][slot].astype(f32)
                outs[which][rows, cols] = mine + gets[group][depth][slot].astype(f32)
                continue
            if j >= 0:
                head = (slice(None),) * j
                tail = tuple(bits[j + 1 :]) + (rows, cols)
                give = head + (1 - bits[j],) + tail
                keep = head + (bits[j],) + tail
                if s == 0:
                    gives[group][0][slot] = source[give].astype(bf16)
                else:
                    got = gets[group][s - 1].at[slot]
                    gives[group][s][slot] = (
                        source[give] + got[head + (1 - bits[j],)].astype(f32)
                    ).astype(bf16)
                    source[keep] = source[keep] + got[head + (bits[j],)].astype(f32)
                target = (rep, partners[j])
            else:
                got = gets[group][s - 1][slot].astype(f32)
                gives[group][s][slot] = (source[tuple(bits) + (rows, cols)] + got).astype(bf16)
                target = (1 - rep, me)
            copy = pltpu.make_async_remote_copy(
                gives[group][s].at[slot],
                gets[group][s].at[slot],
                send.at[b, s],
                recv.at[b, s],
                device_id=target,
                device_id_type=MESH,
            )
            copy.start()
            started[b, s] = copy
    for copy in started.values():
        copy.wait_send()


def scatter_all(n, grads, collective_id):
    depth = int(math.log2(n))
    pieces, views, shapes, sizes = [], [], [], {}
    for i, grad in enumerate(grads):
        r, c = grad.shape[0] // n, grad.shape[1]
        views.append(grad.reshape((2,) * depth + (r, c)))
        shapes.append((r, c))
        high, wide = min(r, 32), min(c, 512)
        for a in range(0, r, high):
            for q in range(0, c, wide):
                slot = sizes.get((high, wide), 0)
                sizes[high, wide] = slot + 1
                pieces.append((i, pl.ds(a, high), pl.ds(q, wide), (high, wide), slot))
    count = len(grads)
    groups = sorted(sizes)
    scratch = []
    for group in groups:
        buffers = [
            VMEM((sizes[group],) + (2,) * max(depth - 1 - s, 0) + group, bf16)
            for s in range(depth + 1)
        ]
        scratch += buffers + buffers
    return pl.pallas_call(
        functools.partial(scatter_kernel, depth, pieces, groups, count),
        out_shape=[jax.ShapeDtypeStruct(s, f32) for s in shapes],
        in_specs=[pl.BlockSpec(memory_space=VMEM)] * count,
        out_specs=[pl.BlockSpec(memory_space=VMEM)] * count,
        scratch_shapes=scratch
        + [
            pltpu.SemaphoreType.DMA((len(pieces), depth + 1)),
            pltpu.SemaphoreType.DMA((len(pieces), depth + 1)),
        ],
        name="scatter_gradients",
        compiler_params=pltpu.CompilerParams(
            collective_id=collective_id, has_side_effects=True, vmem_limit_bytes=60 * 2**20
        ),
    )(*views)


class Gather:
    lag, steps = 2, 3

    def __init__(self, depth, buffers, pieces, send, recv):
        self.depth, self.buffers, self.pieces = depth, buffers, pieces
        self.send, self.recv = send, recv
        self.rep, self.me = lax.axis_index("rep"), lax.axis_index("dp")
        self.bits = own_bits(self.me, depth)
        self.planes = 1 << (depth - 2)
        self.far = [
            (self.rep, lax.rem(self.me + 4 * k, 4 * self.planes)) for k in range(1, self.planes)
        ]
        self.near = [
            (self.rep, partner_of(self.me, self.bits[j], depth, j)) for j in (depth - 2, depth - 1)
        ]
        self.time, self.arrived = 0, set()

    def enter(self):
        barrier = pltpu.get_barrier_semaphore()
        for target in self.far + self.near:
            pl.semaphore_signal(barrier, inc=1, device_id=target, device_id_type=MESH)
        pl.semaphore_wait(barrier, len(self.far) + len(self.near))

    def own(self, which):
        return self.buffers[which].at[tuple(self.bits)]

    def transfers(self, b, j):
        which, rows, cols = self.pieces[b]
        fixed = [0, self.depth - 2, self.depth - 1][j]
        part = self.buffers[which].at[(slice(None),) * fixed + tuple(self.bits[fixed:]) + (rows, cols)]
        targets = self.far if j == 0 else [self.near[j - 1]]
        first = [0, len(self.far), len(self.far) + 1][j]
        return [
            pltpu.make_async_remote_copy(
                part,
                part,
                self.send.at[b, first + i],
                self.recv.at[b, first + i],
                device_id=target,
                device_id_type=MESH,
            )
            for i, target in enumerate(targets)
        ]

    def tick(self):
        for j in reversed(range(self.steps)):
            b = self.time - self.lag * j
            if 0 <= b < len(self.pieces):
                if j > 0:
                    for copy in self.transfers(b, j - 1):
                        copy.wait_recv()
                for copy in self.transfers(b, j):
                    copy.start()
        self.time += 1

    def need(self, count):
        for b in range(count):
            if b in self.arrived:
                continue
            while self.time <= b + self.lag * (self.steps - 1):
                self.tick()
            for copy in self.transfers(b, self.steps - 1):
                copy.wait_recv()
            self.arrived.add(b)

    def finish(self):
        self.need(len(self.pieces))
        for b in range(len(self.pieces)):
            for j in range(self.steps):
                for copy in self.transfers(b, j):
                    copy.wait_send()


class Agenda:
    def __init__(self):
        self.flows = []

    def round(self, *fresh):
        for steps in self.flows:
            if steps:
                steps.pop(0)()
        for steps in fresh:
            steps.pop(0)()
            self.flows.append(steps)

    def busy(self):
        return any(self.flows)


class Scatter:
    def __init__(self, depth, units, refs, send, recv):
        self.planes, self.units = 1 << (depth - 2), units
        self.rep, self.me = lax.axis_index("rep"), lax.axis_index("dp")
        self.core = lax.rem(self.me, 2)
        self.x = lax.rem(self.me // 2, 2)
        self.plane = self.me // 4
        self.send, self.recv = send, recv
        at, mark = 0, 0
        for unit in units:
            unit["parts"] = []
            planes = list(range(self.planes))
            turns = [[lax.rem(self.plane + 1 + p, self.planes)] for p in planes]
            for part in turns if unit["apart"] else [planes]:
                steps = []
                for _ in range(3):
                    steps.append((refs[at], refs[at + 1], mark))
                    at, mark = at + 2, mark + 1
                unit["parts"].append((part, steps))
            unit["across"], unit["last"] = (refs[at], refs[at + 1], mark), (refs[at + 2], refs[at + 3], mark + self.planes - 1)
            at, mark = at + 4, mark + self.planes

    @staticmethod
    def scratch(depth, kinds):
        planes, buffers, marks = 1 << (depth - 2), [], 0
        for wide, kind, apart in kinds:
            half = wide // 2
            for count in [1] * planes if apart else [planes]:
                middle = (count, 32, wide) if kind == 0 else (2 * count, 32, half)
                for dims in [(2 * count, 32, wide), middle, (count, 32, half)]:
                    buffers += [VMEM(dims, bf16)] * 2
                    marks += 1
            buffers += [VMEM((planes, 32, half), bf16), VMEM((planes - 1, 32, half), bf16)]
            buffers += [VMEM((32, half), bf16)] * 2
            marks += planes
        return buffers + [pltpu.SemaphoreType.DMA((marks,))] * 2

    def enter(self, steps=()):
        barrier = pltpu.get_barrier_semaphore()
        targets = [self.near("rep")]
        if steps:
            devices = 4 * self.planes
            targets += [(self.rep, lax.rem(self.me + k, devices)) for k in steps]
        else:
            targets += [self.near("core"), self.near("x")]
            targets += [self.far(k)[1] for k in range(1, self.planes)]
        for target in targets:
            pl.semaphore_signal(barrier, inc=1, device_id=target, device_id_type=MESH)
        pl.semaphore_wait(barrier, len(targets))

    def near(self, dim):
        if dim == "rep":
            return (1 - self.rep, self.me)
        if dim == "x":
            return (self.rep, self.me + 2 * (1 - 2 * self.x))
        return (self.rep, self.me + 1 - 2 * self.core)

    def far(self, k):
        plane = lax.rem(self.plane + k, self.planes)
        return plane, (self.rep, plane * 4 + lax.rem(self.me, 4))

    def transfer(self, give, get, mark, target):
        return pltpu.make_async_remote_copy(
            give,
            get,
            self.send.at[mark],
            self.recv.at[mark],
            device_id=target,
            device_id_type=MESH,
        )

    def part(self, which, index):
        unit = self.units[which]
        planes, buffers = unit["parts"][index]
        source, r, a, c0, wide = (unit[name] for name in ("source", "r", "a", "c0", "wide"))
        half, count = wide // 2, len(planes)
        dims = ["core", "x", "rep"] if unit["kind"] == 0 else ["core", "rep", "x"]
        whole = pl.ds(c0, wide)
        mine = pl.ds(pl.multiple_of(c0 + half * self.rep, 128), half)
        other = pl.ds(pl.multiple_of(c0 + half * (1 - self.rep), 128), half)
        mine_got = pl.ds(pl.multiple_of(half * self.rep, 128), half)
        other_got = pl.ds(pl.multiple_of(half * (1 - self.rep), 128), half)

        def rows(plane, x, core):
            return pl.ds(pl.multiple_of((plane * 4 + x * 2 + core) * r + a, 32), 32)

        def moved(step):
            give, get, mark = buffers[step]
            return self.transfer(give, get, mark, self.near(dims[step]))

        def first():
            give = buffers[0][0]
            for x in range(2):
                for i, plane in enumerate(planes):
                    give[x * count + i] = source[rows(plane, x, 1 - self.core), whole].astype(bf16)
            moved(0).start()

        def over_x(step, columns):
            moved(step - 1).wait_recv()
            give, got = buffers[step][0], buffers[step - 1][1]
            for i, plane in enumerate(planes):
                away = rows(plane, 1 - self.x, self.core)
                here = rows(plane, self.x, self.core)
                give[i] = (
                    source[away, columns] + got[(1 - self.x) * count + i].astype(f32)
                ).astype(bf16)
                source[here, columns] = source[here, columns] + got[self.x * count + i].astype(f32)
            moved(step).start()

        def over_rep(step):
            moved(step - 1).wait_recv()
            give, got = buffers[step][0], buffers[step - 1][1]
            for x in range(2) if step == 1 else [self.x]:
                for i, plane in enumerate(planes):
                    at = x * count + i if step == 1 else i
                    here = rows(plane, x, self.core)
                    give[at] = (source[here, other] + got[at, :, other_got].astype(f32)).astype(bf16)
                    source[here, mine] = source[here, mine] + got[at, :, mine_got].astype(f32)
            moved(step).start()

        def summed():
            moved(2).wait_recv()
            got, across = buffers[2][1], unit["across"][0]
            for i, plane in enumerate(planes):
                here = rows(plane, self.x, self.core)
                total = source[here, mine] + got[i].astype(f32)
                source[here, mine] = total
                across[plane] = total.astype(bf16)
            if unit["apart"] and index + 1 < self.planes:
                self.sent(which, index + 1).start()

        if unit["kind"] == 0:
            return [first, lambda: over_x(1, whole), lambda: over_rep(2), summed]
        return [first, lambda: over_rep(1), lambda: over_x(2, mine), summed]

    def ending(self, which):
        unit = self.units[which]
        source, r, a, c0, wide = (unit[name] for name in ("source", "r", "a", "c0", "wide"))
        out, out_col = unit["out"], unit["out_col"]
        half = wide // 2
        get = unit["across"][1]
        last = self.transfer(*unit["last"], self.near("rep"))
        mine = pl.ds(pl.multiple_of(c0 + half * self.rep, 128), half)

        def across():
            for k in range(1, self.planes):
                self.sent(which, k).start()

        def total():
            value = source[pl.ds(pl.multiple_of(self.me * r + a, 32), 32), mine]
            for k in range(1, self.planes):
                self.sent(which, k).wait_recv()
                value = value + get[k - 1].astype(f32)
            value = value.astype(bf16)
            unit["last"][0][...] = value
            own = pl.ds(pl.multiple_of(out_col + half * self.rep, 128), half)
            out[pl.ds(a, 32), own] = value.astype(f32)
            last.start()

        def rest():
            last.wait_recv()
            other = pl.ds(pl.multiple_of(out_col + half * (1 - self.rep), 128), half)
            out[pl.ds(a, 32), other] = unit["last"][1][...].astype(f32)

        return [total, rest] if unit["apart"] else [across, total, rest]

    def flow(self, which):
        steps, (across, *rest) = self.part(which, 0), self.ending(which)

        def summed():
            steps[-1]()
            across()

        return steps[:-1] + [summed] + rest

    def sent(self, which, k):
        give, get, mark = self.units[which]["across"]
        plane, target = self.far(k)
        return self.transfer(give.at[plane], get.at[k - 1], mark + k - 1, target)

    def leave(self):
        for which, unit in enumerate(self.units):
            dims = ["core", "x", "rep"] if unit["kind"] == 0 else ["core", "rep", "x"]
            for _, buffers in unit["parts"]:
                for step, (give, get, mark) in enumerate(buffers):
                    self.transfer(give, get, mark, self.near(dims[step])).wait_send()
            for k in range(1, self.planes):
                self.sent(which, k).wait_send()
            self.transfer(*unit["last"], self.near("rep")).wait_send()


def units_of(source, r, out, wide, kinds, apart=False):
    units = []
    for a in range(0, r, 32):
        for c0 in range(0, wide, 512):
            units.append(
                dict(
                    source=source, r=r, a=a, c0=c0, wide=min(512, wide - c0), out=out, out_col=c0,
                    kind=next(kinds) % 2, apart=apart,
                )
            )
    return units


def both_heads(pair, low):
    zero = jnp.zeros_like(pair)
    return jnp.concatenate([jnp.where(low, pair, zero), jnp.where(low, zero, pair)], axis=0)


def twice(bias):
    return bias if bias.shape[0] == 1 else jnp.concatenate([bias, bias], axis=0)


def attend_block(q, k, v, ctx, lse, rows, key_rows, keys, bias, size, after=None):
    low = lax.broadcasted_iota(jnp.int32, (size, 128), 1) < HD
    lanes = lax.broadcasted_iota(jnp.int32, (size, 128), 1)
    bias = twice(bias)
    log_sums = jnp.zeros((size, 128), f32)

    def scores(pair):
        cols = pl.ds(128 * pair, 128)
        return dot(both_heads(q[rows, cols], low), k[keys, cols], NT) * SCORE + bias

    following = scores(0)
    for pair in range(HEADS // 2):
        cols = pl.ds(128 * pair, 128)
        s = following
        if pair + 1 < HEADS // 2:
            following = scores(pair + 1)
        largest = jnp.max(s, axis=1, keepdims=True)
        powers = jnp.exp2(s - largest)
        total = jnp.sum(powers, axis=1, keepdims=True)
        c = dot(powers.astype(bf16), v[keys, cols], NN) * (1.0 / total)
        ctx[rows, cols] = jnp.where(low, c[:size], c[size:]).astype(bf16)
        if lse is not None:
            log_sum = largest + jnp.log2(total)
            log_sums = jnp.where(lanes == 2 * pair, log_sum[:size], log_sums)
            log_sums = jnp.where(lanes == 2 * pair + 1, log_sum[size:], log_sums)
        if after is not None:
            after()
    if lse is not None:
        lse[key_rows, :] = log_sums


def column_pair(table, rows, pair):
    return jnp.concatenate(
        [table[rows, 2 * pair : 2 * pair + 1], table[rows, 2 * pair + 1 : 2 * pair + 2]], axis=0
    )


def head_columns(table, pair):
    lanes = lax.broadcasted_iota(jnp.int32, table.shape, 1)
    parts = [jnp.where(lanes == 2 * pair + head, table, 0.0) for head in range(2)]
    return jnp.concatenate([jnp.sum(part, axis=1, keepdims=True) for part in parts], axis=0)


def head_products(left, right):
    value = left.astype(f32) * right.astype(f32)
    low = lax.broadcasted_iota(jnp.int32, value.shape, 1) < HD
    parts = [jnp.where(low, value, 0.0), jnp.where(low, 0.0, value)]
    return jnp.concatenate([jnp.sum(part, axis=1, keepdims=True) for part in parts], axis=0)


def attend_back_pair(q, k, v, g, lse, delta, gq, gk_t, gv_t, rows, keys, bias, size, cols):
    low = lax.broadcasted_iota(jnp.int32, (size, 128), 1) < HD
    q_two = both_heads(q[rows, cols], low)
    g_two = both_heads(g[rows, cols], low)
    k_pair, v_pair = k[keys, cols], v[keys, cols]
    probs = jnp.exp2(dot(q_two, k_pair, NT) * SCORE + twice(bias) - lse)
    grad_s = (probs * (dot(g_two, v_pair, NT) - delta)).astype(bf16)
    gv_t[cols, keys] += dot(g_two, probs.astype(bf16), TN)
    gk_t[cols, keys] += dot(q_two, grad_s, TN)
    d = dot(grad_s, k_pair, NN)
    gq[rows, cols] = (jnp.where(low, d[:size], d[size:]) * SCALING).astype(bf16)


def attend_back_block(
    q, k, v, g, lse, delta, gq, gk_t, gv_t, rows, keys, bias, size, after=None
):
    for pair in range(HEADS // 2):
        attend_back_pair(
            q, k, v, g, column_pair(lse, rows, pair), column_pair(delta, rows, pair),
            gq, gk_t, gv_t, rows, keys, bias, size, pl.ds(128 * pair, 128),
        )
        if after is not None:
            after()


def head_sums(value):
    rows = value.shape[0]
    lanes = lax.broadcasted_iota(jnp.int32, (rows, 128), 1)
    low = lanes < HD
    result = jnp.zeros((rows, 128), f32)
    for pair in range(HEADS // 2):
        part = value[:, 128 * pair : 128 * pair + 128]
        first = jnp.sum(jnp.where(low, part, 0.0), axis=1, keepdims=True)
        second = jnp.sum(jnp.where(low, 0.0, part), axis=1, keepdims=True)
        result = jnp.where(lanes == 2 * pair, first, result)
        result = jnp.where(lanes == 2 * pair + 1, second, result)
    return result


def blocks(total, size, body):
    def step(i, carry):
        body(pl.ds(pl.multiple_of(i * size, size), size))
        return carry

    lax.fori_loop(0, total // size, step, 0)


def normalise(value):
    average = jnp.mean(value, axis=1, keepdims=True)
    centred = value - average
    scale = lax.rsqrt(jnp.mean(centred * centred, axis=1, keepdims=True) + EPSILON)
    return centred * scale, scale


def normalise_back(grad, gain, hat, scale):
    g = grad * gain
    first = jnp.mean(g, axis=1, keepdims=True)
    second = jnp.mean(g * hat, axis=1, keepdims=True)
    return scale * (g - first - hat * second)


def column_sum(value):
    return jnp.sum(value, axis=0, keepdims=True)


def mat(ref):
    value = ref[...]
    return value if value.ndim == 2 else value.reshape(-1, value.shape[-1])


def up_part(win, j):
    if len(win.shape) == 2:
        return win[512 * j : 512 * j + 512, :]
    depth = len(win.shape) - 2
    lead = depth - int(math.log2(512 // win.shape[-2]))
    part = win[tuple((j >> (lead - 1 - i)) & 1 for i in range(lead))]
    return part.reshape(512, part.shape[-1])


def down_part(wout, j):
    if len(wout.shape) == 2:
        return wout[:, 512 * j : 512 * j + 512]
    part = wout[(slice(None),) * (len(wout.shape) - 1) + (slice(512 * j, 512 * j + 512),)]
    return part.reshape(-1, 512)


def prepare_kernel(
    x, t, mem, seg_c, seg_r, key_c, key_r, want_c, lang, wq, wk, wv, wck, wcv, small,
    h, q, k, v, ck, cv,
):
    length = x.shape[0]

    def glanced(rows):
        same = seg_c[rows, :] == seg_r[...]
        doc_length = jnp.sum(same.astype(f32), axis=1, keepdims=True)
        ahead = jnp.logical_and(same, key_r[...] > key_c[rows, :])
        rank = jnp.sum(ahead.astype(f32), axis=1, keepdims=True)
        wanted = jnp.minimum(want_c[rows, :], doc_length.astype(jnp.int32))
        count = lax.shift_right_logical(wanted + 1, jnp.int32(1))
        glance = rank < count.astype(f32)
        plain = x[rows, :].astype(f32)
        h[0, rows, :] = plain + lang[...]
        h[1, rows, :] = jnp.where(glance, t[rows, :].astype(f32), plain) + lang[...]

    blocks(length, 128, glanced)

    def cross(rows):
        m = mem[rows, :]
        ck[rows, :] = dot(m, wck[...], NT).astype(bf16)
        cv[rows, :] = (dot(m, wcv[...], NT) + small[4:5, :]).astype(bf16)

    blocks(mem.shape[0], 512, cross)
    for which in range(2):

        def project(rows):
            low = h[which, rows, :].astype(bf16)
            q[which, rows, :] = (dot(low, wq[...], NT) + small[0:1, :]).astype(bf16)
            k[which, rows, :] = dot(low, wk[...], NT).astype(bf16)
            v[which, rows, :] = (dot(low, wv[...], NT) + small[1:2, :]).astype(bf16)

        blocks(length, 512, project)


def windows(length):
    return [w for w in (256, 384, 512, 640) if w < length] + [length]


def windowed(starts, needs, i, length, body):
    need, begin = needs[i], starts[i]
    sizes = windows(length)
    for at, size in enumerate(sizes):
        fits = need <= size
        if at > 0:
            fits = jnp.logical_and(fits, need > sizes[at - 1])

        @pl.when(fits)
        def _():
            start = pl.multiple_of(jnp.minimum(begin, length - size), 128)
            body(pl.ds(start, size))


def self_kernel(starts, needs, q, k, v, seg_c, seg_r, ctx, lse):
    length = q.shape[1]
    size = 128

    def step(i, carry):
        rows = pl.ds(pl.multiple_of(i * size, size), size)

        def body(keys):
            bias = jnp.where(seg_c[rows, :] == seg_r[:, keys], 0.0, MASKED)
            for which in range(2):
                attend_block(
                    q.at[which], k.at[which], v.at[which], ctx.at[which],
                    lse if which == 1 else None, rows, rows, keys, bias, size,
                )

        windowed(starts, needs, i, length, body)
        return carry

    lax.fori_loop(0, length // size, step, 0)


def after_self(ctx, h, wso, wcq, small, a, cq, rows):
    r1 = h + dot(ctx, mat(wso), NT) + small[2:3, :]
    hat, scale = normalise(r1)
    value = hat * small[10:11, :] + small[7:8, :]
    if a is not None:
        a[rows, :] = value
    low = value.astype(bf16)
    cq[rows, :] = (dot(low, mat(wcq), NT) + small[3:4, :]).astype(bf16)
    return hat, scale, low


def after_cross(a, ctx2, wco, win, wout, small, hidden_bias, hid, slope):
    r2 = a + dot(ctx2, mat(wco), NT) + small[5:6, :]
    hat2, scale2 = normalise(r2)
    b = hat2 * small[11:12, :] + small[8:9, :]
    low = b.astype(bf16)
    total = b + small[6:7, :]
    for j in range(hidden_bias.shape[1] // 512):
        cols = pl.ds(512 * j, 512)
        z = dot(low, up_part(win, j), NT) + hidden_bias[:, cols]
        half = 0.5 + 0.5 * lax.erf(z * 0.7071067811865476)
        hidden = (z * half).astype(bf16)
        if hid is not None:
            hid[:, cols] = hidden
            bell = jnp.exp2(z * z * (-0.5 * LOG2E)) * 0.3989422804014327
            slope[:, cols] = half + z * bell
        total = total + dot(hidden, down_part(wout, j), NT)
    hat3, scale3 = normalise(total)
    y = hat3 * small[12:13, :] + small[9:10, :]
    return y, (hat2, scale2, low, hat3, scale3)


def first_kernel(
    h, ctx, ck, cv, source_bias, wso, wcq, wco, win, wout, small, hidden_bias,
    out, a, cq, ctx2,
):
    length = h.shape[1]

    def before(rows):
        after_self(ctx[0, rows, :], h[0, rows, :], wso, wcq, small, a, cq, rows)

    blocks(length, 512, before)
    every = pl.ds(0, ck.shape[0])
    blocks(
        length,
        256,
        lambda rows: attend_block(cq, ck, cv, ctx2, None, rows, rows, every, source_bias[...], 256),
    )

    def last(rows):
        y, _ = after_cross(
            a[rows, :], ctx2[rows, :], wco, win, wout, small, hidden_bias, None, None
        )
        out[rows, :] = y.astype(bf16)

    blocks(length, 512, last)


def layer_kernel(
    h, ctx, ck, cv, mem, cot, live, source_bias,
    wso, wcq, wck, wcv, wco, win, wout, small, hidden_bias,
    out, gr1, gctx, g_mem,
    g_so, g_cq, g_ck, g_cv, g_co, g_in, g_out, g_small, g_hidden,
    cq, ctx2, lse2, hat1, scale1, low1, hid, slope, delta, gcq, gk_low, gv_low, low2, hat2s,
):
    length = h.shape[1]
    big = 512
    a, gctx2 = gr1, gctx
    for ref in (g_so, g_cq, g_co, g_in, g_out, g_small, g_hidden):
        ref[...] = jnp.zeros_like(ref)

    def before(rows):
        hat, scale, low = after_self(ctx[0, rows, :], h[0, rows, :], wso, wcq, small, a, cq, rows)
        hat1[rows, :] = hat
        scale1[rows, :] = scale
        low1[rows, :] = low

    blocks(length, big, before)
    every = pl.ds(0, ck.shape[0])
    blocks(
        length,
        256,
        lambda rows: attend_block(cq, ck, cv, ctx2, lse2, rows, rows, every, source_bias[...], 256),
    )

    def turn(rows):
        y, (hat2, scale2, low, hat3, scale3) = after_cross(
            a[rows, :], ctx2[rows, :], wco, win, wout, small, hidden_bias, hid, slope
        )
        out[rows, :] = y.astype(bf16)
        low2[...] = low
        hat2s[...] = hat2
        gy = cot[rows, :].astype(f32) * live[rows, :]
        g_small[12:13, :] += column_sum(gy * hat3)
        g_small[9:10, :] += column_sum(gy)
        gr3 = normalise_back(gy, small[12:13, :], hat3, scale3)
        gf = gr3.astype(bf16)
        g_small[6:7, :] += column_sum(gf.astype(f32))
        gb = gr3
        for j in range(win.shape[0] // 512):
            cols = pl.ds(512 * j, 512)
            gz = (dot(gf, wout[:, cols], NN) * slope[:, cols]).astype(bf16)
            g_out[:, cols] += dot(gf, hid[:, cols], TN)
            g_in[cols, :] += dot(gz, low2[...], TN)
            g_hidden[:, cols] += column_sum(gz.astype(f32))
            gb = gb + dot(gz, win[cols, :], NN)
        hat2 = hat2s[...]
        g_small[11:12, :] += column_sum(gb * hat2)
        g_small[8:9, :] += column_sum(gb)
        gr2 = normalise_back(gb, small[11:12, :], hat2, scale2)
        a[rows, :] = gr2
        go2 = gr2.astype(bf16)
        g_small[5:6, :] += column_sum(go2.astype(f32))
        context = ctx2[rows, :]
        g_co[...] += dot(go2, context, TN)
        back = dot(go2, wco[...], NN).astype(bf16)
        gctx2[rows, :] = back
        delta[rows, :] = head_sums(back.astype(f32) * context.astype(f32))

    blocks(length, big, turn)
    gk_t, gv_t = slope.at[:, pl.ds(0, ck.shape[0])], slope.at[:, pl.ds(ck.shape[0], ck.shape[0])]
    slope[...] = jnp.zeros_like(slope)
    blocks(
        length,
        256,
        lambda rows: attend_back_block(
            cq, ck, cv, gctx2, lse2, delta, gcq, gk_t, gv_t, rows, every, source_bias[...], 256
        ),
    )
    gk_low[...] = (gk_t[...] * SCALING).astype(bf16)
    gv_low[...] = gv_t[...].astype(bf16)
    g_ck[...] = dot(gk_low[...], mem[...], NN)
    g_cv[...] = dot(gv_low[...], mem[...], NN)
    ones = jnp.ones((8, mem.shape[0]), bf16)
    g_small[4:5, :] = dot(ones, gv_low[...], NT)[0:1, :]
    for at in range(0, mem.shape[0], 512):
        cols = pl.ds(at, 512)
        g_mem[cols, :] = dot(gk_low[:, cols], wck[...], TN) + dot(gv_low[:, cols], wcv[...], TN)

    def final(rows):
        gq = gcq[rows, :]
        g_small[3:4, :] += column_sum(gq.astype(f32))
        g_cq[...] += dot(gq, low1[rows, :], TN)
        ga = a[rows, :] + dot(gq, wcq[...], NN)
        hat = hat1[rows, :]
        g_small[10:11, :] += column_sum(ga * hat)
        g_small[7:8, :] += column_sum(ga)
        g1 = normalise_back(ga, small[10:11, :], hat, scale1[rows, :])
        gr1[rows, :] = g1
        go = g1.astype(bf16)
        g_small[2:3, :] += column_sum(go.astype(f32))
        g_so[...] += dot(go, ctx[0, rows, :], TN)
        gctx[rows, :] = dot(go, wso[...], NN).astype(bf16)

    blocks(length, big, final)


def self_back_kernel(
    starts, needs, live_blocks, q, k, v, g, ctx, lse, seg_c, seg_r,
    gq, gk_low, gv_low, delta, gk_t, gv_t,
):
    length = q.shape[1]
    size = 128
    gk_t[...] = jnp.zeros_like(gk_t)
    gv_t[...] = jnp.zeros_like(gv_t)
    gq[...] = jnp.zeros_like(gq)

    def step(i, carry):
        rows = pl.ds(pl.multiple_of(i * size, size), size)
        delta[rows, :] = head_sums(g[rows, :].astype(f32) * ctx[0, rows, :].astype(f32))

        def body(keys):
            bias = jnp.where(seg_c[rows, :] == seg_r[:, keys], 0.0, MASKED)
            attend_back_block(
                q.at[0], k.at[0], v.at[0], g, lse, delta, gq, gk_t, gv_t, rows, keys, bias, size
            )

        windowed(starts, needs, i, length, body)
        return carry

    lax.fori_loop(0, live_blocks[0], step, 0)
    gk_low[...] = (gk_t[...] * SCALING).astype(bf16)
    gv_low[...] = gv_t[...].astype(bf16)


def input_kernel(h, gq, gk_low, gv_low, gr1, wq, wk, wv, g_x, g_q, g_k, g_v, sums):
    length = h.shape[1]
    g_q[...] = jnp.zeros_like(g_q)
    g_k[...] = jnp.zeros_like(g_k)
    g_v[...] = jnp.zeros_like(g_v)
    sums[...] = jnp.zeros_like(sums)
    ones = jnp.ones((8, 512), bf16)

    for at in range(0, length, 512):
        rows = pl.ds(at, 512)
        low = h[0, rows, :].astype(bf16)
        part = gq[rows, :]
        g_q[...] += dot(part, low, TN)
        g_k[...] += dot(gk_low[:, rows], low, NN)
        g_v[...] += dot(gv_low[:, rows], low, NN)
        value = gr1[rows, :] + dot(part, wq[...], NN)
        value = value + dot(gk_low[:, rows], wk[...], TN) + dot(gv_low[:, rows], wv[...], TN)
        g_x[rows, :] = value
        sums[0:1, :] += column_sum(part.astype(f32))
        sums[1:2, :] += dot(ones, gv_low[:, rows], NT)[0:1, :]
        sums[2:3, :] += column_sum(value)


def shape(dims, dtype=f32):
    return jax.ShapeDtypeStruct(dims, dtype)


def call(kernel, name, outs, args, scratch=(), scalars=0, specs=None):
    in_specs = [pl.BlockSpec(memory_space=pltpu.SMEM)] * scalars
    for at in range(scalars, len(args)):
        in_specs.append((specs or {}).get(at) or pl.BlockSpec(memory_space=VMEM))
    return pl.pallas_call(
        kernel,
        out_shape=outs,
        in_specs=in_specs,
        out_specs=[pl.BlockSpec(memory_space=VMEM)] * len(outs),
        scratch_shapes=list(scratch),
        name=name,
        compiler_params=pltpu.CompilerParams(vmem_limit_bytes=61 * 2**20),
    )(*args)


def shards_apart(
    n,
    x_copy,
    target_embed,
    memory,
    cotangent,
    segment_ids,
    source_lengths,
    target_lengths,
    hamming,
    priority,
    lang_tag,
    w_self_qkv,
    w_self_out,
    w_cross_q,
    w_cross_kv,
    w_cross_out,
    w_in,
    w_out,
    biases,
    gains,
    b_hidden,
    lang_table,
):
    length, width = x_copy.shape[1:]
    source = memory.shape[1]
    hidden = b_hidden.shape[0] * n
    share = width // n
    fold = hidden // width
    langs = lang_table.shape[0]
    slots = hamming.shape[1]

    table = jnp.concatenate([biases, gains, lang_table, b_hidden.reshape(fold, share)], axis=0)
    kept = table.shape[0]
    table = jnp.pad(table, ((0, 128 - kept), (0, 0)))
    gathered = gather_all(
        n,
        [
            table.T,
            w_cross_kv[0].T,
            w_cross_kv[1].T,
            w_self_qkv[0].T,
            w_self_qkv[1].T,
            w_self_qkv[2].T,
            w_self_out.T,
            w_cross_q.T,
            w_cross_out.T,
            w_in.T,
            w_out.T,
        ],
        0,
    )
    small_t, wck, wcv, wq, wk, wv, wso, wcq, wco, win, wout = gathered
    small = small_t.T.astype(f32)
    first_lang = BIASES + GAINS
    hidden_bias = small[first_lang + langs : first_lang + langs + fold]
    hidden_bias = hidden_bias.reshape(fold, n, share).transpose(1, 0, 2).reshape(1, hidden)
    lang = lax.dynamic_slice_in_dim(small, first_lang + lang_tag[0], 1, 0)
    small = small[:16]

    target_len = target_lengths[0]
    position = jnp.arange(length, dtype=jnp.int32)
    live = position < target_len
    seg = jnp.where(live, segment_ids[0], slots).astype(jnp.int32)
    wanted = jnp.sum(
        jnp.where(seg[:, None] == jnp.arange(slots, dtype=jnp.int32)[None, :], hamming[0][None, :], 0),
        axis=1,
        keepdims=True,
    )
    key = priority[0] * length + (length - 1 - position)
    same_edge = seg.reshape(length // 128, 128)
    first_seg, last_seg = same_edge[:, 0], same_edge[:, -1]
    begin = jnp.sum((seg[None, :] < first_seg[:, None]).astype(jnp.int32), axis=1)
    end = jnp.sum((seg[None, :] <= last_seg[:, None]).astype(jnp.int32), axis=1)
    starts = begin // 128 * 128
    needs = (end + 127) // 128 * 128 - starts
    live_blocks = ((target_len + 127) // 128).reshape(1)
    seg_c, seg_r = seg[:, None], seg[None, :]
    source_bias = jnp.where(
        jnp.arange(source, dtype=jnp.int32) < source_lengths[0], 0.0, MASKED
    ).astype(f32)[None, :]

    mem = memory[0]
    two = (2, length, width)
    h, q, k, v, ck, cv = call(
        prepare_kernel,
        "prepare",
        [shape(two), shape(two, bf16), shape(two, bf16), shape(two, bf16)]
        + [shape((source, width), bf16)] * 2,
        (
            x_copy[0], target_embed[0], mem, seg_c, seg_r, key[:, None], key[None, :], wanted,
            lang, wq, wk, wv, wck, wcv, small,
        ),
    )
    ctx, lse = call(
        self_kernel,
        "self_attention",
        [shape(two, bf16), shape((length, 128))],
        (starts, needs, q, k, v, seg_c, seg_r),
        scalars=2,
    )

    def part(dims, which):
        block = (1,) + dims[1:]
        return pl.BlockSpec(block, lambda i: (which, 0, 0))

    def one(value, which):
        return lax.slice_in_dim(value, which, which + 1, axis=0)

    flat = (length, width)
    (first,) = call(
        first_kernel,
        "first_pass",
        [shape(flat, bf16)],
        (one(h, 0), one(ctx, 0), ck, cv, source_bias, wso, wcq, wco, win, wout, small, hidden_bias),
        scratch=[VMEM(flat, f32), VMEM(flat, bf16), VMEM(flat, bf16)],
    )
    square = shape((width, width))
    h2, ctx_two = one(h, 1), one(ctx, 1)
    big = 512
    (
        final, gr1, gctx, g_mem, g_so, g_cq, g_ck, g_cv, g_co, g_in, g_out, g_small, g_hidden,
    ) = call(
        layer_kernel,
        "second_pass",
        [shape(flat, bf16), shape(flat), shape(flat, bf16), shape((source, width))]
        + [square] * 5
        + [shape((hidden, width)), shape((width, hidden)), shape((16, width)), shape((1, hidden))],
        (
            h2, ctx_two, ck, cv, mem, cotangent[0], live[:, None].astype(f32), source_bias,
            wso, wcq, wck, wcv, wco, win, wout, small, hidden_bias,
        ),
        scratch=[
            VMEM(flat, bf16), VMEM(flat, bf16), VMEM((length, 128), f32),
            VMEM(flat, f32), VMEM((length, 1), f32), VMEM(flat, bf16),
            VMEM((big, hidden), bf16), VMEM((width, max(hidden, 2 * source)), f32),
            VMEM((length, 128), f32), VMEM(flat, bf16),
            VMEM((width, source), bf16), VMEM((width, source), bf16),
            VMEM((big, width), bf16), VMEM((big, width), f32),
        ],
    )
    gq, gk_low, gv_low = call(
        self_back_kernel,
        "self_attention_back",
        [shape(flat, bf16), shape((width, length), bf16), shape((width, length), bf16)],
        (starts, needs, live_blocks, one(q, 1), one(k, 1), one(v, 1), gctx, ctx_two, lse, seg_c, seg_r),
        scratch=[VMEM((length, 128), f32), VMEM((width, length), f32), VMEM((width, length), f32)],
        scalars=3,
    )
    g_x, g_q, g_k, g_v, sums = call(
        input_kernel,
        "input_gradient",
        [shape(flat), square, square, square, shape((8, width))],
        (h2, gq, gk_low, gv_low, gr1, wq, wk, wv),
    )

    tag = jnp.arange(langs, dtype=jnp.int32) == lang_tag[0]
    g_lang = jnp.where(tag[:, None], sums[2:3], 0.0)
    g_fold = g_hidden.reshape(n, fold, share).transpose(1, 0, 2).reshape(fold, width)
    g_table = jnp.concatenate([sums[0:2], g_small[2:13], g_lang, g_fold], axis=0)
    g_table = jnp.pad(g_table, ((0, 128 - kept), (0, 0))).T
    owned = scatter_all(n, [g_in, g_out, g_co, g_ck, g_cv, g_cq, g_so, g_q, g_k, g_v, g_table], 1)
    o_in, o_out, o_co, o_ck, o_cv, o_cq, o_so, o_q, o_k, o_v, o_table = owned
    o_table = o_table.T
    return (
        first[None],
        final[None],
        g_x[None],
        g_mem[None],
        jnp.stack([o_q.T, o_k.T, o_v.T]),
        o_so.T,
        o_cq.T,
        jnp.stack([o_ck.T, o_cv.T]),
        o_co.T,
        o_in.T,
        o_out.T,
        o_table[:BIASES],
        o_table[BIASES:first_lang],
        o_table[first_lang + langs : kept].reshape(hidden // n),
        o_table[first_lang : first_lang + langs],
    )


def add_to(ref, index, value, fresh):
    ref[index] = value if fresh else ref[index] + value


class Copies:
    def __init__(self, semaphores):
        self.semaphores, self.pending, self.count = semaphores, {}, 0

    def start(self, source, target):
        copy = pltpu.make_async_copy(source, target, self.semaphores.at[self.count])
        copy.start()
        self.pending[self.count] = copy
        self.count += 1
        return self.count - 1

    def wait(self, *which):
        for at in which:
            if at in self.pending:
                self.pending.pop(at).wait()

    def wait_all(self):
        self.wait(*list(self.pending))


def column(row, rows):
    size = 128
    down = lax.broadcasted_iota(jnp.int32, (size, size), 0)
    across = lax.broadcasted_iota(jnp.int32, (size, size), 1)
    return jnp.sum(jnp.where(down == across, row[:, rows], 0.0), axis=1, keepdims=True)


def placed(height, offset):
    down = lax.broadcasted_iota(jnp.int32, (height, 128), 0)
    across = lax.broadcasted_iota(jnp.int32, (height, 128), 1)
    return (across == down + offset).astype(bf16)


def apart(body):
    once = jnp.minimum(lax.axis_index("dp") + 1, 1)

    def step(i, carry):
        body()
        return carry

    lax.fori_loop(0, once, step, 0)


def source_row(source_len, count):
    position = lax.broadcasted_iota(jnp.int32, (1, count), 1)
    return jnp.where(position < source_len[0], 0.0, MASKED)


def forward_kernel(
    depth, most, fewest, target_len, tag, hamming, source_len,
    raw, priority, biases, gains, lang_t, w_in, b_mid,
    x_ref, t_ref, mem_ref, qkv_t, ckv_t, so_t, cq_t, co_t, out_t,
    small, seg_c, seg_r, hidden_bias, scale1,
    a1_ref, ctxb1_ref, hat1_ref, low2_ref, q2_ref, k2_ref, v2_ref, lse_ref, ctx2_ref, ck_ref, cv_ref, cq_ref,
    ctxb_ref, lse_cross_ref,
    wq_ref, wk_ref, wv_ref, wck_ref, wcv_ref, wso_ref, wcq_ref, wco_ref, win_ref, wout_ref,
    x, t, mem, small_t, mids, wq, wk, wv, wck, wcv, wso, wcq, wco, win, wout,
    h1, h2, low1, low2, q1, k1, v1, q2, k2, v2, lse, ctx1, ctx2, ck, cv, a1, hat1, cq1, cq,
    ctxb1, ctxb, lse_cross, glance, send, recv, local,
):
    length, count = x.shape[0], mem.shape[0]
    slots, langs = hamming.shape[1], lang_t.shape[1]
    every = (slice(None), slice(None))
    buffers = [small_t, wq, wk, wv, wck, wcv, wso, wcq, mids, wco, win, wout]
    pieces = [(i,) + every for i in range(10)]
    pieces += [(10, pl.ds(at, 32), slice(None)) for at in range(0, w_in.shape[1], 32)]
    pieces += [(11, slice(None), pl.ds(at, 512)) for at in range(0, out_t.shape[1], 512)]
    gather = Gather(depth, buffers, pieces, send, recv)
    copies = Copies(local)
    shares = [qkv_t.at[0], qkv_t.at[1], qkv_t.at[2], ckv_t.at[0], ckv_t.at[1], so_t, cq_t]
    owned = [copies.start(share, gather.own(i + 1)) for i, share in enumerate(shares)]
    owned += [copies.start(co_t, gather.own(9)), copies.start(out_t, gather.own(11))]
    rows_in = [copies.start(a, b) for a, b in ((x_ref, x), (t_ref, t), (mem_ref, mem))]
    table = dot(biases[...], placed(BIASES, langs), TN)
    table = table + dot(gains[...], placed(GAINS, langs + BIASES), TN)
    table = table + dot(lang_t[...], placed(langs, 0), NN)
    small_t[tuple(gather.bits)] = table.astype(bf16)
    win[tuple(gather.bits)] = w_in[...].astype(f32).T.astype(bf16)
    mids[tuple(gather.bits)] = jnp.broadcast_to(b_mid[...], mids.shape[-2:])
    gather.enter()
    gather.tick()
    copies.wait(*owned)
    gather.tick()

    position = lax.broadcasted_iota(jnp.int32, (1, length), 1)
    segments = jnp.where(position < target_len[0], raw[...], slots).astype(f32)
    seg_r[...] = segments
    rank_key = priority[...].astype(f32)
    place = position.astype(f32)

    def glanced(at):
        rows = pl.ds(at, 128)
        seg = column(segments, slice(at, at + 128))
        key = column(rank_key, slice(at, at + 128))
        here = (lax.broadcasted_iota(jnp.int32, (128, 1), 0) + at).astype(f32)
        seg_c[rows, :] = seg
        same = segments == seg
        doc_length = jnp.sum(same.astype(f32), axis=1, keepdims=True)
        ahead = (rank_key > key) | ((rank_key == key) & (place < here))
        rank = jnp.sum((same & ahead).astype(f32), axis=1, keepdims=True)
        wanted = jnp.zeros((128, 1), f32)
        for slot in range(slots):
            wanted = jnp.where(seg == float(slot), hamming[0, slot].astype(f32), wanted)
        glance[rows, :] = (2.0 * rank + 1.0 <= jnp.minimum(wanted, doc_length)).astype(f32)

    for at in range(0, length, 128):
        glanced(at)
        if at % 512 == 384:
            gather.tick()
    gather.need(1)
    items = mat(small_t)
    small[...] = dot(placed(16, langs), items, NT)
    choice = lax.broadcasted_iota(jnp.int32, (8, 128), 1) == tag[0]
    lang = dot(choice.astype(bf16), items, NT)[0:1, :]
    copies.wait(*rows_in)

    def combine(rows):
        plain = x[rows, :].astype(f32)
        one = plain + lang
        two = jnp.where(glance[rows, :] > 0.5, t[rows, :].astype(f32), plain) + lang
        h1[rows, :] = one
        h2[rows, :] = two
        low1[rows, :] = one.astype(bf16)
        low2[rows, :] = two.astype(bf16)

    blocks(length, 256, combine)
    copies.start(low2, low2_ref)

    def project(source, weight, bias, out):
        def step(rows):
            value = dot(source[rows, :], mat(weight), NT)
            if bias is not None:
                value = value + small[bias : bias + 1, :]
            out[rows, :] = value.astype(bf16)

        blocks(source.shape[0], 512, step)

    for at, (weight, bias, one, two) in enumerate(
        [(wq, 0, q1, q2), (wk, None, k1, k2), (wv, 1, v1, v2)]
    ):
        gather.need(2 + at)
        project(low1, weight, bias, one)
        project(low2, weight, bias, two)
    for source, target in ((q2, q2_ref), (k2, k2_ref), (v2, v2_ref)):
        copies.start(source, target)

    pause = gather.tick
    for q, k, v, ctx, log_sums in ((q1, k1, v1, ctx1, None), (q2, k2, v2, ctx2, lse)):
        for at in range(0, length, 256):

            def one_block():
                begin, end = max(0, at - most + 1), min(length, at + 256 + most - 1)
                if at + 256 > fewest:
                    begin, end = min(begin, fewest), length
                begin, end = begin // 128 * 128, (end + 127) // 128 * 128
                rows, keys = pl.ds(at, 256), pl.ds(begin, end - begin)
                masked = jnp.where(seg_c[rows, :] == seg_r[:, keys], 0.0, MASKED)
                attend_block(q, k, v, ctx, log_sums, rows, rows, keys, masked, 256)

            apart(one_block)
            pause()
    copies.start(ctx2, ctx2_ref)
    copies.start(lse, lse_ref)
    gather.need(8)
    project(mem, wck, None, ck)
    project(mem, wcv, 4, cv)
    copies.start(ck, ck_ref)
    copies.start(cv, cv_ref)
    pause()

    def start_one(rows):
        after_self(ctx1[rows, :], h1[rows, :], wso, wcq, small, a1, cq1, rows)

    def start_two(rows):
        hat, scale, _ = after_self(ctx2[rows, :], h2[rows, :], wso, wcq, small, None, cq, rows)
        hat1[rows, :] = hat
        scale1[rows, :] = scale

    blocks(length, 512, start_one)
    copies.start(a1, a1_ref)
    pause()
    blocks(length, 512, start_two)
    copies.start(hat1, hat1_ref)
    copies.start(cq, cq_ref)
    pause()
    every_key = pl.ds(0, count)
    source_bias = source_row(source_len, count)
    for query, context, log_sums in ((cq, ctxb, lse_cross), (cq1, ctxb1, None)):
        for at in range(0, length, 256):

            def one_block():
                rows = pl.ds(at, 256)
                attend_block(
                    query, ck, cv, context, log_sums, rows, rows, every_key, source_bias, 256
                )

            apart(one_block)
            if log_sums is not None:
                pause()
            elif at == 0:
                gather.finish()
                for source, target in (
                    (wq, wq_ref), (wk, wk_ref), (wv, wv_ref), (wck, wck_ref), (wcv, wcv_ref),
                    (wso, wso_ref), (wcq, wcq_ref), (wco, wco_ref), (win, win_ref),
                    (wout, wout_ref),
                ):
                    copies.start(source, target)
        if log_sums is not None:
            copies.start(ctxb, ctxb_ref)
            copies.start(lse_cross, lse_cross_ref)
    copies.start(ctxb1, ctxb1_ref)
    for i in range(2**depth):
        owner = mids.at[tuple((i >> (depth - 1 - j)) & 1 for j in range(depth))]
        hidden_bias[:, 128 * i : 128 * i + 128] = owner[0:1, :].astype(f32)
    copies.wait_all()


def turn_kernel(
    depth, slots, source_len,
    scale1, seg_c, small, hidden_bias,
    hat1_ref, ctxb_ref, wco_ref, win_ref, wout_ref, cot_ref,
    cq_ref, ck_ref, cv_ref, lse_ref, mem_ref, wck_ref, wcv_ref, wcq_ref, wso_ref, ctx_ref,
    gr1, gctx, g_so, g_cq, g_ck, g_cv, g_small, g_hidden, o_in, o_out, o_co, out_ref, g_mem_ref,
    hat1, ctxb, wco, win, wout, cq, ck, cv, lse, mem, wck, wcv, wcq, wso, ctx,
    g_in, g_out, g_co, hid, slope, delta, gcq, low2, hat2s, *rest,
):
    length, count = cq.shape[0], ck.shape[0]
    big = 512
    send, recv, local = rest[-3:]
    kinds = itertools.count()
    units = (
        units_of(g_out, g_out.shape[0] >> depth, o_out, g_out.shape[1], kinds)
        + units_of(g_in, g_in.shape[0] >> depth, o_in, g_in.shape[1], kinds)
        + units_of(g_co, g_co.shape[0] >> depth, o_co, g_co.shape[1], kinds)
    )
    downs = g_out.shape[1] // 512
    scatter = Scatter(depth, units, rest[:-3], send, recv)
    agenda = Agenda()
    copies = Copies(local)
    pairs = [
        (hat1_ref, hat1), (ctxb_ref, ctxb), (wco_ref, wco), (win_ref, win), (wout_ref, wout),
        (cot_ref, gctx),
        (cq_ref, cq), (ck_ref, ck), (cv_ref, cv), (lse_ref, lse),
        (mem_ref, mem), (wck_ref, wck), (wcv_ref, wcv), (wcq_ref, wcq), (wso_ref, wso), (ctx_ref, ctx),
    ]
    fetched = [copies.start(source, target) for source, target in pairs]
    for ref in (g_small, g_hidden):
        ref[...] = jnp.zeros_like(ref)
    scatter.enter()
    copies.wait(*fetched[:3])

    out = gcq
    for at in range(0, length, big):
        rows = pl.ds(at, big)
        final = at + big == length
        a = hat1[rows, :] * small[10:11, :] + small[7:8, :]
        copies.wait(*fetched[3:6])
        y, (hat2, scale2, low, hat3, scale3) = after_cross(
            a, ctxb[rows, :], wco, win, wout, small, hidden_bias, hid, slope
        )
        out[rows, :] = y.astype(bf16)
        low2[...] = low
        hat2s[...] = hat2
        live = (seg_c[rows, :] < slots - 0.5).astype(f32)
        gy = gctx[rows, :].astype(f32) * live
        g_small[12:13, :] += column_sum(gy * hat3)
        g_small[9:10, :] += column_sum(gy)
        gr3 = normalise_back(gy, small[12:13, :], hat3, scale3)
        gf = gr3.astype(bf16)
        g_small[6:7, :] += column_sum(gf.astype(f32))
        gb = gr3
        for j in range(downs):
            cols = pl.ds(512 * j, 512)
            gz = (dot(gf, down_part(wout, j), NN) * slope[:, cols]).astype(bf16)
            add_to(g_out, (slice(None), cols), dot(gf, hid[:, cols], TN), at == 0)
            add_to(g_in, (cols, slice(None)), dot(gz, low2[...], TN), at == 0)
            g_hidden[:, cols] += column_sum(gz.astype(f32))
            gb = gb + dot(gz, up_part(win, j), NN)
            if final and j % 2 == 1:
                agenda.round(*[scatter.flow(i) for i in range(j // 2, j)])
        hat2 = hat2s[...]
        g_small[11:12, :] += column_sum(gb * hat2)
        g_small[8:9, :] += column_sum(gb)
        gr2 = normalise_back(gb, small[11:12, :], hat2, scale2)
        gr1[rows, :] = gr2
        go2 = gr2.astype(bf16)
        g_small[5:6, :] += column_sum(go2.astype(f32))
        context = ctxb[rows, :]
        add_to(g_co, ..., dot(go2, context, TN), at == 0)
        back = dot(go2, mat(wco), NN).astype(bf16)
        gctx[rows, :] = back
        delta[rows, :] = head_sums(back.astype(f32) * context.astype(f32))

    keep_out = copies.start(out, out_ref)
    waiting = list(range(downs - 1, len(units)))

    def onward(count):
        fresh = waiting[:count]
        del waiting[:count]
        agenda.round(*[scatter.flow(which) for which in fresh])

    onward(2)
    gk_t, gv_t = slope.at[:, pl.ds(0, count)], slope.at[:, pl.ds(count, count)]
    slope[...] = jnp.zeros_like(slope)
    copies.wait(keep_out, *fetched[6:10])
    every = pl.ds(0, count)
    source_bias = source_row(source_len, count)

    for at in range(0, length, 256):
        attend_back_block(
            cq, ck, cv, gctx, lse, delta, gcq, gk_t, gv_t, pl.ds(at, 256), every, source_bias, 256
        )
        onward(2)
    copies.wait(*fetched[10:])
    gk_low, gv_low = hid.at[:, pl.ds(0, count)], hid.at[:, pl.ds(count, count)]
    gk_low[...] = (gk_t[...] * SCALING).astype(bf16)
    gv_low[...] = gv_t[...].astype(bf16)
    g_ck[...] = dot(gk_low[...], mem[...], NN)
    g_cv[...] = dot(gv_low[...], mem[...], NN)
    ones = jnp.ones((8, count), bf16)
    g_small[4:5, :] = dot(ones, gv_low[...], NT)[0:1, :]
    for i, at in enumerate(range(0, count, 512)):
        cols = pl.ds(at, 512)
        place = slope.at[:, pl.ds(512 * i, 512)]
        place[...] = dot(gk_low[:, cols], mat(wck), TN) + dot(gv_low[:, cols], mat(wcv), TN)
        copies.start(place, g_mem_ref.at[cols, :])
    agenda.round()
    for at in range(0, length, big):
        rows = pl.ds(at, big)
        gq = gcq[rows, :]
        hat = hat1[rows, :]
        low = (hat * small[10:11, :] + small[7:8, :]).astype(bf16)
        g_small[3:4, :] += column_sum(gq.astype(f32))
        add_to(g_cq, ..., dot(gq, low, TN), at == 0)
        ga = gr1[rows, :] + dot(gq, mat(wcq), NN)
        g_small[10:11, :] += column_sum(ga * hat)
        g_small[7:8, :] += column_sum(ga)
        g1 = normalise_back(ga, small[10:11, :], hat, scale1[rows, :])
        gr1[rows, :] = g1
        go = g1.astype(bf16)
        g_small[2:3, :] += column_sum(go.astype(f32))
        add_to(g_so, ..., dot(go, ctx[rows, :], TN), at == 0)
        gctx[rows, :] = dot(go, mat(wso), NN).astype(bf16)
        agenda.round()
    while agenda.busy():
        agenda.round()
    scatter.leave()
    copies.wait_all()


def close_kernel(
    depth, most, tag,
    seg_c, seg_r, g_small, g_hidden, small, hidden_bias,
    gctx_ref, ctx_ref, q_ref, k_ref, v_ref, lse_ref, ck_ref, cv_ref, cq_ref, so_ref, low_ref,
    gr1_ref, wq_ref, wk_ref, wv_ref, a1_ref, ctxb1_ref, wco_ref, win_ref, wout_ref,
    g_x, first, o_qkv, o_ckv, o_cq, o_so, o_table, o_late,
    gctx, ctx, q, k, v, lse, g_ck, g_cv, g_cq, g_so, low, wq, wk, wv, a1, ctxb1, wco, win, wout,
    g_q, g_k, g_v, gq, gk_t, gv_t, gk_low, gv_low, lines, table, late, late_low, late_got,
    late_give, late_get, *rest,
):
    length = q.shape[0]
    size = 256
    send, recv, late_send, late_recv, local = rest[-5:]
    kinds = itertools.count()
    width = g_q.shape[0]
    share, devices = width >> depth, 1 << depth
    units = []
    for source, out in [(g_ck, o_ckv.at[0]), (g_cv, o_ckv.at[1]), (g_cq, o_cq), (g_so, o_so)]:
        units += units_of(source, share, out, width, kinds)
    units += units_of(table, share, o_table, table.shape[1], kinds)
    for i, source in enumerate((g_q, g_k, g_v)):
        units += units_of(source, share, o_qkv.at[i], width, kinds, apart=True)
    scatter = Scatter(depth, units, rest[:-5], send, recv)
    agenda, aside = Agenda(), Agenda()
    copies = Copies(local)
    pairs = [
        (gctx_ref, gctx), (ctx_ref, ctx), (q_ref, q), (k_ref, k), (v_ref, v), (lse_ref, lse),
        (ck_ref, g_ck), (cv_ref, g_cv), (cq_ref, g_cq), (so_ref, g_so),
        (low_ref, low), (gr1_ref, g_x), (wq_ref, wq), (wk_ref, wk), (wv_ref, wv),
        (a1_ref, a1), (ctxb1_ref, ctxb1), (wco_ref, wco), (win_ref, win), (wout_ref, wout),
    ]
    fetched = [copies.start(source, target) for source, target in pairs[:10]]
    scatter.enter(range(1, devices))
    for ref in (gk_t, gv_t, lines, table):
        ref[...] = jnp.zeros_like(ref)
    langs = lines.shape[0] // 2
    lines[langs : langs + 16, :] = g_small[...]
    table[:, 0:128] = lines[...].T
    for owner in range(devices):
        table[share * owner : share * owner + 1, 128:256] = g_hidden[:, 128 * owner : 128 * owner + 128]
    copies.wait(*fetched[:8])
    aside.round(scatter.flow(0), scatter.flow(1))
    fetched += [copies.start(source, target) for source, target in pairs[10:]]
    copies.wait(*fetched[8:10])
    early = [[2, 3], [4], [], []]
    for turn in range(HEADS // 2):
        pair = lax.rem(scatter.plane + 1 + turn, HEADS // 2)
        cols = pl.ds(pl.multiple_of(128 * pair, 128), 128)
        for at in range(0, length, size):
            begin = max(0, (at - most + 1) // 128 * 128)
            end = min(length, (at + size + most - 1 + 127) // 128 * 128)
            rows, keys = pl.ds(at, size), pl.ds(begin, end - begin)
            masked = jnp.where(seg_c[rows, :] == seg_r[:, keys], 0.0, MASKED)
            attend_back_pair(
                q, k, v, gctx, head_columns(lse[rows, :], pair),
                head_products(gctx[rows, cols], ctx[rows, cols]),
                gq, gk_t, gv_t, rows, keys, masked, size, cols,
            )
        copies.wait(*fetched[10:15])
        gk_low[cols, :] = (gk_t[cols, :] * SCALING).astype(bf16)
        gv_low[cols, :] = gv_t[cols, :].astype(bf16)
        g_q[cols, :] = dot(gq[:, cols], low[...], TN)
        g_k[cols, :] = dot(gk_low[cols, :], low[...], NN)
        g_v[cols, :] = dot(gv_low[cols, :], low[...], NN)
        agenda.round(*[scatter.part(5 + i, turn) for i in range(3)])
        aside.round(*[scatter.flow(which) for which in early[turn]])
    ones = jnp.ones((8, length), bf16)
    sums = [
        dot(ones, gq[...], NN)[0:1, :],
        dot(ones, gk_low[...], NT)[0:1, :],
        dot(ones, gv_low[...], NT)[0:1, :],
    ]
    total = column_sum(g_x[...])
    down = lax.broadcasted_iota(jnp.int32, (8, width), 0)
    for value, weight in zip(sums, (wq, wk, wv)):
        top = value.astype(bf16)
        middle = (value - top.astype(f32)).astype(bf16)
        bottom = (value - top.astype(f32) - middle.astype(f32)).astype(bf16)
        split = jnp.where(down == 0, top.astype(f32), jnp.where(down == 1, middle.astype(f32), 0.0))
        split = jnp.where(down == 2, bottom.astype(f32), split).astype(bf16)
        total = total + column_sum(dot(split, mat(weight), NN))
    down = lax.broadcasted_iota(jnp.int32, lines.shape, 0)
    value = jnp.where(down == tag[0], total, 0.0)
    value = jnp.where(down == langs, sums[0], jnp.where(down == langs + 1, sums[2], value))
    late[...] = value.T
    late_low[...] = late[...].astype(bf16)

    def own_rows(owner):
        return pl.ds(pl.multiple_of(owner * share, share), share)

    def straight(step):
        target = lax.rem(scatter.me + step, devices)
        return pltpu.make_async_remote_copy(
            late_low.at[own_rows(target), :],
            late_got.at[step - 1],
            late_send.at[step],
            late_recv.at[step],
            device_id=(scatter.rep, target),
            device_id_type=MESH,
        )

    def hand_over():
        return pltpu.make_async_remote_copy(
            late_give,
            late_get,
            late_send.at[0],
            late_recv.at[0],
            device_id=scatter.near("rep"),
            device_id_type=MESH,
        )

    for step in range(1, devices):
        straight(step).start()
    agenda.round()
    for at in range(0, length, 512):
        rows = pl.ds(at, 512)
        value = g_x[rows, :] + dot(gq[rows, :], mat(wq), NN)
        value = value + dot(gk_low[:, rows], mat(wk), TN) + dot(gv_low[:, rows], mat(wv), TN)
        g_x[rows, :] = value
    agenda.round()
    aside.round()
    copies.wait_all()
    endings = [scatter.ending(5 + i) for i in range(3)]
    for at in range(0, length, 512):
        rows = pl.ds(at, 512)
        y, _ = after_cross(
            a1[rows, :], ctxb1[rows, :], wco, win, wout, small, hidden_bias, None, None
        )
        first[rows, :] = y.astype(bf16)
        if at > 0:
            continue
        while agenda.busy():
            agenda.round()
        for steps in endings:
            steps.pop(0)()
        aside.round()
        value = late[own_rows(scatter.me), :]
        for step in range(1, devices):
            straight(step).wait_recv()
            value = value + late_got[step - 1].astype(f32)
        value = value.astype(bf16)
        late_give[...] = value
        hand_over().start()
    for steps in endings:
        steps.pop(0)()
    while aside.busy():
        aside.round()
    hand_over().wait_recv()
    o_late[...] = value.astype(f32) + late_get[...].astype(f32)
    scatter.leave()
    for step in range(1, devices):
        straight(step).wait_send()
    hand_over().wait_send()


def finish_kernel(langs, qkv, ckv, cq, so, co, up, down, table, late, *refs):
    large, outs, held, semaphores = refs[:4], refs[4:-5], refs[-5:-1], refs[-1]
    copies = Copies(semaphores)
    moves = []
    for source, place, out in zip(large, held, outs[11:]):
        for at in range(0, source.shape[0], 512):
            rows = pl.ds(at, 512)
            inward = copies.start(source.at[rows, :], place.at[rows, :])
            moves.append((inward, place.at[rows, :], out.at[rows, :]))
    for inward, place, out in moves:
        copies.wait(inward)
        copies.start(place, out)
    for source, out in zip((qkv, ckv, cq, so, co, down), outs):
        out[...] = source[...]
    outs[6][...] = up[...].T
    items = late[...]
    lines, soon = table[:, 0:128].T, items.T
    outs[7][...] = lines[langs : langs + BIASES, :]
    outs[7][0:2, :] = soon[langs : langs + 2, :]
    outs[8][...] = lines[langs + BIASES : langs + BIASES + GAINS, :]
    outs[9][...] = table[0:1, 128:256]
    outs[10][...] = items[:, 0:langs]
    copies.wait_all()


def transfer_call(kernel, name, collective_id, outs, args, scratch, scalars, away, away_out):
    in_specs = [pl.BlockSpec(memory_space=pltpu.SMEM)] * scalars
    for at in range(scalars, len(args)):
        in_specs.append(pl.BlockSpec(memory_space=pl.ANY if at >= away else VMEM))
    out_specs = [
        pl.BlockSpec(memory_space=pl.ANY if at >= away_out else VMEM) for at in range(len(outs))
    ]
    return pl.pallas_call(
        kernel,
        out_shape=outs,
        in_specs=in_specs,
        out_specs=out_specs,
        scratch_shapes=list(scratch),
        name=name,
        compiler_params=pltpu.CompilerParams(
            collective_id=collective_id, has_side_effects=True, vmem_limit_bytes=62 * 2**20
        ),
    )(*args)


def shards(
    n,
    x_copy,
    target_embed,
    memory,
    cotangent,
    segment_ids,
    source_lengths,
    target_lengths,
    hamming,
    priority,
    lang_tag,
    w_self_qkv,
    w_self_out,
    w_cross_q,
    w_cross_kv,
    w_cross_out,
    w_in,
    w_out,
    biases,
    gains,
    b_hidden,
    lang_table,
):
    depth = int(math.log2(n))
    length, width = x_copy.shape[1:]
    source = memory.shape[1]
    hidden = b_hidden.shape[0] * n
    share = width // n
    langs = lang_table.shape[0]
    most, fewest = 256, 384
    bits = (2,) * depth
    flat, side = (length, width), (source, width)
    lse = (length, 128)
    whole, up, down = bits + (share, width), bits + (hidden // n, width), bits + (share, hidden)
    square = (width, width)
    mem = memory[0]

    def low(dims):
        return shape(dims, bf16)

    def scratch(*all_dims, dtype=bf16):
        return [VMEM(dims, dtype) for dims in all_dims]

    kept = [
        shape(flat), low(flat), shape(flat), low(flat), low(flat), low(flat), low(flat), shape(lse), low(flat), low(side),
        low(side), low(flat), low(flat), shape(lse),
    ]
    weights = [low(whole)] * 8 + [low(up), low(down)]
    pieces = 10 + hidden // n // 32 + hidden // 512
    (
        small, seg_c, seg_r, hidden_bias, scale1,
        a1, ctxb1, hat1, low2, q, k, v, lse_self, ctx, ck, cv, cq, ctxb, lse_cross,
        wq, wk, wv, wck, wcv, wso, wcq, wco, win, wout,
    ) = transfer_call(
        functools.partial(forward_kernel, depth, most, fewest),
        "forward",
        2,
        [
            shape((16, width)), shape((length, 1)), shape((1, length)), shape((1, hidden)),
            shape((length, 1)),
        ]
        + kept
        + weights,
        (
            target_lengths, lang_tag, hamming, source_lengths, segment_ids, priority, biases, gains,
            lang_table.T, w_in, b_hidden[None], x_copy[0], target_embed[0], mem,
            w_self_qkv.transpose(0, 2, 1), w_cross_kv.transpose(0, 2, 1), w_self_out.T,
            w_cross_q.T, w_cross_out.T, w_out.T,
        ),
        scratch(flat, flat, side, bits + (share, 128), bits + (16, 128), *[whole] * 8, up, down)
        + scratch(flat, flat, dtype=f32)
        + scratch(*[flat] * 8)
        + scratch(lse, dtype=f32)
        + scratch(flat, flat, side, side)
        + scratch(flat, flat, dtype=f32)
        + scratch(*[flat] * 4)
        + scratch(lse, (length, 1), dtype=f32)
        + [pltpu.SemaphoreType.DMA((pieces, n // 4 + 1))] * 2
        + [pltpu.SemaphoreType.DMA((40,))],
        4,
        11,
        5,
    )
    big = 512
    blocks_in, blocks_out = hidden // n // 32, hidden // 512
    kinds = [(512, i % 2, False) for i in range(blocks_in + blocks_out + 1)]
    (
        gr1, gctx, g_so, g_cq, g_ck, g_cv, g_small, g_hidden, o_in, o_out, o_co, out, g_mem,
    ) = transfer_call(
        functools.partial(turn_kernel, depth, hamming.shape[1]),
        "turn",
        3,
        [shape(flat), low(flat)]
        + [shape(square)] * 4
        + [
            shape((16, width)), shape((1, hidden)), shape((hidden // n, width)),
            shape((share, hidden)), shape((share, width)), low(flat), shape(side),
        ],
        (
            source_lengths, scale1, seg_c, small, hidden_bias,
            hat1, ctxb, wco, win, wout, cotangent[0], cq, ck, cv, lse_cross, mem, wck, wcv, wcq,
            wso, ctx,
        ),
        scratch(flat, dtype=f32)
        + scratch(flat, whole, up, down, flat, side, side)
        + scratch(lse, dtype=f32)
        + scratch(side, whole, whole, whole, whole, flat)
        + scratch((hidden, width), (width, hidden), square, dtype=f32)
        + scratch((big, hidden))
        + scratch((width, max(hidden, 2 * source)), lse, dtype=f32)
        + scratch(flat, (big, width))
        + scratch((big, width), dtype=f32)
        + Scatter.scratch(depth, kinds)
        + [pltpu.SemaphoreType.DMA((24,))],
        1,
        5,
        11,
    )
    kinds = [(512, i % 2, False) for i in range(4)] + [(256, 0, False)]
    kinds += [(512, i % 2, True) for i in range(5, 8)]
    turned = (width, length)
    g_x, first, o_qkv, o_ckv, o_cq, o_so, o_table, o_late = transfer_call(
        functools.partial(close_kernel, depth, most),
        "close",
        4,
        [
            shape(flat), low(flat), shape((3, share, width)), shape((2, share, width)),
            shape((share, width)), shape((share, width)), shape((share, 256)), shape((share, 128)),
        ],
        (
            lang_tag, seg_c, seg_r, g_small, g_hidden, small, hidden_bias,
            gctx, ctx, q, k, v, lse_self, g_ck, g_cv, g_cq, g_so, low2, gr1, wq, wk, wv,
            a1, ctxb1, wco, win, wout,
        ),
        scratch(*[flat] * 5)
        + scratch(lse, *[square] * 4, dtype=f32)
        + scratch(flat, whole, whole, whole)
        + scratch(flat, dtype=f32)
        + scratch(flat, whole, up, down)
        + scratch(*[square] * 3, dtype=f32)
        + scratch(flat)
        + scratch(turned, turned, dtype=f32)
        + scratch(turned, turned)
        + scratch((2 * langs, width), (width, 256), (width, 128), dtype=f32)
        + scratch((width, 128), (n - 1, share, 128), (share, 128), (share, 128))
        + Scatter.scratch(depth, kinds)
        + [pltpu.SemaphoreType.DMA((n,))] * 2
        + [pltpu.SemaphoreType.DMA((24,))],
        1,
        7,
        8,
    )
    own = shape((share, width))
    large = (first, out, g_x, g_mem)
    small_outs = [
        shape((3, share, width)), shape((2, share, width)), own, own, own,
        shape((share, hidden)), shape((width, hidden // n)), shape((BIASES, share)),
        shape((GAINS, share)), shape((1, hidden // n)), shape((share, langs)),
    ]
    here, there = pl.BlockSpec(memory_space=VMEM), pl.BlockSpec(memory_space=pl.ANY)
    g_qkv, g_ckv, g_cq, g_so, g_co, g_out, g_in, g_bias, g_gain, g_mid, g_lang, *large = (
        pl.pallas_call(
            functools.partial(finish_kernel, langs),
            out_shape=small_outs + [jax.ShapeDtypeStruct(v.shape, v.dtype) for v in large],
            in_specs=[here] * 9 + [there] * 4,
            out_specs=[here] * 11 + [there] * 4,
            scratch_shapes=[VMEM(v.shape, v.dtype) for v in large]
            + [pltpu.SemaphoreType.DMA((16,))],
            name="finish",
            compiler_params=pltpu.CompilerParams(vmem_limit_bytes=61 * 2**20),
        )(o_qkv, o_ckv, o_cq, o_so, o_co, o_in, o_out, o_table, o_late, *large)
    )
    first, out, g_x, g_mem = large
    return (
        first[None],
        out[None],
        g_x[None],
        g_mem[None],
        g_qkv.transpose(0, 2, 1),
        g_so.T,
        g_cq.T,
        g_ckv.transpose(0, 2, 1),
        g_co.T,
        g_in,
        g_out.T,
        g_bias,
        g_gain,
        g_mid[0],
        g_lang.T,
    )


def choose(n):
    return shards if n * 32 == 512 else shards_apart


def solution(mesh):
    n = mesh.shape["dp"]
    row3, row2, row1 = P(("rep", "dp"), None, None), P(("rep", "dp"), None), P(("rep", "dp"))
    wide, tall, flat = P(None, None, "dp"), P(None, "dp"), P("dp")
    parameters = (wide, tall, tall, wide, tall, tall, tall, tall, tall, flat, tall)
    return jax.shard_map(
        functools.partial(choose(n), n),
        mesh=mesh,
        in_specs=(row3, row3, row3, row3, row2, row1, row1, row2, row2, row1) + parameters,
        out_specs=(row3, row3, row3, row3) + parameters,
        check_vma=False,
    )
```

```python
import functools
import itertools
import math

import jax
import jax.numpy as jnp
from jax import lax
from jax.experimental import pallas as pl
from jax.experimental.pallas import tpu as pltpu
from jax.sharding import PartitionSpec as P

f32, bf16 = jnp.float32, jnp.bfloat16
MESH = pl.DeviceIdType.MESH
VMEM = pltpu.VMEM

HEADS = 8
HD = 64
EPSILON = 1e-05
MASKED = -1000000000.0
LOG2E = 1.4426950408889634
SCORE = LOG2E * HD ** (-0.5)
SCALING = HD ** (-0.5)

NT = (((1,), (1,)), ((), ()))
NN = (((1,), (0,)), ((), ()))
TN = (((0,), (0,)), ((), ()))

BIASES, GAINS = 10, 3


def dot(left, right, form):
    return lax.dot_general(left, right, form, preferred_element_type=f32)


def own_bits(index, depth):
    return [lax.rem(index // (1 << (depth - 1 - j)), 2) for j in range(depth)]


def partner_of(index, bit, depth, j):
    return index + (1 - 2 * bit) * (1 << (depth - 1 - j))


def enter(rep, me, partners, with_rep):
    barrier = pltpu.get_barrier_semaphore()
    for partner in partners:
        pl.semaphore_signal(barrier, inc=1, device_id=(rep, partner), device_id_type=MESH)
    if with_rep:
        pl.semaphore_signal(barrier, inc=1, device_id=(1 - rep, me), device_id_type=MESH)
    pl.semaphore_wait(barrier, len(partners) + int(with_rep))


def gather_kernel(depth, pieces, count, *refs):
    ins, outs = refs[:count], refs[count : 2 * count]
    send, recv, local = refs[2 * count :]
    rep, me = lax.axis_index("rep"), lax.axis_index("dp")
    bits = own_bits(me, depth)
    partners = [partner_of(me, bits[j], depth, j) for j in range(depth)]
    copies = [
        pltpu.make_async_copy(ins[i], outs[i].at[tuple(bits)], local.at[i]) for i in range(count)
    ]
    for copy in copies:
        copy.start()
    enter(rep, me, partners, False)
    for copy in copies:
        copy.wait()
    started = {}
    for tick in range(len(pieces) + depth - 1):
        for j in reversed(range(depth)):
            b = tick - j
            if not 0 <= b < len(pieces):
                continue
            if j > 0:
                started[b, j - 1].wait_recv()
            which, rows, cols = pieces[b]
            part = outs[which].at[(slice(None),) * j + tuple(bits[j:]) + (rows, cols)]
            copy = pltpu.make_async_remote_copy(
                part,
                part,
                send.at[b, j],
                recv.at[b, j],
                device_id=(rep, partners[j]),
                device_id_type=MESH,
            )
            copy.start()
            started[b, j] = copy
    for (b, j), copy in started.items():
        copy.wait_send()
        if j == depth - 1:
            copy.wait_recv()


def gather_all(n, shards, collective_id):
    depth = int(math.log2(n))
    pieces = []
    for i, shard in enumerate(shards):
        r, c = shard.shape
        if c > 512:
            pieces += [(i, slice(None), pl.ds(at, 512)) for at in range(0, c, 512)]
        elif r >= 128:
            pieces += [(i, pl.ds(at, 32), slice(None)) for at in range(0, r, 32)]
        else:
            pieces.append((i, slice(None), slice(None)))
    count = len(shards)
    outs = pl.pallas_call(
        functools.partial(gather_kernel, depth, pieces, count),
        out_shape=[jax.ShapeDtypeStruct((2,) * depth + s.shape, s.dtype) for s in shards],
        in_specs=[pl.BlockSpec(memory_space=pl.ANY)] * count,
        out_specs=[pl.BlockSpec(memory_space=pl.ANY)] * count,
        scratch_shapes=[
            pltpu.SemaphoreType.DMA((len(pieces), depth)),
            pltpu.SemaphoreType.DMA((len(pieces), depth)),
            pltpu.SemaphoreType.DMA((count,)),
        ],
        name="gather_weights",
        compiler_params=pltpu.CompilerParams(collective_id=collective_id, has_side_effects=True),
    )(*shards)
    return [out.reshape(n * s.shape[0], s.shape[1]) for out, s in zip(outs, shards)]


def scatter_kernel(depth, pieces, groups, count, *refs):
    ins, outs = refs[:count], refs[count : 2 * count]
    at = 2 * count
    stages = depth + 1
    gives = {}
    gets = {}
    for group in groups:
        gives[group] = refs[at : at + stages]
        gets[group] = refs[at + stages : at + 2 * stages]
        at += 2 * stages
    send, recv = refs[at:]
    rep, me = lax.axis_index("rep"), lax.axis_index("dp")
    bits = own_bits(me, depth)
    partners = [partner_of(me, bits[j], depth, j) for j in range(depth)]
    enter(rep, me, partners, True)
    started = {}
    for tick in range(len(pieces) + depth + 1):
        for s in reversed(range(depth + 2)):
            b = tick - s
            if not 0 <= b < len(pieces):
                continue
            which, rows, cols, group, slot = pieces[b]
            source = ins[which]
            j = depth - 1 - s
            if s > 0:
                started[b, s - 1].wait_recv()
            if s == depth + 1:
                mine = gives[group][depth][slot].astype(f32)
                outs[which][rows, cols] = mine + gets[group][depth][slot].astype(f32)
                continue
            if j >= 0:
                head = (slice(None),) * j
                tail = tuple(bits[j + 1 :]) + (rows, cols)
                give = head + (1 - bits[j],) + tail
                keep = head + (bits[j],) + tail
                if s == 0:
                    gives[group][0][slot] = source[give].astype(bf16)
                else:
                    got = gets[group][s - 1].at[slot]
                    gives[group][s][slot] = (
                        source[give] + got[head + (1 - bits[j],)].astype(f32)
                    ).astype(bf16)
                    source[keep] = source[keep] + got[head + (bits[j],)].astype(f32)
                target = (rep, partners[j])
            else:
                got = gets[group][s - 1][slot].astype(f32)
                gives[group][s][slot] = (source[tuple(bits) + (rows, cols)] + got).astype(bf16)
                target = (1 - rep, me)
            copy = pltpu.make_async_remote_copy(
                gives[group][s].at[slot],
                gets[group][s].at[slot],
                send.at[b, s],
                recv.at[b, s],
                device_id=target,
                device_id_type=MESH,
            )
            copy.start()
            started[b, s] = copy
    for copy in started.values():
        copy.wait_send()


def scatter_all(n, grads, collective_id):
    depth = int(math.log2(n))
    pieces, views, shapes, sizes = [], [], [], {}
    for i, grad in enumerate(grads):
        r, c = grad.shape[0] // n, grad.shape[1]
        views.append(grad.reshape((2,) * depth + (r, c)))
        shapes.append((r, c))
        high, wide = min(r, 32), min(c, 512)
        for a in range(0, r, high):
            for q in range(0, c, wide):
                slot = sizes.get((high, wide), 0)
                sizes[high, wide] = slot + 1
                pieces.append((i, pl.ds(a, high), pl.ds(q, wide), (high, wide), slot))
    count = len(grads)
    groups = sorted(sizes)
    scratch = []
    for group in groups:
        buffers = [
            VMEM((sizes[group],) + (2,) * max(depth - 1 - s, 0) + group, bf16)
            for s in range(depth + 1)
        ]
        scratch += buffers + buffers
    return pl.pallas_call(
        functools.partial(scatter_kernel, depth, pieces, groups, count),
        out_shape=[jax.ShapeDtypeStruct(s, f32) for s in shapes],
        in_specs=[pl.BlockSpec(memory_space=VMEM)] * count,
        out_specs=[pl.BlockSpec(memory_space=VMEM)] * count,
        scratch_shapes=scratch
        + [
            pltpu.SemaphoreType.DMA((len(pieces), depth + 1)),
            pltpu.SemaphoreType.DMA((len(pieces), depth + 1)),
        ],
        name="scatter_gradients",
        compiler_params=pltpu.CompilerParams(
            collective_id=collective_id, has_side_effects=True, vmem_limit_bytes=60 * 2**20
        ),
    )(*views)


class Gather:
    lag, steps = 2, 3

    def __init__(self, depth, buffers, pieces, send, recv):
        self.depth, self.buffers, self.pieces = depth, buffers, pieces
        self.send, self.recv = send, recv
        self.rep, self.me = lax.axis_index("rep"), lax.axis_index("dp")
        self.bits = own_bits(self.me, depth)
        self.planes = 1 << (depth - 2)
        self.far = [
            (self.rep, lax.rem(self.me + 4 * k, 4 * self.planes)) for k in range(1, self.planes)
        ]
        self.near = [
            (self.rep, partner_of(self.me, self.bits[j], depth, j)) for j in (depth - 2, depth - 1)
        ]
        self.time, self.arrived = 0, set()

    def enter(self):
        barrier = pltpu.get_barrier_semaphore()
        for target in self.far + self.near:
            pl.semaphore_signal(barrier, inc=1, device_id=target, device_id_type=MESH)
        pl.semaphore_wait(barrier, len(self.far) + len(self.near))

    def own(self, which):
        return self.buffers[which].at[tuple(self.bits)]

    def transfers(self, b, j):
        which, rows, cols = self.pieces[b]
        fixed = [0, self.depth - 2, self.depth - 1][j]
        part = self.buffers[which].at[(slice(None),) * fixed + tuple(self.bits[fixed:]) + (rows, cols)]
        targets = self.far if j == 0 else [self.near[j - 1]]
        first = [0, len(self.far), len(self.far) + 1][j]
        return [
            pltpu.make_async_remote_copy(
                part,
                part,
                self.send.at[b, first + i],
                self.recv.at[b, first + i],
                device_id=target,
                device_id_type=MESH,
            )
            for i, target in enumerate(targets)
        ]

    def tick(self):
        for j in reversed(range(self.steps)):
            b = self.time - self.lag * j
            if 0 <= b < len(self.pieces):
                if j > 0:
                    for copy in self.transfers(b, j - 1):
                        copy.wait_recv()
                for copy in self.transfers(b, j):
                    copy.start()
        self.time += 1

    def need(self, count):
        for b in range(count):
            if b in self.arrived:
                continue
            while self.time <= b + self.lag * (self.steps - 1):
                self.tick()
            for copy in self.transfers(b, self.steps - 1):
                copy.wait_recv()
            self.arrived.add(b)

    def finish(self):
        self.need(len(self.pieces))
        for b in range(len(self.pieces)):
            for j in range(self.steps):
                for copy in self.transfers(b, j):
                    copy.wait_send()


class Agenda:
    def __init__(self):
        self.flows = []

    def round(self, *fresh):
        for steps in self.flows:
            if steps:
                steps.pop(0)()
        for steps in fresh:
            steps.pop(0)()
            self.flows.append(steps)

    def busy(self):
        return any(self.flows)


class Scatter:
    def __init__(self, depth, units, refs, send, recv):
        self.planes, self.units = 1 << (depth - 2), units
        self.rep, self.me = lax.axis_index("rep"), lax.axis_index("dp")
        self.core = lax.rem(self.me, 2)
        self.x = lax.rem(self.me // 2, 2)
        self.plane = self.me // 4
        self.send, self.recv = send, recv
        at, mark = 0, 0
        for unit in units:
            unit["parts"] = []
            planes = list(range(self.planes))
            turns = [[lax.rem(self.plane + 1 + p, self.planes)] for p in planes]
            for part in turns if unit["apart"] else [planes]:
                steps = []
                for _ in range(3):
                    steps.append((refs[at], refs[at + 1], mark))
                    at, mark = at + 2, mark + 1
                unit["parts"].append((part, steps))
            unit["across"], unit["last"] = (refs[at], refs[at + 1], mark), (refs[at + 2], refs[at + 3], mark + self.planes - 1)
            at, mark = at + 4, mark + self.planes

    @staticmethod
    def scratch(depth, kinds):
        planes, buffers, marks = 1 << (depth - 2), [], 0
        for wide, kind, apart in kinds:
            half = wide // 2
            for count in [1] * planes if apart else [planes]:
                middle = (count, 32, wide) if kind == 0 else (2 * count, 32, half)
                for dims in [(2 * count, 32, wide), middle, (count, 32, half)]:
                    buffers += [VMEM(dims, bf16)] * 2
                    marks += 1
            buffers += [VMEM((planes, 32, half), bf16), VMEM((planes - 1, 32, half), bf16)]
            buffers += [VMEM((32, half), bf16)] * 2
            marks += planes
        return buffers + [pltpu.SemaphoreType.DMA((marks,))] * 2

    def enter(self, steps=()):
        barrier = pltpu.get_barrier_semaphore()
        targets = [self.near("rep")]
        if steps:
            devices = 4 * self.planes
            targets += [(self.rep, lax.rem(self.me + k, devices)) for k in steps]
        else:
            targets += [self.near("core"), self.near("x")]
            targets += [self.far(k)[1] for k in range(1, self.planes)]
        for target in targets:
            pl.semaphore_signal(barrier, inc=1, device_id=target, device_id_type=MESH)
        pl.semaphore_wait(barrier, len(targets))

    def near(self, dim):
        if dim == "rep":
            return (1 - self.rep, self.me)
        if dim == "x":
            return (self.rep, self.me + 2 * (1 - 2 * self.x))
        return (self.rep, self.me + 1 - 2 * self.core)

    def far(self, k):
        plane = lax.rem(self.plane + k, self.planes)
        return plane, (self.rep, plane * 4 + lax.rem(self.me, 4))

    def transfer(self, give, get, mark, target):
        return pltpu.make_async_remote_copy(
            give,
            get,
            self.send.at[mark],
            self.recv.at[mark],
            device_id=target,
            device_id_type=MESH,
        )

    def part(self, which, index):
        unit = self.units[which]
        planes, buffers = unit["parts"][index]
        source, r, a, c0, wide = (unit[name] for name in ("source", "r", "a", "c0", "wide"))
        half, count = wide // 2, len(planes)
        dims = ["core", "x", "rep"] if unit["kind"] == 0 else ["core", "rep", "x"]
        whole = pl.ds(c0, wide)
        mine = pl.ds(pl.multiple_of(c0 + half * self.rep, 128), half)
        other = pl.ds(pl.multiple_of(c0 + half * (1 - self.rep), 128), half)
        mine_got = pl.ds(pl.multiple_of(half * self.rep, 128), half)
        other_got = pl.ds(pl.multiple_of(half * (1 - self.rep), 128), half)

        def rows(plane, x, core):
            return pl.ds(pl.multiple_of((plane * 4 + x * 2 + core) * r + a, 32), 32)

        def moved(step):
            give, get, mark = buffers[step]
            return self.transfer(give, get, mark, self.near(dims[step]))

        def first():
            give = buffers[0][0]
            for x in range(2):
                for i, plane in enumerate(planes):
                    give[x * count + i] = source[rows(plane, x, 1 - self.core), whole].astype(bf16)
            moved(0).start()

        def over_x(step, columns):
            moved(step - 1).wait_recv()
            give, got = buffers[step][0], buffers[step - 1][1]
            for i, plane in enumerate(planes):
                away = rows(plane, 1 - self.x, self.core)
                here = rows(plane, self.x, self.core)
                give[i] = (
                    source[away, columns] + got[(1 - self.x) * count + i].astype(f32)
                ).astype(bf16)
                source[here, columns] = source[here, columns] + got[self.x * count + i].astype(f32)
            moved(step).start()

        def over_rep(step):
            moved(step - 1).wait_recv()
            give, got = buffers[step][0], buffers[step - 1][1]
            for x in range(2) if step == 1 else [self.x]:
                for i, plane in enumerate(planes):
                    at = x * count + i if step == 1 else i
                    here = rows(plane, x, self.core)
                    give[at] = (source[here, other] + got[at, :, other_got].astype(f32)).astype(bf16)
                    source[here, mine] = source[here, mine] + got[at, :, mine_got].astype(f32)
            moved(step).start()

        def summed():
            moved(2).wait_recv()
            got, across = buffers[2][1], unit["across"][0]
            for i, plane in enumerate(planes):
                here = rows(plane, self.x, self.core)
                total = source[here, mine] + got[i].astype(f32)
                source[here, mine] = total
                across[plane] = total.astype(bf16)
            if unit["apart"] and index + 1 < self.planes:
                self.sent(which, index + 1).start()

        if unit["kind"] == 0:
            return [first, lambda: over_x(1, whole), lambda: over_rep(2), summed]
        return [first, lambda: over_rep(1), lambda: over_x(2, mine), summed]

    def ending(self, which):
        unit = self.units[which]
        source, r, a, c0, wide = (unit[name] for name in ("source", "r", "a", "c0", "wide"))
        out, out_col = unit["out"], unit["out_col"]
        half = wide // 2
        get = unit["across"][1]
        last = self.transfer(*unit["last"], self.near("rep"))
        mine = pl.ds(pl.multiple_of(c0 + half * self.rep, 128), half)

        def across():
            for k in range(1, self.planes):
                self.sent(which, k).start()

        def total():
            value = source[pl.ds(pl.multiple_of(self.me * r + a, 32), 32), mine]
            for k in range(1, self.planes):
                self.sent(which, k).wait_recv()
                value = value + get[k - 1].astype(f32)
            value = value.astype(bf16)
            unit["last"][0][...] = value
            own = pl.ds(pl.multiple_of(out_col + half * self.rep, 128), half)
            out[pl.ds(a, 32), own] = value.astype(f32)
            last.start()

        def rest():
            last.wait_recv()
            other = pl.ds(pl.multiple_of(out_col + half * (1 - self.rep), 128), half)
            out[pl.ds(a, 32), other] = unit["last"][1][...].astype(f32)

        return [total, rest] if unit["apart"] else [across, total, rest]

    def flow(self, which):
        steps, (across, *rest) = self.part(which, 0), self.ending(which)

        def summed():
            steps[-1]()
            across()

        return steps[:-1] + [summed] + rest

    def sent(self, which, k):
        give, get, mark = self.units[which]["across"]
        plane, target = self.far(k)
        return self.transfer(give.at[plane], get.at[k - 1], mark + k - 1, target)

    def leave(self):
        for which, unit in enumerate(self.units):
            dims = ["core", "x", "rep"] if unit["kind"] == 0 else ["core", "rep", "x"]
            for _, buffers in unit["parts"]:
                for step, (give, get, mark) in enumerate(buffers):
                    self.transfer(give, get, mark, self.near(dims[step])).wait_send()
            for k in range(1, self.planes):
                self.sent(which, k).wait_send()
            self.transfer(*unit["last"], self.near("rep")).wait_send()


def units_of(source, r, out, wide, kinds, apart=False):
    units = []
    for a in range(0, r, 32):
        for c0 in range(0, wide, 512):
            units.append(
                dict(
                    source=source, r=r, a=a, c0=c0, wide=min(512, wide - c0), out=out, out_col=c0,
                    kind=next(kinds) % 2, apart=apart,
                )
            )
    return units


def both_heads(pair, low):
    zero = jnp.zeros_like(pair)
    return jnp.concatenate([jnp.where(low, pair, zero), jnp.where(low, zero, pair)], axis=0)


def twice(bias):
    return bias if bias.shape[0] == 1 else jnp.concatenate([bias, bias], axis=0)


def attend_block(q, k, v, ctx, lse, rows, key_rows, keys, bias, size, after=None):
    low = lax.broadcasted_iota(jnp.int32, (size, 128), 1) < HD
    lanes = lax.broadcasted_iota(jnp.int32, (size, 128), 1)
    bias = twice(bias)
    log_sums = jnp.zeros((size, 128), f32)

    def scores(pair):
        cols = pl.ds(128 * pair, 128)
        return dot(both_heads(q[rows, cols], low), k[keys, cols], NT) * SCORE + bias

    following = scores(0)
    for pair in range(HEADS // 2):
        cols = pl.ds(128 * pair, 128)
        s = following
        if pair + 1 < HEADS // 2:
            following = scores(pair + 1)
        largest = jnp.max(s, axis=1, keepdims=True)
        powers = jnp.exp2(s - largest)
        total = jnp.sum(powers, axis=1, keepdims=True)
        c = dot(powers.astype(bf16), v[keys, cols], NN) * (1.0 / total)
        ctx[rows, cols] = jnp.where(low, c[:size], c[size:]).astype(bf16)
        if lse is not None:
            log_sum = largest + jnp.log2(total)
            log_sums = jnp.where(lanes == 2 * pair, log_sum[:size], log_sums)
            log_sums = jnp.where(lanes == 2 * pair + 1, log_sum[size:], log_sums)
        if after is not None:
            after()
    if lse is not None:
        lse[key_rows, :] = log_sums


def column_pair(table, rows, pair):
    return jnp.concatenate(
        [table[rows, 2 * pair : 2 * pair + 1], table[rows, 2 * pair + 1 : 2 * pair + 2]], axis=0
    )


def head_columns(table, pair):
    lanes = lax.broadcasted_iota(jnp.int32, table.shape, 1)
    parts = [jnp.where(lanes == 2 * pair + head, table, 0.0) for head in range(2)]
    return jnp.concatenate([jnp.sum(part, axis=1, keepdims=True) for part in parts], axis=0)


def head_products(left, right):
    value = left.astype(f32) * right.astype(f32)
    low = lax.broadcasted_iota(jnp.int32, value.shape, 1) < HD
    parts = [jnp.where(low, value, 0.0), jnp.where(low, 0.0, value)]
    return jnp.concatenate([jnp.sum(part, axis=1, keepdims=True) for part in parts], axis=0)


def attend_back_pair(q, k, v, g, lse, delta, gq, gk_t, gv_t, rows, keys, bias, size, cols):
    low = lax.broadcasted_iota(jnp.int32, (size, 128), 1) < HD
    q_two = both_heads(q[rows, cols], low)
    g_two = both_heads(g[rows, cols], low)
    k_pair, v_pair = k[keys, cols], v[keys, cols]
    probs = jnp.exp2(dot(q_two, k_pair, NT) * SCORE + twice(bias) - lse)
    grad_s = (probs * (dot(g_two, v_pair, NT) - delta)).astype(bf16)
    gv_t[cols, keys] += dot(g_two, probs.astype(bf16), TN)
    gk_t[cols, keys] += dot(q_two, grad_s, TN)
    d = dot(grad_s, k_pair, NN)
    gq[rows, cols] = (jnp.where(low, d[:size], d[size:]) * SCALING).astype(bf16)


def attend_back_block(
    q, k, v, g, lse, delta, gq, gk_t, gv_t, rows, keys, bias, size, after=None
):
    for pair in range(HEADS // 2):
        attend_back_pair(
            q, k, v, g, column_pair(lse, rows, pair), column_pair(delta, rows, pair),
            gq, gk_t, gv_t, rows, keys, bias, size, pl.ds(128 * pair, 128),
        )
        if after is not None:
            after()


def head_sums(value):
    rows = value.shape[0]
    lanes = lax.broadcasted_iota(jnp.int32, (rows, 128), 1)
    low = lanes < HD
    result = jnp.zeros((rows, 128), f32)
    for pair in range(HEADS // 2):
        part = value[:, 128 * pair : 128 * pair + 128]
        first = jnp.sum(jnp.where(low, part, 0.0), axis=1, keepdims=True)
        second = jnp.sum(jnp.where(low, 0.0, part), axis=1, keepdims=True)
        result = jnp.where(lanes == 2 * pair, first, result)
        result = jnp.where(lanes == 2 * pair + 1, second, result)
    return result


def blocks(total, size, body):
    def step(i, carry):
        body(pl.ds(pl.multiple_of(i * size, size), size))
        return carry

    lax.fori_loop(0, total // size, step, 0)


def normalise(value):
    average = jnp.mean(value, axis=1, keepdims=True)
    centred = value - average
    scale = lax.rsqrt(jnp.mean(centred * centred, axis=1, keepdims=True) + EPSILON)
    return centred * scale, scale


def normalise_back(grad, gain, hat, scale):
    g = grad * gain
    first = jnp.mean(g, axis=1, keepdims=True)
    second = jnp.mean(g * hat, axis=1, keepdims=True)
    return scale * (g - first - hat * second)


def column_sum(value):
    return jnp.sum(value, axis=0, keepdims=True)


def mat(ref):
    value = ref[...]
    return value if value.ndim == 2 else value.reshape(-1, value.shape[-1])


def up_part(win, j):
    if len(win.shape) == 2:
        return win[512 * j : 512 * j + 512, :]
    depth = len(win.shape) - 2
    lead = depth - int(math.log2(512 // win.shape[-2]))
    part = win[tuple((j >> (lead - 1 - i)) & 1 for i in range(lead))]
    return part.reshape(512, part.shape[-1])


def down_part(wout, j):
    if len(wout.shape) == 2:
        return wout[:, 512 * j : 512 * j + 512]
    part = wout[(slice(None),) * (len(wout.shape) - 1) + (slice(512 * j, 512 * j + 512),)]
    return part.reshape(-1, 512)


def prepare_kernel(
    x, t, mem, seg_c, seg_r, key_c, key_r, want_c, lang, wq, wk, wv, wck, wcv, small,
    h, q, k, v, ck, cv,
):
    length = x.shape[0]

    def glanced(rows):
        same = seg_c[rows, :] == seg_r[...]
        doc_length = jnp.sum(same.astype(f32), axis=1, keepdims=True)
        ahead = jnp.logical_and(same, key_r[...] > key_c[rows, :])
        rank = jnp.sum(ahead.astype(f32), axis=1, keepdims=True)
        wanted = jnp.minimum(want_c[rows, :], doc_length.astype(jnp.int32))
        count = lax.shift_right_logical(wanted + 1, jnp.int32(1))
        glance = rank < count.astype(f32)
        plain = x[rows, :].astype(f32)
        h[0, rows, :] = plain + lang[...]
        h[1, rows, :] = jnp.where(glance, t[rows, :].astype(f32), plain) + lang[...]

    blocks(length, 128, glanced)

    def cross(rows):
        m = mem[rows, :]
        ck[rows, :] = dot(m, wck[...], NT).astype(bf16)
        cv[rows, :] = (dot(m, wcv[...], NT) + small[4:5, :]).astype(bf16)

    blocks(mem.shape[0], 512, cross)
    for which in range(2):

        def project(rows):
            low = h[which, rows, :].astype(bf16)
            q[which, rows, :] = (dot(low, wq[...], NT) + small[0:1, :]).astype(bf16)
            k[which, rows, :] = dot(low, wk[...], NT).astype(bf16)
            v[which, rows, :] = (dot(low, wv[...], NT) + small[1:2, :]).astype(bf16)

        blocks(length, 512, project)


def windows(length):
    return [w for w in (256, 384, 512, 640) if w < length] + [length]


def windowed(starts, needs, i, length, body):
    need, begin = needs[i], starts[i]
    sizes = windows(length)
    for at, size in enumerate(sizes):
        fits = need <= size
        if at > 0:
            fits = jnp.logical_and(fits, need > sizes[at - 1])

        @pl.when(fits)
        def _():
            start = pl.multiple_of(jnp.minimum(begin, length - size), 128)
            body(pl.ds(start, size))


def self_kernel(starts, needs, q, k, v, seg_c, seg_r, ctx, lse):
    length = q.shape[1]
    size = 128

    def step(i, carry):
        rows = pl.ds(pl.multiple_of(i * size, size), size)

        def body(keys):
            bias = jnp.where(seg_c[rows, :] == seg_r[:, keys], 0.0, MASKED)
            for which in range(2):
                attend_block(
                    q.at[which], k.at[which], v.at[which], ctx.at[which],
                    lse if which == 1 else None, rows, rows, keys, bias, size,
                )

        windowed(starts, needs, i, length, body)
        return carry

    lax.fori_loop(0, length // size, step, 0)


def after_self(ctx, h, wso, wcq, small, a, cq, rows):
    r1 = h + dot(ctx, mat(wso), NT) + small[2:3, :]
    hat, scale = normalise(r1)
    value = hat * small[10:11, :] + small[7:8, :]
    if a is not None:
        a[rows, :] = value
    low = value.astype(bf16)
    cq[rows, :] = (dot(low, mat(wcq), NT) + small[3:4, :]).astype(bf16)
    return hat, scale, low


def after_cross(a, ctx2, wco, win, wout, small, hidden_bias, hid, slope, ready=None):
    r2 = a + dot(ctx2, mat(wco), NT) + small[5:6, :]
    hat2, scale2 = normalise(r2)
    b = hat2 * small[11:12, :] + small[8:9, :]
    low = b.astype(bf16)
    total = b + small[6:7, :]
    if ready is not None:
        ready()
    for j in range(hidden_bias.shape[1] // 512):
        cols = pl.ds(512 * j, 512)
        z = dot(low, up_part(win, j), NT) + hidden_bias[:, cols]
        half = 0.5 + 0.5 * lax.erf(z * 0.7071067811865476)
        hidden = (z * half).astype(bf16)
        if hid is not None:
            hid[:, cols] = hidden
            bell = jnp.exp2(z * z * (-0.5 * LOG2E)) * 0.3989422804014327
            slope[:, cols] = half + z * bell
        total = total + dot(hidden, down_part(wout, j), NT)
    hat3, scale3 = normalise(total)
    y = hat3 * small[12:13, :] + small[9:10, :]
    return y, (hat2, scale2, low, hat3, scale3)


def first_kernel(
    h, ctx, ck, cv, source_bias, wso, wcq, wco, win, wout, small, hidden_bias,
    out, a, cq, ctx2,
):
    length = h.shape[1]

    def before(rows):
        after_self(ctx[0, rows, :], h[0, rows, :], wso, wcq, small, a, cq, rows)

    blocks(length, 512, before)
    every = pl.ds(0, ck.shape[0])
    blocks(
        length,
        256,
        lambda rows: attend_block(cq, ck, cv, ctx2, None, rows, rows, every, source_bias[...], 256),
    )

    def last(rows):
        y, _ = after_cross(
            a[rows, :], ctx2[rows, :], wco, win, wout, small, hidden_bias, None, None
        )
        out[rows, :] = y.astype(bf16)

    blocks(length, 512, last)


def layer_kernel(
    h, ctx, ck, cv, mem, cot, live, source_bias,
    wso, wcq, wck, wcv, wco, win, wout, small, hidden_bias,
    out, gr1, gctx, g_mem,
    g_so, g_cq, g_ck, g_cv, g_co, g_in, g_out, g_small, g_hidden,
    cq, ctx2, lse2, hat1, scale1, low1, hid, slope, delta, gcq, gk_low, gv_low, low2, hat2s,
):
    length = h.shape[1]
    big = 512
    a, gctx2 = gr1, gctx
    for ref in (g_so, g_cq, g_co, g_in, g_out, g_small, g_hidden):
        ref[...] = jnp.zeros_like(ref)

    def before(rows):
        hat, scale, low = after_self(ctx[0, rows, :], h[0, rows, :], wso, wcq, small, a, cq, rows)
        hat1[rows, :] = hat
        scale1[rows, :] = scale
        low1[rows, :] = low

    blocks(length, big, before)
    every = pl.ds(0, ck.shape[0])
    blocks(
        length,
        256,
        lambda rows: attend_block(cq, ck, cv, ctx2, lse2, rows, rows, every, source_bias[...], 256),
    )

    def turn(rows):
        y, (hat2, scale2, low, hat3, scale3) = after_cross(
            a[rows, :], ctx2[rows, :], wco, win, wout, small, hidden_bias, hid, slope
        )
        out[rows, :] = y.astype(bf16)
        low2[...] = low
        hat2s[...] = hat2
        gy = cot[rows, :].astype(f32) * live[rows, :]
        g_small[12:13, :] += column_sum(gy * hat3)
        g_small[9:10, :] += column_sum(gy)
        gr3 = normalise_back(gy, small[12:13, :], hat3, scale3)
        gf = gr3.astype(bf16)
        g_small[6:7, :] += column_sum(gf.astype(f32))
        gb = gr3
        for j in range(win.shape[0] // 512):
            cols = pl.ds(512 * j, 512)
            gz = (dot(gf, wout[:, cols], NN) * slope[:, cols]).astype(bf16)
            g_out[:, cols] += dot(gf, hid[:, cols], TN)
            g_in[cols, :] += dot(gz, low2[...], TN)
            g_hidden[:, cols] += column_sum(gz.astype(f32))
            gb = gb + dot(gz, win[cols, :], NN)
        hat2 = hat2s[...]
        g_small[11:12, :] += column_sum(gb * hat2)
        g_small[8:9, :] += column_sum(gb)
        gr2 = normalise_back(gb, small[11:12, :], hat2, scale2)
        a[rows, :] = gr2
        go2 = gr2.astype(bf16)
        g_small[5:6, :] += column_sum(go2.astype(f32))
        context = ctx2[rows, :]
        g_co[...] += dot(go2, context, TN)
        back = dot(go2, wco[...], NN).astype(bf16)
        gctx2[rows, :] = back
        delta[rows, :] = head_sums(back.astype(f32) * context.astype(f32))

    blocks(length, big, turn)
    gk_t, gv_t = slope.at[:, pl.ds(0, ck.shape[0])], slope.at[:, pl.ds(ck.shape[0], ck.shape[0])]
    slope[...] = jnp.zeros_like(slope)
    blocks(
        length,
        256,
        lambda rows: attend_back_block(
            cq, ck, cv, gctx2, lse2, delta, gcq, gk_t, gv_t, rows, every, source_bias[...], 256
        ),
    )
    gk_low[...] = (gk_t[...] * SCALING).astype(bf16)
    gv_low[...] = gv_t[...].astype(bf16)
    g_ck[...] = dot(gk_low[...], mem[...], NN)
    g_cv[...] = dot(gv_low[...], mem[...], NN)
    ones = jnp.ones((8, mem.shape[0]), bf16)
    g_small[4:5, :] = dot(ones, gv_low[...], NT)[0:1, :]
    for at in range(0, mem.shape[0], 512):
        cols = pl.ds(at, 512)
        g_mem[cols, :] = dot(gk_low[:, cols], wck[...], TN) + dot(gv_low[:, cols], wcv[...], TN)

    def final(rows):
        gq = gcq[rows, :]
        g_small[3:4, :] += column_sum(gq.astype(f32))
        g_cq[...] += dot(gq, low1[rows, :], TN)
        ga = a[rows, :] + dot(gq, wcq[...], NN)
        hat = hat1[rows, :]
        g_small[10:11, :] += column_sum(ga * hat)
        g_small[7:8, :] += column_sum(ga)
        g1 = normalise_back(ga, small[10:11, :], hat, scale1[rows, :])
        gr1[rows, :] = g1
        go = g1.astype(bf16)
        g_small[2:3, :] += column_sum(go.astype(f32))
        g_so[...] += dot(go, ctx[0, rows, :], TN)
        gctx[rows, :] = dot(go, wso[...], NN).astype(bf16)

    blocks(length, big, final)


def self_back_kernel(
    starts, needs, live_blocks, q, k, v, g, ctx, lse, seg_c, seg_r,
    gq, gk_low, gv_low, delta, gk_t, gv_t,
):
    length = q.shape[1]
    size = 128
    gk_t[...] = jnp.zeros_like(gk_t)
    gv_t[...] = jnp.zeros_like(gv_t)
    gq[...] = jnp.zeros_like(gq)

    def step(i, carry):
        rows = pl.ds(pl.multiple_of(i * size, size), size)
        delta[rows, :] = head_sums(g[rows, :].astype(f32) * ctx[0, rows, :].astype(f32))

        def body(keys):
            bias = jnp.where(seg_c[rows, :] == seg_r[:, keys], 0.0, MASKED)
            attend_back_block(
                q.at[0], k.at[0], v.at[0], g, lse, delta, gq, gk_t, gv_t, rows, keys, bias, size
            )

        windowed(starts, needs, i, length, body)
        return carry

    lax.fori_loop(0, live_blocks[0], step, 0)
    gk_low[...] = (gk_t[...] * SCALING).astype(bf16)
    gv_low[...] = gv_t[...].astype(bf16)


def input_kernel(h, gq, gk_low, gv_low, gr1, wq, wk, wv, g_x, g_q, g_k, g_v, sums):
    length = h.shape[1]
    g_q[...] = jnp.zeros_like(g_q)
    g_k[...] = jnp.zeros_like(g_k)
    g_v[...] = jnp.zeros_like(g_v)
    sums[...] = jnp.zeros_like(sums)
    ones = jnp.ones((8, 512), bf16)

    for at in range(0, length, 512):
        rows = pl.ds(at, 512)
        low = h[0, rows, :].astype(bf16)
        part = gq[rows, :]
        g_q[...] += dot(part, low, TN)
        g_k[...] += dot(gk_low[:, rows], low, NN)
        g_v[...] += dot(gv_low[:, rows], low, NN)
        value = gr1[rows, :] + dot(part, wq[...], NN)
        value = value + dot(gk_low[:, rows], wk[...], TN) + dot(gv_low[:, rows], wv[...], TN)
        g_x[rows, :] = value
        sums[0:1, :] += column_sum(part.astype(f32))
        sums[1:2, :] += dot(ones, gv_low[:, rows], NT)[0:1, :]
        sums[2:3, :] += column_sum(value)


def shape(dims, dtype=f32):
    return jax.ShapeDtypeStruct(dims, dtype)


def call(kernel, name, outs, args, scratch=(), scalars=0, specs=None):
    in_specs = [pl.BlockSpec(memory_space=pltpu.SMEM)] * scalars
    for at in range(scalars, len(args)):
        in_specs.append((specs or {}).get(at) or pl.BlockSpec(memory_space=VMEM))
    return pl.pallas_call(
        kernel,
        out_shape=outs,
        in_specs=in_specs,
        out_specs=[pl.BlockSpec(memory_space=VMEM)] * len(outs),
        scratch_shapes=list(scratch),
        name=name,
        compiler_params=pltpu.CompilerParams(vmem_limit_bytes=61 * 2**20),
    )(*args)


def shards_apart(
    n,
    x_copy,
    target_embed,
    memory,
    cotangent,
    segment_ids,
    source_lengths,
    target_lengths,
    hamming,
    priority,
    lang_tag,
    w_self_qkv,
    w_self_out,
    w_cross_q,
    w_cross_kv,
    w_cross_out,
    w_in,
    w_out,
    biases,
    gains,
    b_hidden,
    lang_table,
):
    length, width = x_copy.shape[1:]
    source = memory.shape[1]
    hidden = b_hidden.shape[0] * n
    share = width // n
    fold = hidden // width
    langs = lang_table.shape[0]
    slots = hamming.shape[1]

    table = jnp.concatenate([biases, gains, lang_table, b_hidden.reshape(fold, share)], axis=0)
    kept = table.shape[0]
    table = jnp.pad(table, ((0, 128 - kept), (0, 0)))
    gathered = gather_all(
        n,
        [
            table.T,
            w_cross_kv[0].T,
            w_cross_kv[1].T,
            w_self_qkv[0].T,
            w_self_qkv[1].T,
            w_self_qkv[2].T,
            w_self_out.T,
            w_cross_q.T,
            w_cross_out.T,
            w_in.T,
            w_out.T,
        ],
        0,
    )
    small_t, wck, wcv, wq, wk, wv, wso, wcq, wco, win, wout = gathered
    small = small_t.T.astype(f32)
    first_lang = BIASES + GAINS
    hidden_bias = small[first_lang + langs : first_lang + langs + fold]
    hidden_bias = hidden_bias.reshape(fold, n, share).transpose(1, 0, 2).reshape(1, hidden)
    lang = lax.dynamic_slice_in_dim(small, first_lang + lang_tag[0], 1, 0)
    small = small[:16]

    target_len = target_lengths[0]
    position = jnp.arange(length, dtype=jnp.int32)
    live = position < target_len
    seg = jnp.where(live, segment_ids[0], slots).astype(jnp.int32)
    wanted = jnp.sum(
        jnp.where(seg[:, None] == jnp.arange(slots, dtype=jnp.int32)[None, :], hamming[0][None, :], 0),
        axis=1,
        keepdims=True,
    )
    key = priority[0] * length + (length - 1 - position)
    same_edge = seg.reshape(length // 128, 128)
    first_seg, last_seg = same_edge[:, 0], same_edge[:, -1]
    begin = jnp.sum((seg[None, :] < first_seg[:, None]).astype(jnp.int32), axis=1)
    end = jnp.sum((seg[None, :] <= last_seg[:, None]).astype(jnp.int32), axis=1)
    starts = begin // 128 * 128
    needs = (end + 127) // 128 * 128 - starts
    live_blocks = ((target_len + 127) // 128).reshape(1)
    seg_c, seg_r = seg[:, None], seg[None, :]
    source_bias = jnp.where(
        jnp.arange(source, dtype=jnp.int32) < source_lengths[0], 0.0, MASKED
    ).astype(f32)[None, :]

    mem = memory[0]
    two = (2, length, width)
    h, q, k, v, ck, cv = call(
        prepare_kernel,
        "prepare",
        [shape(two), shape(two, bf16), shape(two, bf16), shape(two, bf16)]
        + [shape((source, width), bf16)] * 2,
        (
            x_copy[0], target_embed[0], mem, seg_c, seg_r, key[:, None], key[None, :], wanted,
            lang, wq, wk, wv, wck, wcv, small,
        ),
    )
    ctx, lse = call(
        self_kernel,
        "self_attention",
        [shape(two, bf16), shape((length, 128))],
        (starts, needs, q, k, v, seg_c, seg_r),
        scalars=2,
    )

    def part(dims, which):
        block = (1,) + dims[1:]
        return pl.BlockSpec(block, lambda i: (which, 0, 0))

    def one(value, which):
        return lax.slice_in_dim(value, which, which + 1, axis=0)

    flat = (length, width)
    (first,) = call(
        first_kernel,
        "first_pass",
        [shape(flat, bf16)],
        (one(h, 0), one(ctx, 0), ck, cv, source_bias, wso, wcq, wco, win, wout, small, hidden_bias),
        scratch=[VMEM(flat, f32), VMEM(flat, bf16), VMEM(flat, bf16)],
    )
    square = shape((width, width))
    h2, ctx_two = one(h, 1), one(ctx, 1)
    big = 512
    (
        final, gr1, gctx, g_mem, g_so, g_cq, g_ck, g_cv, g_co, g_in, g_out, g_small, g_hidden,
    ) = call(
        layer_kernel,
        "second_pass",
        [shape(flat, bf16), shape(flat), shape(flat, bf16), shape((source, width))]
        + [square] * 5
        + [shape((hidden, width)), shape((width, hidden)), shape((16, width)), shape((1, hidden))],
        (
            h2, ctx_two, ck, cv, mem, cotangent[0], live[:, None].astype(f32), source_bias,
            wso, wcq, wck, wcv, wco, win, wout, small, hidden_bias,
        ),
        scratch=[
            VMEM(flat, bf16), VMEM(flat, bf16), VMEM((length, 128), f32),
            VMEM(flat, f32), VMEM((length, 1), f32), VMEM(flat, bf16),
            VMEM((big, hidden), bf16), VMEM((width, max(hidden, 2 * source)), f32),
            VMEM((length, 128), f32), VMEM(flat, bf16),
            VMEM((width, source), bf16), VMEM((width, source), bf16),
            VMEM((big, width), bf16), VMEM((big, width), f32),
        ],
    )
    gq, gk_low, gv_low = call(
        self_back_kernel,
        "self_attention_back",
        [shape(flat, bf16), shape((width, length), bf16), shape((width, length), bf16)],
        (starts, needs, live_blocks, one(q, 1), one(k, 1), one(v, 1), gctx, ctx_two, lse, seg_c, seg_r),
        scratch=[VMEM((length, 128), f32), VMEM((width, length), f32), VMEM((width, length), f32)],
        scalars=3,
    )
    g_x, g_q, g_k, g_v, sums = call(
        input_kernel,
        "input_gradient",
        [shape(flat), square, square, square, shape((8, width))],
        (h2, gq, gk_low, gv_low, gr1, wq, wk, wv),
    )

    tag = jnp.arange(langs, dtype=jnp.int32) == lang_tag[0]
    g_lang = jnp.where(tag[:, None], sums[2:3], 0.0)
    g_fold = g_hidden.reshape(n, fold, share).transpose(1, 0, 2).reshape(fold, width)
    g_table = jnp.concatenate([sums[0:2], g_small[2:13], g_lang, g_fold], axis=0)
    g_table = jnp.pad(g_table, ((0, 128 - kept), (0, 0))).T
    owned = scatter_all(n, [g_in, g_out, g_co, g_ck, g_cv, g_cq, g_so, g_q, g_k, g_v, g_table], 1)
    o_in, o_out, o_co, o_ck, o_cv, o_cq, o_so, o_q, o_k, o_v, o_table = owned
    o_table = o_table.T
    return (
        first[None],
        final[None],
        g_x[None],
        g_mem[None],
        jnp.stack([o_q.T, o_k.T, o_v.T]),
        o_so.T,
        o_cq.T,
        jnp.stack([o_ck.T, o_cv.T]),
        o_co.T,
        o_in.T,
        o_out.T,
        o_table[:BIASES],
        o_table[BIASES:first_lang],
        o_table[first_lang + langs : kept].reshape(hidden // n),
        o_table[first_lang : first_lang + langs],
    )


def add_to(ref, index, value, fresh):
    ref[index] = value if fresh else ref[index] + value


class Copies:
    def __init__(self, semaphores):
        self.semaphores, self.pending, self.count = semaphores, {}, 0

    def start(self, source, target):
        copy = pltpu.make_async_copy(source, target, self.semaphores.at[self.count])
        copy.start()
        self.pending[self.count] = copy
        self.count += 1
        return self.count - 1

    def wait(self, *which):
        for at in which:
            if at in self.pending:
                self.pending.pop(at).wait()

    def wait_all(self):
        self.wait(*list(self.pending))


def column(row, rows):
    size = 128
    down = lax.broadcasted_iota(jnp.int32, (size, size), 0)
    across = lax.broadcasted_iota(jnp.int32, (size, size), 1)
    return jnp.sum(jnp.where(down == across, row[:, rows], 0.0), axis=1, keepdims=True)


def placed(height, offset):
    down = lax.broadcasted_iota(jnp.int32, (height, 128), 0)
    across = lax.broadcasted_iota(jnp.int32, (height, 128), 1)
    return (across == down + offset).astype(bf16)


def apart(body):
    once = jnp.minimum(lax.axis_index("dp") + 1, 1)

    def step(i, carry):
        body()
        return carry

    lax.fori_loop(0, once, step, 0)


def source_row(source_len, count):
    position = lax.broadcasted_iota(jnp.int32, (1, count), 1)
    return jnp.where(position < source_len[0], 0.0, MASKED)


def forward_kernel(
    depth, most, fewest, target_len, tag, hamming, source_len,
    raw, priority, biases, gains, lang_t, w_in, b_mid,
    x_ref, t_ref, mem_ref, qkv_t, ckv_t, so_t, cq_t, co_t, out_t,
    small, seg_c, seg_r, hidden_bias, scale1,
    a1_ref, ctxb1_ref, hat1_ref, low2_ref, q2_ref, k2_ref, v2_ref, lse_ref, ctx2_ref, ck_ref, cv_ref, cq_ref,
    ctxb_ref, lse_cross_ref,
    wq_ref, wk_ref, wv_ref, wck_ref, wcv_ref, wso_ref, wcq_ref, wco_ref, win_ref, wout_ref,
    x, t, mem, small_t, mids, wq, wk, wv, wck, wcv, wso, wcq, wco, win, wout,
    h1, h2, low1, low2, q1, k1, v1, q2, k2, v2, lse, ctx1, ctx2, ck, cv, a1, hat1, cq1, cq,
    ctxb1, ctxb, lse_cross, glance, send, recv, local,
):
    length, count = x.shape[0], mem.shape[0]
    slots, langs = hamming.shape[1], lang_t.shape[1]
    every = (slice(None), slice(None))
    buffers = [small_t, wq, wk, wv, wck, wcv, wso, wcq, mids, wco, win, wout]
    pieces = [(i,) + every for i in range(10)]
    pieces += [(10, pl.ds(at, 32), slice(None)) for at in range(0, w_in.shape[1], 32)]
    pieces += [(11, slice(None), pl.ds(at, 512)) for at in range(0, out_t.shape[1], 512)]
    gather = Gather(depth, buffers, pieces, send, recv)
    copies = Copies(local)
    shares = [qkv_t.at[0], qkv_t.at[1], qkv_t.at[2], ckv_t.at[0], ckv_t.at[1], so_t, cq_t]
    owned = [copies.start(share, gather.own(i + 1)) for i, share in enumerate(shares)]
    owned += [copies.start(co_t, gather.own(9)), copies.start(out_t, gather.own(11))]
    rows_in = [copies.start(a, b) for a, b in ((x_ref, x), (t_ref, t), (mem_ref, mem))]
    table = dot(biases[...], placed(BIASES, langs), TN)
    table = table + dot(gains[...], placed(GAINS, langs + BIASES), TN)
    table = table + dot(lang_t[...], placed(langs, 0), NN)
    small_t[tuple(gather.bits)] = table.astype(bf16)
    win[tuple(gather.bits)] = w_in[...].astype(f32).T.astype(bf16)
    mids[tuple(gather.bits)] = jnp.broadcast_to(b_mid[...], mids.shape[-2:])
    gather.enter()
    gather.tick()
    copies.wait(*owned)
    gather.tick()

    position = lax.broadcasted_iota(jnp.int32, (1, length), 1)
    segments = jnp.where(position < target_len[0], raw[...], slots).astype(f32)
    seg_r[...] = segments
    rank_key = priority[...].astype(f32)
    place = position.astype(f32)

    def glanced(at):
        rows = pl.ds(at, 128)
        seg = column(segments, slice(at, at + 128))
        key = column(rank_key, slice(at, at + 128))
        here = (lax.broadcasted_iota(jnp.int32, (128, 1), 0) + at).astype(f32)
        seg_c[rows, :] = seg
        same = segments == seg
        doc_length = jnp.sum(same.astype(f32), axis=1, keepdims=True)
        ahead = (rank_key > key) | ((rank_key == key) & (place < here))
        rank = jnp.sum((same & ahead).astype(f32), axis=1, keepdims=True)
        wanted = jnp.zeros((128, 1), f32)
        for slot in range(slots):
            wanted = jnp.where(seg == float(slot), hamming[0, slot].astype(f32), wanted)
        glance[rows, :] = (2.0 * rank + 1.0 <= jnp.minimum(wanted, doc_length)).astype(f32)

    for at in range(0, length, 128):
        glanced(at)
        if at % 512 == 384:
            gather.tick()
    gather.need(1)
    items = mat(small_t)
    small[...] = dot(placed(16, langs), items, NT)
    choice = lax.broadcasted_iota(jnp.int32, (8, 128), 1) == tag[0]
    lang = dot(choice.astype(bf16), items, NT)[0:1, :]
    copies.wait(*rows_in)

    def combine(rows):
        plain = x[rows, :].astype(f32)
        one = plain + lang
        two = jnp.where(glance[rows, :] > 0.5, t[rows, :].astype(f32), plain) + lang
        h1[rows, :] = one
        h2[rows, :] = two
        low1[rows, :] = one.astype(bf16)
        low2[rows, :] = two.astype(bf16)

    blocks(length, 256, combine)
    copies.start(low2, low2_ref)

    def project(source, weight, bias, out):
        def step(rows):
            value = dot(source[rows, :], mat(weight), NT)
            if bias is not None:
                value = value + small[bias : bias + 1, :]
            out[rows, :] = value.astype(bf16)

        blocks(source.shape[0], 512, step)

    for at, (weight, bias, one, two) in enumerate(
        [(wq, 0, q1, q2), (wk, None, k1, k2), (wv, 1, v1, v2)]
    ):
        gather.need(2 + at)
        project(low1, weight, bias, one)
        project(low2, weight, bias, two)
    for source, target in ((q2, q2_ref), (k2, k2_ref), (v2, v2_ref)):
        copies.start(source, target)

    pause = gather.tick
    for q, k, v, ctx, log_sums in ((q1, k1, v1, ctx1, None), (q2, k2, v2, ctx2, lse)):
        for at in range(0, length, 256):

            def one_block():
                begin, end = max(0, at - most + 1), min(length, at + 256 + most - 1)
                if at + 256 > fewest:
                    begin, end = min(begin, fewest), length
                begin, end = begin // 128 * 128, (end + 127) // 128 * 128
                rows, keys = pl.ds(at, 256), pl.ds(begin, end - begin)
                masked = jnp.where(seg_c[rows, :] == seg_r[:, keys], 0.0, MASKED)
                attend_block(q, k, v, ctx, log_sums, rows, rows, keys, masked, 256)

            apart(one_block)
            pause()
    copies.start(ctx2, ctx2_ref)
    copies.start(lse, lse_ref)
    gather.need(8)
    project(mem, wck, None, ck)
    project(mem, wcv, 4, cv)
    copies.start(ck, ck_ref)
    copies.start(cv, cv_ref)
    pause()

    def start_one(rows):
        after_self(ctx1[rows, :], h1[rows, :], wso, wcq, small, a1, cq1, rows)

    def start_two(rows):
        hat, scale, _ = after_self(ctx2[rows, :], h2[rows, :], wso, wcq, small, None, cq, rows)
        hat1[rows, :] = hat
        scale1[rows, :] = scale

    blocks(length, 512, start_one)
    copies.start(a1, a1_ref)
    pause()
    blocks(length, 512, start_two)
    copies.start(hat1, hat1_ref)
    copies.start(cq, cq_ref)
    pause()
    every_key = pl.ds(0, count)
    source_bias = source_row(source_len, count)
    for query, context, log_sums in ((cq, ctxb, lse_cross), (cq1, ctxb1, None)):
        for at in range(0, length, 256):

            def one_block():
                rows = pl.ds(at, 256)
                attend_block(
                    query, ck, cv, context, log_sums, rows, rows, every_key, source_bias, 256
                )

            apart(one_block)
            if log_sums is not None:
                pause()
            elif at == 0:
                gather.finish()
                for source, target in (
                    (wq, wq_ref), (wk, wk_ref), (wv, wv_ref), (wck, wck_ref), (wcv, wcv_ref),
                    (wso, wso_ref), (wcq, wcq_ref), (wco, wco_ref), (win, win_ref),
                    (wout, wout_ref),
                ):
                    copies.start(source, target)
        if log_sums is not None:
            copies.start(ctxb, ctxb_ref)
            copies.start(lse_cross, lse_cross_ref)
    copies.start(ctxb1, ctxb1_ref)
    for i in range(2**depth):
        owner = mids.at[tuple((i >> (depth - 1 - j)) & 1 for j in range(depth))]
        hidden_bias[:, 128 * i : 128 * i + 128] = owner[0:1, :].astype(f32)
    copies.wait_all()


def turn_kernel(
    depth, slots, source_len,
    scale1, seg_c, small, hidden_bias,
    hat1_ref, ctxb_ref, wco_ref, win_ref, wout_ref, cot_ref,
    cq_ref, ck_ref, cv_ref, lse_ref, mem_ref, wck_ref, wcv_ref, wcq_ref, wso_ref, ctx_ref,
    gr1, gctx, g_so, g_cq, g_small, g_hidden, o_in, o_out, o_co, out_ref, g_mem_ref, g_ck_ref, g_cv_ref,
    hat1, ctxb, wco, win, wout, cq, ck, cv, lse, mem, wck, wcv, wcq, wso, ctx,
    g_in, g_out, g_co, g_ck, g_cv, hid, slope, delta, gcq, low2, hat2s, *rest,
):
    length, count = cq.shape[0], ck.shape[0]
    big = 512
    send, recv, local = rest[-3:]
    kinds = itertools.count()
    units = (
        units_of(g_out, g_out.shape[0] >> depth, o_out, g_out.shape[1], kinds)
        + units_of(g_in, g_in.shape[0] >> depth, o_in, g_in.shape[1], kinds)
        + units_of(g_co, g_co.shape[0] >> depth, o_co, g_co.shape[1], kinds)
    )
    downs = g_out.shape[1] // 512
    scatter = Scatter(depth, units, rest[:-3], send, recv)
    agenda = Agenda()
    copies = Copies(local)
    pairs = [
        (hat1_ref, hat1), (ctxb_ref, ctxb), (wco_ref, wco), (win_ref, win), (wout_ref, wout),
        (cot_ref, gctx),
        (cq_ref, cq), (ck_ref, ck), (cv_ref, cv), (lse_ref, lse),
        (mem_ref, mem), (wck_ref, wck), (wcv_ref, wcv), (wcq_ref, wcq), (wso_ref, wso), (ctx_ref, ctx),
    ]
    fetched = [copies.start(source, target) for source, target in pairs]
    for ref in (g_small, g_hidden):
        ref[...] = jnp.zeros_like(ref)
    scatter.enter()
    copies.wait(*fetched[:3])

    out = gcq
    for at in range(0, length, big):
        rows = pl.ds(at, big)
        final = at + big == length
        a = hat1[rows, :] * small[10:11, :] + small[7:8, :]
        y, (hat2, scale2, low, hat3, scale3) = after_cross(
            a, ctxb[rows, :], wco, win, wout, small, hidden_bias, hid, slope,
            lambda: copies.wait(*fetched[3:6]),
        )
        out[rows, :] = y.astype(bf16)
        low2[...] = low
        hat2s[...] = hat2
        live = (seg_c[rows, :] < slots - 0.5).astype(f32)
        gy = gctx[rows, :].astype(f32) * live
        g_small[12:13, :] += column_sum(gy * hat3)
        g_small[9:10, :] += column_sum(gy)
        gr3 = normalise_back(gy, small[12:13, :], hat3, scale3)
        gf = gr3.astype(bf16)
        g_small[6:7, :] += column_sum(gf.astype(f32))
        gb = gr3
        for j in range(downs):
            cols = pl.ds(512 * j, 512)
            gz = (dot(gf, down_part(wout, j), NN) * slope[:, cols]).astype(bf16)
            add_to(g_out, (slice(None), cols), dot(gf, hid[:, cols], TN), at == 0)
            add_to(g_in, (cols, slice(None)), dot(gz, low2[...], TN), at == 0)
            g_hidden[:, cols] += column_sum(gz.astype(f32))
            gb = gb + dot(gz, up_part(win, j), NN)
            if final and j % 2 == 1:
                agenda.round(*[scatter.flow(i) for i in range(j // 2, j)])
        hat2 = hat2s[...]
        g_small[11:12, :] += column_sum(gb * hat2)
        g_small[8:9, :] += column_sum(gb)
        gr2 = normalise_back(gb, small[11:12, :], hat2, scale2)
        gr1[rows, :] = gr2
        go2 = gr2.astype(bf16)
        g_small[5:6, :] += column_sum(go2.astype(f32))
        context = ctxb[rows, :]
        add_to(g_co, ..., dot(go2, context, TN), at == 0)
        back = dot(go2, mat(wco), NN).astype(bf16)
        gctx[rows, :] = back
        delta[rows, :] = head_sums(back.astype(f32) * context.astype(f32))

    keep_out = copies.start(out, out_ref)
    waiting = list(range(downs - 1, len(units)))

    def onward(count):
        fresh = waiting[:count]
        del waiting[:count]
        agenda.round(*[scatter.flow(which) for which in fresh])

    onward(2)
    gk_t, gv_t = slope.at[:, pl.ds(0, count)], slope.at[:, pl.ds(count, count)]
    slope[...] = jnp.zeros_like(slope)
    copies.wait(keep_out, *fetched[6:10])
    every = pl.ds(0, count)
    source_bias = source_row(source_len, count)

    for at in range(0, length, 256):
        attend_back_block(
            cq, ck, cv, gctx, lse, delta, gcq, gk_t, gv_t, pl.ds(at, 256), every, source_bias, 256
        )
        onward(2)
    copies.wait(*fetched[10:])
    gk_low, gv_low = hid.at[:, pl.ds(0, count)], hid.at[:, pl.ds(count, count)]
    gk_low[...] = (gk_t[...] * SCALING).astype(bf16)
    gv_low[...] = gv_t[...].astype(bf16)
    g_ck[...] = dot(gk_low[...], mem[...], NN)
    g_cv[...] = dot(gv_low[...], mem[...], NN)
    copies.start(g_ck, g_ck_ref)
    copies.start(g_cv, g_cv_ref)
    ones = jnp.ones((8, count), bf16)
    g_small[4:5, :] = dot(ones, gv_low[...], NT)[0:1, :]
    for i, at in enumerate(range(0, count, 512)):
        cols = pl.ds(at, 512)
        place = slope.at[:, pl.ds(512 * i, 512)]
        place[...] = dot(gk_low[:, cols], mat(wck), TN) + dot(gv_low[:, cols], mat(wcv), TN)
        copies.start(place, g_mem_ref.at[cols, :])
    agenda.round()
    for at in range(0, length, big):
        rows = pl.ds(at, big)
        gq = gcq[rows, :]
        hat = hat1[rows, :]
        low = (hat * small[10:11, :] + small[7:8, :]).astype(bf16)
        g_small[3:4, :] += column_sum(gq.astype(f32))
        add_to(g_cq, ..., dot(gq, low, TN), at == 0)
        ga = gr1[rows, :] + dot(gq, mat(wcq), NN)
        g_small[10:11, :] += column_sum(ga * hat)
        g_small[7:8, :] += column_sum(ga)
        g1 = normalise_back(ga, small[10:11, :], hat, scale1[rows, :])
        gr1[rows, :] = g1
        go = g1.astype(bf16)
        g_small[2:3, :] += column_sum(go.astype(f32))
        add_to(g_so, ..., dot(go, ctx[rows, :], TN), at == 0)
        gctx[rows, :] = dot(go, mat(wso), NN).astype(bf16)
        agenda.round()
    while agenda.busy():
        agenda.round()
    scatter.leave()
    copies.wait_all()


def close_kernel(
    depth, most, tag,
    seg_c, seg_r, g_small, g_hidden, small, hidden_bias,
    gctx_ref, ctx_ref, q_ref, k_ref, v_ref, lse_ref, ck_ref, cv_ref, cq_ref, so_ref, low_ref,
    gr1_ref, wq_ref, wk_ref, wv_ref, a1_ref, ctxb1_ref, wco_ref, win_ref, wout_ref,
    g_x, first, o_qkv, o_ckv, o_cq, o_so, o_table, o_late,
    gctx, ctx, q, k, v, lse, g_ck, g_cv, g_cq, g_so, low, wq, wk, wv, a1, ctxb1, wco, win, wout,
    g_q, g_k, g_v, gq, gk_t, gv_t, gk_low, gv_low, lines, table, late, late_low, late_got,
    late_give, late_get, *rest,
):
    length = q.shape[0]
    size = 256
    send, recv, late_send, late_recv, local = rest[-5:]
    kinds = itertools.count()
    width = g_q.shape[0]
    share, devices = width >> depth, 1 << depth
    units = []
    for source, out in [(g_ck, o_ckv.at[0]), (g_cv, o_ckv.at[1]), (g_cq, o_cq), (g_so, o_so)]:
        units += units_of(source, share, out, width, kinds)
    units += units_of(table, share, o_table, table.shape[1], kinds)
    for i, source in enumerate((g_q, g_k, g_v)):
        units += units_of(source, share, o_qkv.at[i], width, kinds, apart=True)
    scatter = Scatter(depth, units, rest[:-5], send, recv)
    agenda, aside = Agenda(), Agenda()
    copies = Copies(local)
    pairs = [
        (gctx_ref, gctx), (ctx_ref, ctx), (q_ref, q), (k_ref, k), (v_ref, v), (lse_ref, lse),
        (ck_ref, g_ck), (cv_ref, g_cv), (cq_ref, g_cq), (so_ref, g_so),
        (low_ref, low), (gr1_ref, g_x), (wq_ref, wq), (wk_ref, wk), (wv_ref, wv),
        (a1_ref, a1), (ctxb1_ref, ctxb1), (wco_ref, wco), (win_ref, win), (wout_ref, wout),
    ]
    fetched = [copies.start(source, target) for source, target in pairs[:10]]
    scatter.enter(range(1, devices))
    for ref in (gk_t, gv_t, lines, table):
        ref[...] = jnp.zeros_like(ref)
    langs = lines.shape[0] // 2
    lines[langs : langs + 16, :] = g_small[...]
    table[:, 0:128] = lines[...].T
    for owner in range(devices):
        table[share * owner : share * owner + 1, 128:256] = g_hidden[:, 128 * owner : 128 * owner + 128]
    copies.wait(*fetched[:8])
    aside.round(scatter.flow(0), scatter.flow(1))
    fetched += [copies.start(source, target) for source, target in pairs[10:]]
    copies.wait(*fetched[8:10])
    early = [[2, 3], [4], [], []]
    for turn in range(HEADS // 2):
        pair = lax.rem(scatter.plane + 1 + turn, HEADS // 2)
        cols = pl.ds(pl.multiple_of(128 * pair, 128), 128)
        for at in range(0, length, size):
            begin = max(0, (at - most + 1) // 128 * 128)
            end = min(length, (at + size + most - 1 + 127) // 128 * 128)
            rows, keys = pl.ds(at, size), pl.ds(begin, end - begin)
            masked = jnp.where(seg_c[rows, :] == seg_r[:, keys], 0.0, MASKED)
            attend_back_pair(
                q, k, v, gctx, head_columns(lse[rows, :], pair),
                head_products(gctx[rows, cols], ctx[rows, cols]),
                gq, gk_t, gv_t, rows, keys, masked, size, cols,
            )
        copies.wait(*fetched[10:15])
        gk_low[cols, :] = (gk_t[cols, :] * SCALING).astype(bf16)
        gv_low[cols, :] = gv_t[cols, :].astype(bf16)
        g_q[cols, :] = dot(gq[:, cols], low[...], TN)
        g_k[cols, :] = dot(gk_low[cols, :], low[...], NN)
        g_v[cols, :] = dot(gv_low[cols, :], low[...], NN)
        agenda.round(*[scatter.part(5 + i, turn) for i in range(3)])
        aside.round(*[scatter.flow(which) for which in early[turn]])
    ones = jnp.ones((8, length), bf16)
    sums = [
        dot(ones, gq[...], NN)[0:1, :],
        dot(ones, gk_low[...], NT)[0:1, :],
        dot(ones, gv_low[...], NT)[0:1, :],
    ]
    total = column_sum(g_x[...])
    down = lax.broadcasted_iota(jnp.int32, (8, width), 0)
    for value, weight in zip(sums, (wq, wk, wv)):
        top = value.astype(bf16)
        middle = (value - top.astype(f32)).astype(bf16)
        bottom = (value - top.astype(f32) - middle.astype(f32)).astype(bf16)
        split = jnp.where(down == 0, top.astype(f32), jnp.where(down == 1, middle.astype(f32), 0.0))
        split = jnp.where(down == 2, bottom.astype(f32), split).astype(bf16)
        total = total + column_sum(dot(split, mat(weight), NN))
    down = lax.broadcasted_iota(jnp.int32, lines.shape, 0)
    value = jnp.where(down == tag[0], total, 0.0)
    value = jnp.where(down == langs, sums[0], jnp.where(down == langs + 1, sums[2], value))
    late[...] = value.T
    late_low[...] = late[...].astype(bf16)

    def own_rows(owner):
        return pl.ds(pl.multiple_of(owner * share, share), share)

    def straight(step):
        target = lax.rem(scatter.me + step, devices)
        return pltpu.make_async_remote_copy(
            late_low.at[own_rows(target), :],
            late_got.at[step - 1],
            late_send.at[step],
            late_recv.at[step],
            device_id=(scatter.rep, target),
            device_id_type=MESH,
        )

    def hand_over():
        return pltpu.make_async_remote_copy(
            late_give,
            late_get,
            late_send.at[0],
            late_recv.at[0],
            device_id=scatter.near("rep"),
            device_id_type=MESH,
        )

    for step in range(1, devices):
        straight(step).start()
    agenda.round()
    for at in range(0, length, 512):
        rows = pl.ds(at, 512)
        value = g_x[rows, :] + dot(gq[rows, :], mat(wq), NN)
        value = value + dot(gk_low[:, rows], mat(wk), TN) + dot(gv_low[:, rows], mat(wv), TN)
        g_x[rows, :] = value
    agenda.round()
    aside.round()
    copies.wait_all()
    endings = [scatter.ending(5 + i) for i in range(3)]
    for at in range(0, length, 512):
        rows = pl.ds(at, 512)
        y, _ = after_cross(
            a1[rows, :], ctxb1[rows, :], wco, win, wout, small, hidden_bias, None, None
        )
        first[rows, :] = y.astype(bf16)
        if at > 0:
            continue
        while agenda.busy():
            agenda.round()
        for steps in endings:
            steps.pop(0)()
        aside.round()
        value = late[own_rows(scatter.me), :]
        for step in range(1, devices):
            straight(step).wait_recv()
            value = value + late_got[step - 1].astype(f32)
        value = value.astype(bf16)
        late_give[...] = value
        hand_over().start()
    for steps in endings:
        steps.pop(0)()
    while aside.busy():
        aside.round()
    hand_over().wait_recv()
    o_late[...] = value.astype(f32) + late_get[...].astype(f32)
    scatter.leave()
    for step in range(1, devices):
        straight(step).wait_send()
    hand_over().wait_send()


def finish_kernel(langs, qkv, ckv, cq, so, co, up, down, table, late, *refs):
    large, outs, held, semaphores = refs[:4], refs[4:-5], refs[-5:-1], refs[-1]
    copies = Copies(semaphores)
    moves = []
    for source, place, out in zip(large, held, outs[11:]):
        for at in range(0, source.shape[0], 512):
            rows = pl.ds(at, 512)
            inward = copies.start(source.at[rows, :], place.at[rows, :])
            moves.append((inward, place.at[rows, :], out.at[rows, :]))
    for inward, place, out in moves:
        copies.wait(inward)
        copies.start(place, out)
    for source, out in zip((qkv, ckv, cq, so, co, down), outs):
        out[...] = source[...]
    outs[6][...] = up[...].T
    items = late[...]
    lines, soon = table[:, 0:128].T, items.T
    outs[7][...] = lines[langs : langs + BIASES, :]
    outs[7][0:2, :] = soon[langs : langs + 2, :]
    outs[8][...] = lines[langs + BIASES : langs + BIASES + GAINS, :]
    outs[9][...] = table[0:1, 128:256]
    outs[10][...] = items[:, 0:langs]
    copies.wait_all()


def transfer_call(kernel, name, collective_id, outs, args, scratch, scalars, away, away_out):
    in_specs = [pl.BlockSpec(memory_space=pltpu.SMEM)] * scalars
    for at in range(scalars, len(args)):
        in_specs.append(pl.BlockSpec(memory_space=pl.ANY if at >= away else VMEM))
    out_specs = [
        pl.BlockSpec(memory_space=pl.ANY if at >= away_out else VMEM) for at in range(len(outs))
    ]
    return pl.pallas_call(
        kernel,
        out_shape=outs,
        in_specs=in_specs,
        out_specs=out_specs,
        scratch_shapes=list(scratch),
        name=name,
        compiler_params=pltpu.CompilerParams(
            collective_id=collective_id, has_side_effects=True, vmem_limit_bytes=62 * 2**20
        ),
    )(*args)


def shards(
    n,
    x_copy,
    target_embed,
    memory,
    cotangent,
    segment_ids,
    source_lengths,
    target_lengths,
    hamming,
    priority,
    lang_tag,
    w_self_qkv,
    w_self_out,
    w_cross_q,
    w_cross_kv,
    w_cross_out,
    w_in,
    w_out,
    biases,
    gains,
    b_hidden,
    lang_table,
):
    depth = int(math.log2(n))
    length, width = x_copy.shape[1:]
    source = memory.shape[1]
    hidden = b_hidden.shape[0] * n
    share = width // n
    langs = lang_table.shape[0]
    most, fewest = 256, 384
    bits = (2,) * depth
    flat, side = (length, width), (source, width)
    lse = (length, 128)
    whole, up, down = bits + (share, width), bits + (hidden // n, width), bits + (share, hidden)
    square = (width, width)
    mem = memory[0]

    def low(dims):
        return shape(dims, bf16)

    def scratch(*all_dims, dtype=bf16):
        return [VMEM(dims, dtype) for dims in all_dims]

    kept = [
        shape(flat), low(flat), shape(flat), low(flat), low(flat), low(flat), low(flat), shape(lse), low(flat), low(side),
        low(side), low(flat), low(flat), shape(lse),
    ]
    weights = [low(whole)] * 8 + [low(up), low(down)]
    pieces = 10 + hidden // n // 32 + hidden // 512
    (
        small, seg_c, seg_r, hidden_bias, scale1,
        a1, ctxb1, hat1, low2, q, k, v, lse_self, ctx, ck, cv, cq, ctxb, lse_cross,
        wq, wk, wv, wck, wcv, wso, wcq, wco, win, wout,
    ) = transfer_call(
        functools.partial(forward_kernel, depth, most, fewest),
        "forward",
        2,
        [
            shape((16, width)), shape((length, 1)), shape((1, length)), shape((1, hidden)),
            shape((length, 1)),
        ]
        + kept
        + weights,
        (
            target_lengths, lang_tag, hamming, source_lengths, segment_ids, priority, biases, gains,
            lang_table.T, w_in, b_hidden[None], x_copy[0], target_embed[0], mem,
            w_self_qkv.transpose(0, 2, 1), w_cross_kv.transpose(0, 2, 1), w_self_out.T,
            w_cross_q.T, w_cross_out.T, w_out.T,
        ),
        scratch(flat, flat, side, bits + (share, 128), bits + (16, 128), *[whole] * 8, up, down)
        + scratch(flat, flat, dtype=f32)
        + scratch(*[flat] * 8)
        + scratch(lse, dtype=f32)
        + scratch(flat, flat, side, side)
        + scratch(flat, flat, dtype=f32)
        + scratch(*[flat] * 4)
        + scratch(lse, (length, 1), dtype=f32)
        + [pltpu.SemaphoreType.DMA((pieces, n // 4 + 1))] * 2
        + [pltpu.SemaphoreType.DMA((40,))],
        4,
        11,
        5,
    )
    big = 512
    blocks_in, blocks_out = hidden // n // 32, hidden // 512
    kinds = [(512, i % 2, False) for i in range(blocks_in + blocks_out + 1)]
    (
        gr1, gctx, g_so, g_cq, g_small, g_hidden, o_in, o_out, o_co, out, g_mem, g_ck, g_cv,
    ) = transfer_call(
        functools.partial(turn_kernel, depth, hamming.shape[1]),
        "turn",
        3,
        [shape(flat), low(flat)]
        + [shape(square)] * 2
        + [
            shape((16, width)), shape((1, hidden)), shape((hidden // n, width)),
            shape((share, hidden)), shape((share, width)), low(flat), shape(side),
            shape(square), shape(square),
        ],
        (
            source_lengths, scale1, seg_c, small, hidden_bias,
            hat1, ctxb, wco, win, wout, cotangent[0], cq, ck, cv, lse_cross, mem, wck, wcv, wcq,
            wso, ctx,
        ),
        scratch(flat, dtype=f32)
        + scratch(flat, whole, up, down, flat, side, side)
        + scratch(lse, dtype=f32)
        + scratch(side, whole, whole, whole, whole, flat)
        + scratch((hidden, width), (width, hidden), square, square, square, dtype=f32)
        + scratch((big, hidden))
        + scratch((width, max(hidden, 2 * source)), lse, dtype=f32)
        + scratch(flat, (big, width))
        + scratch((big, width), dtype=f32)
        + Scatter.scratch(depth, kinds)
        + [pltpu.SemaphoreType.DMA((24,))],
        1,
        5,
        9,
    )
    kinds = [(512, i % 2, False) for i in range(4)] + [(256, 0, False)]
    kinds += [(512, i % 2, True) for i in range(5, 8)]
    turned = (width, length)
    g_x, first, o_qkv, o_ckv, o_cq, o_so, o_table, o_late = transfer_call(
        functools.partial(close_kernel, depth, most),
        "close",
        4,
        [
            shape(flat), low(flat), shape((3, share, width)), shape((2, share, width)),
            shape((share, width)), shape((share, width)), shape((share, 256)), shape((share, 128)),
        ],
        (
            lang_tag, seg_c, seg_r, g_small, g_hidden, small, hidden_bias,
            gctx, ctx, q, k, v, lse_self, g_ck, g_cv, g_cq, g_so, low2, gr1, wq, wk, wv,
            a1, ctxb1, wco, win, wout,
        ),
        scratch(*[flat] * 5)
        + scratch(lse, *[square] * 4, dtype=f32)
        + scratch(flat, whole, whole, whole)
        + scratch(flat, dtype=f32)
        + scratch(flat, whole, up, down)
        + scratch(*[square] * 3, dtype=f32)
        + scratch(flat)
        + scratch(turned, turned, dtype=f32)
        + scratch(turned, turned)
        + scratch((2 * langs, width), (width, 256), (width, 128), dtype=f32)
        + scratch((width, 128), (n - 1, share, 128), (share, 128), (share, 128))
        + Scatter.scratch(depth, kinds)
        + [pltpu.SemaphoreType.DMA((n,))] * 2
        + [pltpu.SemaphoreType.DMA((24,))],
        1,
        7,
        8,
    )
    own = shape((share, width))
    large = (first, out, g_x, g_mem)
    small_outs = [
        shape((3, share, width)), shape((2, share, width)), own, own, own,
        shape((share, hidden)), shape((width, hidden // n)), shape((BIASES, share)),
        shape((GAINS, share)), shape((1, hidden // n)), shape((share, langs)),
    ]
    here, there = pl.BlockSpec(memory_space=VMEM), pl.BlockSpec(memory_space=pl.ANY)
    g_qkv, g_ckv, g_cq, g_so, g_co, g_out, g_in, g_bias, g_gain, g_mid, g_lang, *large = (
        pl.pallas_call(
            functools.partial(finish_kernel, langs),
            out_shape=small_outs + [jax.ShapeDtypeStruct(v.shape, v.dtype) for v in large],
            in_specs=[here] * 9 + [there] * 4,
            out_specs=[here] * 11 + [there] * 4,
            scratch_shapes=[VMEM(v.shape, v.dtype) for v in large]
            + [pltpu.SemaphoreType.DMA((16,))],
            name="finish",
            compiler_params=pltpu.CompilerParams(vmem_limit_bytes=61 * 2**20),
        )(o_qkv, o_ckv, o_cq, o_so, o_co, o_in, o_out, o_table, o_late, *large)
    )
    first, out, g_x, g_mem = large
    return (
        first[None],
        out[None],
        g_x[None],
        g_mem[None],
        g_qkv.transpose(0, 2, 1),
        g_so.T,
        g_cq.T,
        g_ckv.transpose(0, 2, 1),
        g_co.T,
        g_in,
        g_out.T,
        g_bias,
        g_gain,
        g_mid[0],
        g_lang.T,
    )


def choose(n):
    return shards if n * 32 == 512 else shards_apart


def solution(mesh):
    n = mesh.shape["dp"]
    row3, row2, row1 = P(("rep", "dp"), None, None), P(("rep", "dp"), None), P(("rep", "dp"))
    wide, tall, flat = P(None, None, "dp"), P(None, "dp"), P("dp")
    parameters = (wide, tall, tall, wide, tall, tall, tall, tall, tall, flat, tall)
    return jax.shard_map(
        functools.partial(choose(n), n),
        mesh=mesh,
        in_specs=(row3, row3, row3, row3, row2, row1, row1, row2, row2, row1) + parameters,
        out_specs=(row3, row3, row3, row3) + parameters,
        check_vma=False,
    )
```
